32 devices in a mesh: items: 8 (over z, x), seq: 4 (over y, core).
Axes of the slice: x: 2, y: 2, z: 4, core: 2. Of those that a mesh axis runs over, the one named last changes fastest.
Arguments:
- media: bfloat16 [8, 2048, 1536], P('items', 'seq'), may hold values from -6 to 6
- latents: bfloat16 [8, 64, 1536], P('items', 'seq'), may hold values from -6 to 6
- frames: int32 [8], P('items'), may hold values from 1 to 8, as said below
- time_embed: float32 [8, 1536], replicated, may hold values from -4 to 4
- media_gain: float32 [1536], replicated, may hold values from 0.5 to 1.5
- media_bias: float32 [1536], replicated, may hold values from -2 to 2
- latent_gain: float32 [1536], replicated, may hold values from 0.5 to 1.5
- latent_bias: float32 [1536], replicated, may hold values from -2 to 2
- ffn_gain: float32 [1536], replicated, may hold values from 0.5 to 1.5
- ffn_bias: float32 [1536], replicated, may hold values from -2 to 2
- w_query: bfloat16 [1536, 1536], P(('items', 'seq')), may hold values from -0.15625 to 0.15625
- w_key: bfloat16 [1536, 1536], P(('items', 'seq')), may hold values from -0.15625 to 0.15625
- w_value: bfloat16 [1536, 1536], P(('items', 'seq')), may hold values from -0.15625 to 0.15625
- w_out: bfloat16 [1536, 1536], P(('items', 'seq')), may hold values from -2.5 to 2.5
- w_up: bfloat16 [1536, 6144], P(('items', 'seq')), may hold values from -0.15625 to 0.15625
- w_down: bfloat16 [6144, 1536], P(('items', 'seq')), may hold values from -0.078125 to 0.078125
- grad_out: bfloat16 [8, 64, 1536], P('items', 'seq'), may hold values from -6 to 6
Outputs:
- latents_out: bfloat16 [8, 64, 1536], P('items', 'seq')
- latents_grad: bfloat16 [8, 64, 1536], P('items', 'seq')
- media_grad: bfloat16 [8, 2048, 1536], P('items', 'seq')
- time_grad: float32 [8, 1536], replicated
- media_gain_grad: float32 [1536], replicated
- media_bias_grad: float32 [1536], replicated
- latent_gain_grad: float32 [1536], replicated
- latent_bias_grad: float32 [1536], replicated
- ffn_gain_grad: float32 [1536], replicated
- ffn_bias_grad: float32 [1536], replicated
- query_grad: float32 [1536, 1536], P(('items', 'seq'))
- key_grad: float32 [1536, 1536], P(('items', 'seq'))
- value_grad: float32 [1536, 1536], P(('items', 'seq'))
- out_grad: float32 [1536, 1536], P(('items', 'seq'))
- up_grad: float32 [1536, 6144], P(('items', 'seq'))
- down_grad: float32 [6144, 1536], P(('items', 'seq'))
The draws below stay inside these ranges and needn't reach their ends.
Inputs may be any that keep to these rules, and one draw needn't show every extreme that they name: `frames`: each entry is 1 (an image) or 8 (a clip); both values occur in every draw.
All inputs are finite; a program needn't handle non-finite values.
Results may differ from the reference program's by a relative error of at most 0.012.
Values may be sent and summed in bfloat16 or wider, within the bound.
No kernel may reach another device: no remote copies, remote signals or barrier semaphores. Data moves between devices by JAX's collectives and lax.ppermute only.
A program may use at most 448 MiB of HBM per device.

```python
import jax
import jax.numpy as jnp
from jax import lax

D = 1536
H = 16
FF = 6144
DH = 96
LAT = 64
FRAMES = 8
PATCH = 256
ITEMS = 8


def draw_frames(key, part):
    key = jax.random.fold_in(key, 7)
    key_a, key_b, key_c = jax.random.split(key, 3)
    choose = jax.random.randint(key_a, (ITEMS,), 0, 2)
    counts = jnp.where(choose == 1, FRAMES, 1)
    long_at = jax.random.randint(key_b, (), 0, ITEMS)
    short_at = (long_at + 1 + jax.random.randint(key_c, (), 0, ITEMS - 1)) % ITEMS
    counts = counts.at[long_at].set(FRAMES).at[short_at].set(1)
    return counts.astype(jnp.int32)


def shard_levels(rng, extent, pieces, low, high):
    factor_of = 1.0
    for dim, blocks in pieces:
        heights = jax.random.uniform(jax.random.fold_in(jax.random.fold_in(rng, 6), dim), (blocks,), jnp.float32, low / len(pieces), high / len(pieces))
        factor_of = factor_of * jnp.repeat(jnp.exp(heights), extent[dim] // blocks).reshape((-1,) + (1,) * (len(extent) - 1 - dim))
    return factor_of


def scatter_about(stream_key, extent, scale, limit, pieces=(), kind=jnp.bfloat16):
    values = scale * jax.random.normal(stream_key, extent, jnp.float32)
    if pieces:
        values = values * shard_levels(stream_key, extent, pieces, -0.22, 0.18)
    return jnp.clip(values, -limit, limit).astype(kind)


def setup_inputs(seed: int = 0) -> dict:
    key_of = jax.random.split(jax.random.key(seed), 18)
    media = scatter_about(key_of[0], (ITEMS, FRAMES * PATCH, D), 1.0, 6.0, ((0, 8), (1, 4)))
    latents = scatter_about(key_of[1], (ITEMS, LAT, D), 1.0, 6.0, ((0, 8), (1, 4)))
    frames = draw_frames(jax.random.fold_in(key_of[17], 71), 0)
    time_embed = scatter_about(key_of[3], (FRAMES, D), 0.5, 4.0, (), jnp.float32)
    media_gain = jnp.clip(1.0 + 0.1 * jax.random.normal(key_of[4], (D,), jnp.float32), 0.5, 1.5)
    media_bias = scatter_about(key_of[5], (D,), 0.3, 2.0, (), jnp.float32)
    latent_gain = jnp.clip(1.0 + 0.1 * jax.random.normal(key_of[6], (D,), jnp.float32), 0.5, 1.5)
    latent_bias = scatter_about(key_of[7], (D,), 0.3, 2.0, (), jnp.float32)
    ffn_gain = jnp.clip(1.0 + 0.1 * jax.random.normal(key_of[8], (D,), jnp.float32), 0.5, 1.5)
    ffn_bias = scatter_about(key_of[9], (D,), 0.3, 2.0, (), jnp.float32)
    w_query = scatter_about(key_of[10], (D, D), D ** -0.5, 0.15625, ((0, 32),))
    w_key = scatter_about(key_of[11], (D, D), D ** -0.5, 0.15625, ((0, 32),))
    w_value = scatter_about(key_of[12], (D, D), D ** -0.5, 0.15625, ((0, 32),))
    w_out = scatter_about(key_of[13], (D, D), (max(D // 256, 1)) ** -0.5, 2.5, ((0, 32),))
    w_up = scatter_about(key_of[14], (D, FF), D ** -0.5, 0.15625, ((0, 32),))
    w_down = scatter_about(key_of[15], (FF, D), FF ** -0.5, 0.078125, ((0, 32),))
    grad_out = scatter_about(key_of[16], (ITEMS, LAT, D), 1.0, 6.0, ((0, 8), (1, 4)))
    return dict(media=media, latents=latents, frames=frames, time_embed=time_embed, media_gain=media_gain, media_bias=media_bias, latent_gain=latent_gain, latent_bias=latent_bias, ffn_gain=ffn_gain, ffn_bias=ffn_bias, w_query=w_query, w_key=w_key, w_value=w_value, w_out=w_out, w_up=w_up, w_down=w_down, grad_out=grad_out)


@jax.custom_vjp
def low(v):
    return lax.optimization_barrier(v.astype(jnp.bfloat16)).astype(jnp.float32)

@jax.custom_vjp
def low_back(v):
    return v

def low_keep(v):
    return (low(v), None)

def low_pass(kept, grad):
    return (grad,)

def back_keep(v):
    return (v, None)

def back_low(kept, grad):
    return (low(grad),)
low.defvjp(low_keep, low_pass)
low_back.defvjp(back_keep, back_low)

def layer_norm(values, gain, bias):
    center = lax.optimization_barrier(jnp.mean(values, axis=-1, keepdims=True))
    spread = lax.optimization_barrier(jnp.mean(jnp.square(values - center), axis=-1, keepdims=True))
    return (values - center) * lax.rsqrt(spread + 1e-05) * gain + bias

def matmul(left, right):
    return jnp.dot(left, right, precision=lax.Precision.HIGHEST)

def forward_item(params, media_item, latent_item, frame_count):
    time_embed, media_gain, media_bias, latent_gain, latent_bias, ffn_gain, ffn_bias, query_w, key_w, value_w, out_w, up_w, down_w = params
    shifted = (media_item.reshape(FRAMES, PATCH, D) + time_embed[:, None, :]).reshape(FRAMES * PATCH, D)
    media_normed = low(layer_norm(shifted, media_gain, media_bias))
    latent_normed = low(layer_norm(latent_item, latent_gain, latent_bias))
    query_rows = low_back(low(matmul(latent_normed, query_w) * DH ** (-0.5)))
    sources = jnp.concatenate([media_normed, latent_normed], axis=0)
    key_rows = low_back(low(matmul(sources, key_w)))
    value_rows = low_back(low(matmul(sources, value_w)))
    frame_of = jnp.arange(FRAMES * PATCH, dtype=jnp.int32) // PATCH
    visible = jnp.concatenate([frame_of < frame_count, jnp.ones((LAT,), dtype=bool)])
    scores = jnp.einsum('qhd,khd->hqk', query_rows.reshape(LAT, H, DH), key_rows.reshape(-1, H, DH), precision=lax.Precision.HIGHEST)
    scores = low_back(scores)
    scores = jnp.where(visible[None, None, :], scores, -1e+30)
    row_max = lax.optimization_barrier(jnp.max(scores, axis=-1, keepdims=True))
    weights = jnp.exp(scores - row_max)
    weights_low = low(weights / lax.optimization_barrier(jnp.sum(weights, axis=-1, keepdims=True)))
    mixture = jnp.einsum('hqk,khd->qhd', weights_low, value_rows.reshape(-1, H, DH), precision=lax.Precision.HIGHEST).reshape(LAT, D)
    mixture = low_back(low(mixture))
    attended = low_back(matmul(mixture, out_w))
    hidden = latent_item + attended
    ffn_in = low(layer_norm(hidden, ffn_gain, ffn_bias))
    pre_act = low_back(matmul(ffn_in, up_w))
    active = low(jax.nn.gelu(pre_act))
    return hidden + low_back(matmul(active, down_w))

def reference(media, latents, frames, time_embed, media_gain, media_bias, latent_gain, latent_bias, ffn_gain, ffn_bias, w_query, w_key, w_value, w_out, w_up, w_down, grad_out):
    params = tuple((array.astype(jnp.float32) for array in (time_embed, media_gain, media_bias, latent_gain, latent_bias, ffn_gain, ffn_bias, w_query, w_key, w_value, w_out, w_up, w_down)))

    def forward(params_in, media_all, latent_all):
        step_fn = jax.checkpoint(lambda batch: forward_item(params_in, batch[0], batch[1], batch[2]))
        return lax.map(step_fn, (media_all, latent_all, frames))
    result, pullback = jax.vjp(forward, params, media.astype(jnp.float32), latents.astype(jnp.float32))
    grad_params, grad_media, grad_latents = pullback(grad_out.astype(jnp.float32))
    return (result.astype(jnp.bfloat16), grad_latents.astype(jnp.bfloat16), grad_media.astype(jnp.bfloat16), grad_params[0], grad_params[1], grad_params[2], grad_params[3], grad_params[4], grad_params[5], grad_params[6], grad_params[7], grad_params[8], grad_params[9], grad_params[10], grad_params[11], grad_params[12])
```

```python
import jax
import jax.numpy as jnp
from jax import lax
from jax.experimental import pallas as pl
from jax.experimental.pallas import tpu as pltpu
from jax.sharding import PartitionSpec as P

H = 16
FRAMES = 8
PATCH = 256
AXES = ("items", "seq")
BF = jnp.bfloat16
F32 = jnp.float32


def layer_norm(values, gain, bias):
    center = jnp.mean(values, axis=-1, keepdims=True)
    spread = jnp.mean(jnp.square(values - center), axis=-1, keepdims=True)
    rstd = lax.rsqrt(spread + 1e-05)
    unit = (values - center) * rstd
    return unit * gain + bias, unit, rstd


def layer_norm_back(grad, unit, rstd, gain):
    scaled = grad * gain
    inner = scaled - jnp.mean(scaled, axis=-1, keepdims=True)
    inner = inner - unit * jnp.mean(scaled * unit, axis=-1, keepdims=True)
    return inner * rstd, jnp.sum(grad * unit, axis=0), jnp.sum(grad, axis=0)


def dot(a, b, dims=((1,), (0,))):
    return lax.dot_general(a, b, (dims, ((), ())), preferred_element_type=F32)


def trade(x, mask, count):
    return lax.ppermute(x, AXES, [(i, i ^ mask) for i in range(count)])


def gather_rel(x, order, count):
    x = x[None]
    for mask in order:
        x = jnp.concatenate([x, trade(x, mask, count)], axis=0)
    return x


def scatter_rel(x, order, count):
    for mask in reversed(order):
        half = x.shape[0] // 2
        x = x[:half].astype(F32) + trade(x[half:].astype(BF), mask, count).astype(F32)
    return x[0]


def gather_abs(x, order, count, me):
    done = []
    for mask in order:
        other = trade(x, mask, count)
        axis = sum(m > mask for m in done)
        mine, other = jnp.expand_dims(x, axis), jnp.expand_dims(other, axis)
        x = jnp.where(
            (me & mask) != 0,
            jnp.concatenate([other, mine], axis),
            jnp.concatenate([mine, other], axis),
        )
        done.append(mask)
    return x.reshape(-1, x.shape[-1])


def scatter_abs(x, order, count, me):
    steps = len(order)
    x = x.reshape((2,) * steps + (x.shape[0] // count, x.shape[1]))
    left = sorted(order, reverse=True)
    for mask in order:
        axis = left.index(mask)
        left.remove(mask)
        bit = ((me & mask) != 0).astype(jnp.int32)
        keep = lax.dynamic_index_in_dim(x, bit, axis, keepdims=False)
        send = lax.dynamic_index_in_dim(x, 1 - bit, axis, keepdims=False)
        x = keep.astype(F32) + trade(send.astype(BF), mask, count).astype(F32)
    return x


def sum_all(x, order, count):
    for mask in order:
        x = x + trade(x, mask, count)
    return x


def share_seq(x, seq_count, count):
    return jnp.concatenate([x] + [trade(x, m, count) for m in range(1, seq_count)], axis=0)


def windows(width):
    size = width // H
    for pair in range(H // 2):
        base = (pair // 2) * 4 * size + (pair % 2) * 128
        yield pair, base, (2 * pair * size - base, (2 * pair + 1) * size - base, (2 * pair + 2) * size - base)


def stacked(rows, edges):
    column = lax.broadcasted_iota(jnp.int32, rows.shape, 1)
    first = (column >= edges[0]) & (column < edges[1])
    second = (column >= edges[1]) & (column < edges[2])
    zero = jnp.zeros_like(rows)
    return jnp.concatenate([jnp.where(first, rows, zero), jnp.where(second, rows, zero)], axis=0)


def unstacked(both, edges):
    count = both.shape[0] // 2
    column = lax.broadcasted_iota(jnp.int32, (count, both.shape[1]), 1)
    first = (column >= edges[0]) & (column < edges[1])
    second = (column >= edges[1]) & (column < edges[2])
    return jnp.where(first, both[:count], jnp.where(second, both[count:], 0.0))


def masked_scores(seen, queries, keys, media_rows):
    scores = dot(queries, keys, ((1,), (1,)))
    place = lax.broadcasted_iota(jnp.int32, scores.shape, 1)
    return jnp.where((place < seen) | (place >= media_rows), scores, -1e30)


def attend_kernel(media_rows, seen_ref, q_ref, k_ref, v_ref, out_ref, stat_ref):
    count, width = q_ref.shape
    seen = seen_ref[0]
    lane = lax.broadcasted_iota(jnp.int32, (count, 128), 1)
    stats = jnp.zeros((count, 128), F32)
    carry = None
    for pair, base, edges in windows(width):
        cols = slice(base, base + 256)
        scores = masked_scores(seen, stacked(q_ref[:, cols], edges), k_ref[:, cols], media_rows)
        top = jnp.max(scores, axis=1, keepdims=True)
        probs = jnp.exp(scores - top)
        total = jnp.sum(probs, axis=1, keepdims=True)
        mixed = unstacked(dot(probs.astype(BF), v_ref[:, cols]), edges)
        if pair % 2 == 0:
            out_ref[:, base : base + 128] = mixed[:, :128]
            carry = mixed[:, 128:]
        else:
            out_ref[:, base : base + 128] = carry + mixed[:, :128]
            out_ref[:, base + 128 : base + 256] = mixed[:, 128:]
        for k in range(2):
            rows = slice(k * count, (k + 1) * count)
            stats = jnp.where(lane == 2 * pair + k, top[rows], stats)
            stats = jnp.where(lane == H + 2 * pair + k, total[rows], stats)
    stat_ref[...] = stats


def attend_back_kernel(
    media_rows, seen_ref, q_ref, g_ref, stat_ref, k_ref, v_ref, dq_ref, dk_ref, dv_ref
):
    count, width = q_ref.shape
    seen = seen_ref[0]
    lane = lax.broadcasted_iota(jnp.int32, (count, 128), 1)
    stats = stat_ref[...]

    def column(at):
        parts = [
            jnp.sum(jnp.where(lane == at + k, stats, 0.0), axis=1, keepdims=True) for k in range(2)
        ]
        return jnp.concatenate(parts, axis=0)

    carry = None
    for pair, base, edges in windows(width):
        cols = slice(base, base + 256)
        queries, grads = stacked(q_ref[:, cols], edges), stacked(g_ref[:, cols], edges)
        keys, values = k_ref[:, cols], v_ref[:, cols]
        scores = masked_scores(seen, queries, keys, media_rows)
        probs = jnp.exp(scores - column(2 * pair))
        prob_grad = dot(grads, values, ((1,), (1,)))
        score_grad = (probs * (prob_grad - column(H + 2 * pair))).astype(BF)
        dq = unstacked(dot(score_grad, keys), edges)
        dk = dot(score_grad, queries, ((0,), (0,)))
        dv = dot(probs.astype(BF), grads, ((0,), (0,)))
        if pair % 2 == 0:
            dq_ref[:, base : base + 128] = dq[:, :128]
            dk_ref[:, base : base + 128] = dk[:, :128].astype(BF)
            dv_ref[:, base : base + 128] = dv[:, :128].astype(BF)
            carry = (dq[:, 128:], dk[:, 128:], dv[:, 128:])
        else:
            for ref, full, old in zip((dq_ref, dk_ref, dv_ref), (dq, dk, dv), carry):
                ref[:, base : base + 128] = (old + full[:, :128]).astype(ref.dtype)
                ref[:, base + 128 : base + 256] = full[:, 128:].astype(ref.dtype)


def call(kernel, inputs, outputs, flops):
    smem = pl.BlockSpec(memory_space=pltpu.SMEM)
    vmem = pl.BlockSpec(memory_space=pltpu.VMEM)
    nbytes = sum(x.size * x.dtype.itemsize for x in inputs)
    nbytes += sum(x.size * x.dtype.itemsize for x in outputs)
    return pl.pallas_call(
        kernel,
        out_shape=tuple(outputs),
        in_specs=[smem] + [vmem] * (len(inputs) - 1),
        out_specs=tuple(vmem for _ in outputs),
        compiler_params=pltpu.CompilerParams(vmem_limit_bytes=40 << 20),
        cost_estimate=pl.CostEstimate(flops=flops, bytes_accessed=nbytes, transcendentals=0),
    )(*inputs)


def shards(
    media,
    latents,
    frames,
    time_embed,
    media_gain,
    media_bias,
    latent_gain,
    latent_bias,
    ffn_gain,
    ffn_bias,
    w_query,
    w_key,
    w_value,
    w_out,
    w_up,
    w_down,
    grad_out,
):
    item_count, seq_count = lax.axis_size("items"), lax.axis_size("seq")
    count = item_count * seq_count
    seq_index = lax.axis_index("seq")
    me = lax.axis_index("items") * seq_count + seq_index
    unused_items, media_rows, width = media.shape
    latent_rows = latents.shape[1]
    head_size = width // H
    frames_here = media_rows // PATCH
    scaling = head_size ** (-0.5)

    item_bits = [m for m in (1 << k for k in reversed(range(30))) if seq_count <= m < count]
    seq_bits = [m for m in (1 << k for k in reversed(range(30))) if m < seq_count]
    order_a = item_bits + seq_bits
    order_b = item_bits[:-1] + seq_bits[:-1] + item_bits[-1:] + seq_bits[-1:]
    orders = (order_a, order_b)

    def gather_rows(x):
        half = x.shape[0] // 2
        return jnp.concatenate(
            [
                gather_rel(part, order, count).reshape(-1, x.shape[1])
                for part, order in zip((x[:half], x[half:]), orders)
            ],
            axis=0,
        )

    def scatter_rows(x):
        half = x.shape[0] // 2
        return jnp.concatenate(
            [
                scatter_rel(part.reshape(count, -1, x.shape[1]), order, count)
                for part, order in zip((x[:half], x[half:]), orders)
            ],
            axis=0,
        )

    key_full = gather_abs(w_key, order_a, count, me)
    query_full = gather_abs(w_query, order_b, count, me)
    value_full = gather_abs(w_value, order_a, count, me)
    out_full = gather_abs(w_out, order_b, count, me)

    time_rows = lax.dynamic_slice_in_dim(time_embed, seq_index * frames_here, frames_here, 0)
    shifted = (
        media[0].astype(F32).reshape(frames_here, PATCH, width) + time_rows[:, None, :]
    ).reshape(media_rows, width)
    media_normed, media_unit, media_rstd = layer_norm(shifted, media_gain, media_bias)
    latent_in = latents[0].astype(F32)
    latent_normed, latent_unit, latent_rstd = layer_norm(latent_in, latent_gain, latent_bias)
    latent_normed = latent_normed.astype(BF)
    sources = jnp.concatenate([media_normed.astype(BF), latent_normed], axis=0)

    queries = share_seq(
        (dot(latent_normed, query_full) * scaling).astype(BF), seq_count, count
    )
    keys = dot(sources, key_full).astype(BF)
    values = dot(sources, value_full).astype(BF)
    seen = jnp.clip((frames - seq_index * frames_here) * PATCH, 0, media_rows).astype(jnp.int32)
    all_rows = queries.shape[0]
    pair_flops = 2 * H // 2 * 2 * all_rows * 256 * sources.shape[0]
    mixed, stats = call(
        lambda *refs: attend_kernel(media_rows, *refs),
        (seen, queries, keys, values),
        (jax.ShapeDtypeStruct((all_rows, width), F32), jax.ShapeDtypeStruct((all_rows, 128), F32)),
        2 * pair_flops,
    )

    def own_parts(x):
        blocks = x.reshape(seq_count, latent_rows, x.shape[1])
        return jnp.stack([blocks[0]] + [trade(blocks[m], m, count) for m in range(1, seq_count)])

    mixed_parts, stat_parts = own_parts(mixed), own_parts(stats)
    tops, totals = stat_parts[:, :, :H], stat_parts[:, :, H : 2 * H]
    top = jnp.max(tops, axis=0)
    weights = jnp.exp(tops - top)
    total = jnp.sum(weights * totals, axis=0)
    weights = weights / total
    log_total = top + jnp.log(total)
    mixture_wide = jnp.sum(
        mixed_parts.reshape(seq_count, latent_rows, H, head_size) * weights[..., None], axis=0
    ).reshape(latent_rows, width)
    mixture = mixture_wide.astype(BF)

    hidden = latent_in + dot(mixture, out_full)
    ffn_in, ffn_unit, ffn_rstd = layer_norm(hidden, ffn_gain, ffn_bias)
    ffn_in = ffn_in.astype(BF)

    up_mine = lax.all_to_all(w_up, AXES, split_axis=1, concat_axis=0, tiled=True)
    grad_rows = gather_rows(grad_out[0])
    ffn_rows = gather_rows(ffn_in)
    pre_act = dot(ffn_rows, up_mine)
    active, gelu_back = jax.vjp(jax.nn.gelu, pre_act)
    active = active.astype(BF)
    active_grad = dot(grad_rows, w_down, ((1,), (1,)))
    pre_grad = gelu_back(active_grad)[0].astype(BF)
    ffn_in_grad = scatter_rows(dot(pre_grad, up_mine, ((1,), (1,))))
    latents_out = hidden + scatter_rows(dot(active, w_down))
    down_grad = dot(active, grad_rows, ((0,), (0,)))
    up_grad_mine = dot(ffn_rows, pre_grad, ((0,), (0,))).astype(BF)
    up_grad = lax.all_to_all(up_grad_mine, AXES, split_axis=0, concat_axis=1, tiled=True)

    hidden_norm_grad, ffn_gain_grad, ffn_bias_grad = layer_norm_back(
        ffn_in_grad, ffn_unit, ffn_rstd, ffn_gain
    )
    hidden_grad = grad_out[0].astype(F32) + hidden_norm_grad
    attended_low = hidden_grad.astype(BF)
    mixture_grad = dot(attended_low, out_full, ((1,), (1,))).astype(BF)
    inner = jnp.sum(
        (mixture_wide * mixture_grad.astype(F32)).reshape(latent_rows, H, head_size), axis=-1
    )
    back_stats = jnp.concatenate(
        [log_total, inner, jnp.zeros((latent_rows, 128 - 2 * H), F32)], axis=1
    )
    query_part, key_row_grad, value_row_grad = call(
        lambda *refs: attend_back_kernel(media_rows, *refs),
        (
            seen,
            queries,
            share_seq(mixture_grad, seq_count, count),
            share_seq(back_stats, seq_count, count),
            keys,
            values,
        ),
        (
            jax.ShapeDtypeStruct((all_rows, width), F32),
            jax.ShapeDtypeStruct(keys.shape, BF),
            jax.ShapeDtypeStruct(keys.shape, BF),
        ),
        5 * pair_flops,
    )
    query_row_grad = jnp.sum(own_parts(query_part), axis=0).astype(BF)

    value_grad = scatter_abs(
        dot(sources, value_row_grad, ((0,), (0,))), order_a[::-1], count, me
    )
    key_grad = scatter_abs(dot(sources, key_row_grad, ((0,), (0,))), order_b[::-1], count, me)
    share = width // count

    def my_columns(x):
        return lax.dynamic_slice_in_dim(x, me * share, share, 1)

    out_grad = dot(my_columns(gather_rows(mixture)), gather_rows(attended_low), ((0,), (0,)))
    query_grad = scaling * dot(
        my_columns(gather_rows(latent_normed)), gather_rows(query_row_grad), ((0,), (0,))
    )

    source_grad = dot(key_row_grad, key_full, ((1,), (1,))) + dot(
        value_row_grad, value_full, ((1,), (1,))
    )
    latent_norm_grad = (
        source_grad[media_rows:] + dot(query_row_grad, query_full, ((1,), (1,))) * scaling
    )
    shifted_grad, media_gain_grad, media_bias_grad = layer_norm_back(
        source_grad[:media_rows], media_unit, media_rstd, media_gain
    )
    frame_sums = jnp.sum(shifted_grad.reshape(frames_here, PATCH, width), axis=1)
    time_local = lax.dynamic_update_slice_in_dim(
        jnp.zeros((FRAMES, width), F32), frame_sums, seq_index * frames_here, 0
    )
    latent_in_grad, latent_gain_grad, latent_bias_grad = layer_norm_back(
        latent_norm_grad, latent_unit, latent_rstd, latent_gain
    )
    latents_grad = hidden_grad + latent_in_grad
    sums = jnp.concatenate(
        [
            time_local,
            jnp.stack(
                [
                    media_gain_grad,
                    media_bias_grad,
                    latent_gain_grad,
                    latent_bias_grad,
                    ffn_gain_grad,
                    ffn_bias_grad,
                    jnp.zeros((width,), F32),
                    jnp.zeros((width,), F32),
                ]
            ),
        ],
        axis=0,
    )
    sums = sum_all(sums, order_a, count)
    return (
        latents_out.astype(BF)[None],
        latents_grad.astype(BF)[None],
        shifted_grad.astype(BF)[None],
        sums[:FRAMES],
        sums[FRAMES],
        sums[FRAMES + 1],
        sums[FRAMES + 2],
        sums[FRAMES + 3],
        sums[FRAMES + 4],
        sums[FRAMES + 5],
        query_grad,
        key_grad,
        value_grad,
        out_grad,
        up_grad.astype(F32),
        down_grad,
    )


def solution(mesh):
    rows, split = P("items", "seq", None), P(AXES, None)
    return jax.shard_map(
        shards,
        mesh=mesh,
        in_specs=(rows, rows, P("items")) + (P(),) * 7 + (split,) * 6 + (rows,),
        out_specs=(rows,) * 3 + (P(),) * 7 + (split,) * 6,
        check_vma=False,
    )
```

```python
import jax
import jax.numpy as jnp
from jax import lax
from jax.experimental import pallas as pl
from jax.experimental.pallas import tpu as pltpu
from jax.sharding import PartitionSpec as P

H = 16
FRAMES = 8
PATCH = 256
AXES = ("items", "seq")
BF = jnp.bfloat16
F32 = jnp.float32


def layer_norm(values, gain, bias):
    center = jnp.mean(values, axis=-1, keepdims=True)
    spread = jnp.mean(jnp.square(values - center), axis=-1, keepdims=True)
    rstd = lax.rsqrt(spread + 1e-05)
    unit = (values - center) * rstd
    return unit * gain + bias, unit, rstd


def layer_norm_back(grad, unit, rstd, gain):
    scaled = grad * gain
    inner = scaled - jnp.mean(scaled, axis=-1, keepdims=True)
    inner = inner - unit * jnp.mean(scaled * unit, axis=-1, keepdims=True)
    return inner * rstd, jnp.sum(grad * unit, axis=0), jnp.sum(grad, axis=0)


def dot(a, b, dims=((1,), (0,))):
    return lax.dot_general(a, b, (dims, ((), ())), preferred_element_type=F32)


def trade(x, mask, count):
    return lax.ppermute(x, AXES, [(i, i ^ mask) for i in range(count)])


def after(x, *others):
    return lax.optimization_barrier((x,) + others)[0]


class Gather:
    def __init__(self, x, order, me):
        self.x, self.order, self.me, self.done = x, list(order), me, []

    def send(self):
        return self.x, self.order[0]

    def take(self, sent, other):
        mask = self.order.pop(0)
        axis = sum(m > mask for m in self.done)
        mine, other = jnp.expand_dims(sent, axis), jnp.expand_dims(other, axis)
        self.x = jnp.where(
            (self.me & mask) != 0,
            jnp.concatenate([other, mine], axis),
            jnp.concatenate([mine, other], axis),
        )
        self.done.append(mask)


class GatherRel:
    def __init__(self, x, order):
        self.order, self.x = list(order), x

    def send(self):
        return self.x, self.order[0]

    def take(self, sent, other):
        self.order.pop(0)
        self.x = jnp.concatenate([sent, other], axis=0)


class GatherApart(GatherRel):
    def take(self, sent, other):
        if len(self.order) > 2:
            GatherRel.take(self, sent, other)
        else:
            self.order.pop(0)
            self.x = (sent, other)

    def last(self, count, token):
        mask = self.order.pop(0)
        pieces = lax.optimization_barrier(tuple(self.x) + (token,))[:2]
        self.x = [*pieces, *[trade(x, mask, count) for x in pieces]]
        return pieces[0]


class Halves:
    def __init__(self, keep, send, orders):
        self.orders, self.keep, self.sends = [list(order) for order in orders], keep, send

    def step(self, count, wait=()):
        sent = lax.optimization_barrier(tuple(self.sends) + tuple(wait))
        masks = [order.pop() for order in self.orders]
        self.others = [trade(x, mask, count) for x, mask in zip(sent, masks)]
        self.token = sent[0]

    def split(self, parts=1):
        self.keep, self.sends = add_split(self.keep, self.others, parts)

    def total(self):
        return [k.astype(F32) + o.astype(F32) for k, o in zip(self.keep, self.others)]


def add_split_kernel(pairs, *refs):
    ins, outs = refs[: 4 * pairs], refs[4 * pairs :]
    for k in range(pairs):
        keep, keep2, other, other2 = ins[4 * k : 4 * k + 4]
        out, send = outs[2 * k : 2 * k + 2]
        out[...] = (keep[...].astype(F32) + other[...].astype(F32)).reshape(out.shape)
        send[...] = (keep2[...].astype(F32) + other2[...].astype(F32)).astype(BF).reshape(send.shape)


def add_split(keeps, others, parts=1):
    shape = keeps[0].shape[-3:]
    half = shape[0] // 2
    some = min(half, 2)
    ins, specs, outs = [], [], []
    for keep, other in zip(keeps, others):
        for part in range(parts):

            def spec(at, part=part):
                if parts == 1:
                    return pl.BlockSpec((some,) + shape[1:], lambda i: (i + at, 0, 0))
                return pl.BlockSpec((1, some) + shape[1:], lambda i: (part, i + at, 0, 0))

            ins += [keep, keep, other, other]
            specs += [spec(0), spec(half // some), spec(0), spec(half // some)]
            outs += [
                jax.ShapeDtypeStruct((half,) + shape[1:], F32),
                jax.ShapeDtypeStruct((half,) + shape[1:], BF),
            ]
    out = pl.pallas_call(
        lambda *refs: add_split_kernel(len(ins) // 4, *refs),
        grid=(half // some,),
        out_shape=tuple(outs),
        in_specs=specs,
        out_specs=tuple(pl.BlockSpec((some,) + shape[1:], lambda i: (i, 0, 0)) for x in outs),
        compiler_params=pltpu.CompilerParams(vmem_limit_bytes=56 << 20),
        cost_estimate=pl.CostEstimate(
            flops=1, bytes_accessed=sum(6 * x.size for x in outs), transcendentals=0
        ),
    )(*ins)
    return list(out[::2]), list(out[1::2])


class Sum:
    def __init__(self, x, order):
        self.order, self.x = list(order), x

    def send(self):
        return self.x, self.order[0]

    def take(self, sent, other):
        self.order.pop(0)
        self.x = self.x + other


def exchange(count, *jobs, wait=()):
    sends = [job.send() for job in jobs]
    sent = lax.optimization_barrier(tuple(x for x, unused in sends) + tuple(wait))
    for job, x, (unused, mask) in zip(jobs, sent, sends):
        job.take(x, trade(x, mask, count))
    return sent[0]


def share_seq(x, seq_count, count):
    return jnp.concatenate([x] + [trade(x, m, count) for m in range(1, seq_count)], axis=0)


def windows(width):
    size = width // H
    for pair in range(H // 2):
        base = (pair // 2) * 4 * size + (pair % 2) * 128
        yield pair, base, (2 * pair * size - base, (2 * pair + 1) * size - base, (2 * pair + 2) * size - base)


def stacked(rows, edges):
    column = lax.broadcasted_iota(jnp.int32, rows.shape, 1)
    first = (column >= edges[0]) & (column < edges[1])
    second = (column >= edges[1]) & (column < edges[2])
    zero = jnp.zeros_like(rows)
    return jnp.concatenate([jnp.where(first, rows, zero), jnp.where(second, rows, zero)], axis=0)


def unstacked(both, edges):
    count = both.shape[0] // 2
    column = lax.broadcasted_iota(jnp.int32, (count, both.shape[1]), 1)
    first = (column >= edges[0]) & (column < edges[1])
    second = (column >= edges[1]) & (column < edges[2])
    return jnp.where(first, both[:count], jnp.where(second, both[count:], 0.0))


def masked_scores(seen, queries, keys, media_rows):
    scores = dot(queries, keys, ((1,), (1,)))
    place = lax.broadcasted_iota(jnp.int32, scores.shape, 1)
    return jnp.where((place < seen) | (place >= media_rows), scores, -1e30)


def attend_kernel(media_rows, seen_ref, q_ref, kv_ref, out_ref):
    count, width = q_ref.shape
    seen = seen_ref[0]
    lane = lax.broadcasted_iota(jnp.int32, (count, 128), 1)
    stats = jnp.zeros((count, 128), F32)
    carry = None
    for pair, base, edges in windows(width):
        cols, value_cols = slice(base, base + 256), slice(width + base, width + base + 256)
        scores = masked_scores(seen, stacked(q_ref[:, cols], edges), kv_ref[:, cols], media_rows)
        top = jnp.max(scores, axis=1, keepdims=True)
        probs = jnp.exp(scores - top)
        total = jnp.sum(probs, axis=1, keepdims=True)
        mixed = unstacked(dot(probs.astype(BF), kv_ref[:, value_cols]) / total, edges)
        if pair % 2 == 0:
            out_ref[:, base : base + 128] = mixed[:, :128].astype(BF)
            carry = mixed[:, 128:]
        else:
            out_ref[:, base : base + 128] = (carry + mixed[:, :128]).astype(BF)
            out_ref[:, base + 128 : base + 256] = mixed[:, 128:].astype(BF)
        for k in range(2):
            rows = slice(k * count, (k + 1) * count)
            for n, value in enumerate((top, total)):
                value = value[rows]
                for term in range(3):
                    low = value.astype(BF).astype(F32)
                    stats = jnp.where(lane == (3 * n + term) * H + 2 * pair + k, low, stats)
                    value = value - low
    out_ref[:, width:] = stats.astype(BF)


def attend_back_kernel(media_rows, pieces, seen_ref, q_ref, kv_ref, *refs):
    dq_ref, dkv_ref = refs[pieces:]
    count, width = q_ref.shape
    seen = seen_ref[0]
    lane = lax.broadcasted_iota(jnp.int32, (count, 128), 1)
    packed = jnp.concatenate([ref[...] for ref in refs[:pieces]], axis=0)
    stats = packed[:, width:].astype(F32)

    def column(at):
        parts = []
        for k in range(2):
            here = (lane == at + k) | (lane == at + H + k) | (lane == at + 2 * H + k)
            parts.append(jnp.sum(jnp.where(here, stats, 0.0), axis=1, keepdims=True))
        return jnp.concatenate(parts, axis=0)

    carry = None
    for pair, base, edges in windows(width):
        cols = slice(base, base + 256)
        queries, grads = stacked(q_ref[:, cols], edges), stacked(packed[:, cols], edges)
        keys, values = kv_ref[:, cols], kv_ref[:, width + base : width + base + 256]
        scores = masked_scores(seen, queries, keys, media_rows)
        probs = jnp.exp(scores - column(2 * pair))
        prob_grad = dot(grads, values, ((1,), (1,)))
        score_grad = (probs * (prob_grad - column(3 * H + 2 * pair))).astype(BF)
        new = (
            (dq_ref, 0, dot(score_grad, keys)),
            (dkv_ref, 0, dot(score_grad, queries, ((0,), (0,)))),
            (dkv_ref, width, dot(probs.astype(BF), grads, ((0,), (0,)))),
        )
        new = [(ref, at + base, unstacked(x, edges) if ref is dq_ref else x) for ref, at, x in new]
        if pair % 2 == 0:
            for ref, at, x in new:
                ref[:, at : at + 128] = x[:, :128].astype(BF)
            carry = [x[:, 128:] for unused_ref, unused_at, x in new]
        else:
            for (ref, at, x), old in zip(new, carry):
                ref[:, at : at + 128] = (old + x[:, :128]).astype(BF)
                ref[:, at + 128 : at + 256] = x[:, 128:].astype(BF)


def lane_heads(shape, width, dim):
    lane = lax.broadcasted_iota(jnp.int32, shape, dim)
    column = lax.broadcasted_iota(jnp.int32, shape, 1 - dim)
    size = width // H
    first = (lane % H) * size
    return lane // H, column - first, (column >= first) & (column < first + size)


def three_terms(x):
    terms = []
    for unused in range(3):
        terms.append(x.astype(BF))
        x = x - terms[-1].astype(F32)
    return terms


def combine_kernel(pieces, whole, me_ref, *refs):
    parts, refs = refs[:pieces], refs[pieces:]
    latent_ref, gain_ref, bias_ref, *refs = refs
    *refs, wide_ref, low_ref, stat_ref, hidden_ref, ffn_ref, w_ref, sems = refs
    waits = whole.fetch(me_ref[0], refs, w_ref, sems)
    rows, width = latent_ref.shape
    group, unused, inside = lane_heads((128, width), width, 0)
    spread_top = jnp.where(inside & (group < 3), 1.0, 0.0).astype(BF)
    spread_total = jnp.where(inside & (group >= 3) & (group < 6), 1.0, 0.0).astype(BF)
    tops = [dot(ref[:, width:], spread_top) for ref in parts]
    top = tops[0]
    for other in tops[1:]:
        top = jnp.maximum(top, other)
    total = jnp.zeros((rows, width), F32)
    mixed = jnp.zeros((rows, width), F32)
    for ref, mine in zip(parts, tops):
        weight = jnp.exp(mine - top) * dot(ref[:, width:], spread_total)
        total += weight
        mixed += weight * ref[:, :width].astype(F32)
    mixed = mixed / total
    wide_ref[...] = mixed
    low = mixed.astype(BF)
    low_ref[...] = low
    group, offset, unused = lane_heads((width, 128), width, 1)
    stats = jnp.zeros((rows, 128), F32)
    for k, term in enumerate(three_terms(top + jnp.log(total))):
        pick = jnp.where((group == k) & (offset == 0), 1.0, 0.0).astype(BF)
        stats += dot(term, pick)
    stat_ref[...] = stats
    for wait in waits:
        wait.wait()
    hidden = latent_ref[...].astype(F32) + dot(low, w_ref[...])
    hidden_ref[...] = hidden
    ffn_ref[...] = layer_norm(hidden, gain_ref[...], bias_ref[...])[0].astype(BF)


def hidden_back_kernel(whole, me_ref, *refs):
    keep_ref, other_ref, hidden_ref, upstream_ref, wide_ref, stat_ref, gain_ref, *refs = refs
    *refs, hidden_grad_ref, low_ref, packed_ref, sums_ref, w_ref, sems = refs
    waits = whole.fetch(me_ref[0], refs, w_ref, sems)
    rows, width = hidden_ref.shape
    grad = keep_ref[0].astype(F32) + other_ref[0].astype(F32)
    gain = gain_ref[...]
    unused, unit, rstd = layer_norm(hidden_ref[...], gain, gain)
    norm_grad, gain_grad, bias_grad = layer_norm_back(grad, unit, rstd, gain)
    row = lax.broadcasted_iota(jnp.int32, (8, width), 0)
    sums_ref[...] = jnp.where(row == 0, gain_grad[None], jnp.where(row == 1, bias_grad[None], 0.0))
    hidden_grad = upstream_ref[...].astype(F32) + norm_grad
    hidden_grad_ref[...] = hidden_grad
    low = hidden_grad.astype(BF)
    low_ref[...] = low
    for wait in waits:
        wait.wait()
    mixture_grad = dot(low, w_ref[...], ((1,), (1,))).astype(BF)
    packed_ref[:, :width] = mixture_grad
    group, unused, inside = lane_heads((width, 128), width, 1)
    heads = jnp.where(inside & (group >= 3) & (group < 6), 1.0, 0.0).astype(BF)
    inner = jnp.zeros((rows, 128), F32)
    for term in three_terms(wide_ref[...] * mixture_grad.astype(F32)):
        inner += dot(term, heads)
    lane = lax.broadcasted_iota(jnp.int32, (rows, 128), 1) // H
    stats = stat_ref[...]
    for k, term in enumerate(three_terms(inner)):
        stats = jnp.where(lane == 3 + k, term.astype(F32), stats)
    packed_ref[:, width:] = stats.astype(BF)


def owner_of(place, order):
    return sum(mask for k, mask in enumerate(order) if (place >> k) % 2)


def place_of(owner, order):
    return sum(((owner // mask) % 2) << k for k, mask in enumerate(order))


class Stacks:
    def __init__(self, parts, orders):
        self.each = len(parts[0])
        self.arrays = [x for pieces in parts for x in pieces]
        self.orders = orders
        self.cols = sum(pieces[0].shape[2] for pieces in parts)
        self.ends = [parts[0][0].shape[2] * (k + 1) for k in range(len(parts))]

    def fetch(self, me, refs, into, sems):
        at, waits = 0, []
        for k, order in enumerate(self.orders):
            pieces = refs[self.each * k : self.each * (k + 1)]
            some, block, cols = pieces[0].shape
            for place in range(self.each * some):
                owner = me ^ owner_of(place, order)
                to = into.at[pl.ds(pl.multiple_of(owner * block, 16), block), at : at + cols]
                source = pieces[place // some].at[place % some]
                pltpu.make_async_copy(source, to, sems.at[k]).start()
            part = into.at[:, at : at + cols]
            waits.append(pltpu.make_async_copy(part, part, sems.at[k]))
            at += cols
        return waits


class Plain:
    def __init__(self, x):
        self.arrays, self.orders = [x], (None,)
        self.cols = x.shape[1]
        self.ends = [self.cols]

    def fetch(self, me, refs, into, sems):
        copy = pltpu.make_async_copy(refs[0], into, sems.at[0])
        copy.start()
        return [copy]


def halves_kernel(me_ref, s_ref, mine_ref, other_ref):
    block = 48
    for parity in range(2):

        @pl.when(me_ref[0] % 2 == parity)
        def _():
            for out_ref, which in ((mine_ref, parity), (other_ref, 1 - parity)):
                for n in range(out_ref.shape[1] // block):
                    at = (2 * n + which) * block
                    out_ref[:, n * block : (n + 1) * block] = s_ref[:, at : at + block]


def order_kernel(whole, me_ref, *refs):
    *refs, out_ref, sems = refs
    for wait in whole.fetch(me_ref[0], refs, out_ref, sems):
        wait.wait()


def project_kernel(whole, me_ref, s_ref, *refs):
    *refs, out_ref, w_ref, sems = refs
    at = 0
    for wait, end in zip(whole.fetch(me_ref[0], refs, w_ref, sems), whole.ends):
        wait.wait()
        out_ref[:, at:end] = dot(s_ref[...], w_ref[:, at:end]).astype(BF)
        at = end


def gelu_parts(x):
    c = 0.7978845608028654
    t = jnp.tanh(c * (x + 0.044715 * (x * x * x)))
    slope = 0.5 * (1.0 + t) + 0.5 * x * (1.0 - t * t) * (c * (1.0 + 3 * 0.044715 * (x * x)))
    return 0.5 * x * (1.0 + t), slope


def ffn_kernel(
    order,
    me_ref,
    mine_ref,
    other_ref,
    up_ref,
    down_ref,
    all_ref,
    keep_ref,
    send_ref,
    active_ref,
    pre_ref,
    rows_ref,
    grad_rows_ref,
    sem,
):
    some, each, width = mine_ref.shape
    for place in range(2 * some):
        owner = me_ref[0] ^ owner_of(place, order)
        pltpu.make_async_copy(
            all_ref.at[owner, :, width : 2 * width],
            grad_rows_ref.at[place * each : (place + 1) * each],
            sem,
        ).start()
    rows_ref[: some * each, :] = mine_ref[...].reshape(some * each, width)
    rows_ref[some * each :, :] = other_ref[...].reshape(some * each, width)
    active, slope = gelu_parts(dot(rows_ref[...], up_ref[...]))
    active_ref[...] = active.astype(BF)
    pltpu.make_async_copy(grad_rows_ref, grad_rows_ref, sem).wait()
    pre_grad = (dot(grad_rows_ref[...], down_ref[...], ((1,), (1,))) * slope).astype(BF)
    pre_ref[...] = pre_grad
    total = dot(pre_grad, up_ref[...], ((1,), (1,)))
    keep_ref[...] = total[: some * each].reshape(keep_ref.shape)
    send_ref[...] = total[some * each :].astype(BF).reshape(send_ref.shape)


def ffn_sums_kernel(
    rows_ref,
    grad_rows_ref,
    active_ref,
    pre_ref,
    down_ref,
    down_keep_ref,
    down_send_ref,
    up_ref,
    keep_ref,
    send_ref,
):
    first = ((0,), (0,))
    units = down_keep_ref.shape[0]
    down = dot(active_ref[...], grad_rows_ref[...], first)
    down_keep_ref[...] = down[:units]
    down_send_ref[...] = down[units:].astype(BF)
    up_ref[...] = dot(rows_ref[...], pre_ref[...], first).astype(BF)
    out = dot(active_ref[...], down_ref[...])
    half = out.shape[0] // 2
    keep_ref[...] = out[:half].reshape(keep_ref.shape)
    send_ref[...] = out[half:].astype(BF).reshape(send_ref.shape)


def source_kernel(whole, me_ref, g_ref, media_ref, time_ref, gain_ref, *refs):
    *refs, media_grad_ref, latent_ref, sums_ref, acc_ref, w_ref, sems = refs
    at = 0
    for wait, end in zip(whole.fetch(me_ref[0], refs, w_ref, sems), whole.ends):
        wait.wait()
        new = dot(g_ref[:, at:end], w_ref[:, at:end], ((1,), (1,)))
        acc_ref[...] = acc_ref[...] + new if at else new
        at = end
    media_rows, width = media_ref.shape
    gain = gain_ref[...]
    rows = [jnp.zeros((1, width), F32), jnp.zeros((1, width), F32)]
    for frame in range(media_rows // PATCH):
        here = slice(frame * PATCH, (frame + 1) * PATCH)
        shifted = media_ref[here, :].astype(F32) + time_ref[frame : frame + 1, :]
        unused, unit, rstd = layer_norm(shifted, gain, gain)
        grad = acc_ref[here, :]
        shifted_grad, gain_grad, bias_grad = layer_norm_back(grad, unit, rstd, gain)
        media_grad_ref[here, :] = shifted_grad.astype(BF)
        rows[0] += gain_grad[None]
        rows[1] += bias_grad[None]
        rows.append(jnp.sum(shifted_grad, axis=0, keepdims=True))
    at = lax.broadcasted_iota(jnp.int32, sums_ref.shape, 0)
    sums = jnp.zeros(sums_ref.shape, F32)
    for k, row in enumerate(rows):
        sums = jnp.where(at == k, row, sums)
    sums_ref[...] = sums
    latent_ref[...] = acc_ref[media_rows:, :]


def latent_kernel(pieces, scaling, *refs):
    parts, refs = refs[:pieces], refs[pieces:]
    source_ref, latent_ref, gain_ref, hidden_grad_ref, out_ref, sums_ref = refs
    gain = gain_ref[...]
    width = gain.shape[1]
    query_side = sum(ref[:, :width].astype(F32) for ref in parts)
    grad = source_ref[...] + query_side * scaling
    unused, unit, rstd = layer_norm(latent_ref[...].astype(F32), gain, gain)
    latent_grad, gain_grad, bias_grad = layer_norm_back(grad, unit, rstd, gain)
    out_ref[...] = (hidden_grad_ref[...] + latent_grad).astype(BF)
    at = lax.broadcasted_iota(jnp.int32, sums_ref.shape, 0)
    sums_ref[...] = jnp.where(
        at == 0, gain_grad[None], jnp.where(at == 1, bias_grad[None], 0.0)
    )


def sums_kernel(orders, me_ref, s_ref, s2_ref, g_ref, g2_ref, *refs):
    *out_refs, s_held, g_held, held, sems = refs
    me = me_ref[0] - me_ref[0] % 2
    half, block, cols = out_refs[0].shape
    rows = s_ref.shape[0]
    for k, ref in enumerate((s_ref, s2_ref)):
        pltpu.make_async_copy(ref, s_held.at[k * rows : (k + 1) * rows], sems.at[0]).start()
    for part in range(len(orders)):
        columns = slice(part * cols, (part + 1) * cols)
        for k, ref in enumerate((g_ref, g2_ref)):
            to = g_held.at[k * rows : (k + 1) * rows, columns]
            pltpu.make_async_copy(ref.at[:, columns], to, sems.at[1 + part]).start()
    pltpu.make_async_copy(s_held, s_held, sems.at[0]).wait()
    some = held.shape[0]
    for part, order in enumerate(orders):
        columns = slice(part * cols, (part + 1) * cols)
        here = g_held.at[:, columns]
        pltpu.make_async_copy(here, here, sems.at[1 + part]).wait()
        first = (me // order[-1]) % 2
        for start in range(0, 2 * half, some):
            full = dot(s_held[:, start * block : (start + some) * block], here[...], ((0,), (0,)))
            held[...] = full.astype(BF).reshape(held.shape)
            for bit in range(2):

                @pl.when(first == bit)
                def _(bit=bit, start=start, part=part, order=order):
                    for n in range(some):
                        owner = 2 * (start + n)
                        place = place_of(owner ^ me, order) % half
                        send = (owner // order[-1]) % 2 != bit
                        out_refs[2 * part + send][place] = held[n]


SCALAR = pl.BlockSpec(memory_space=pltpu.SMEM)
FAR = pl.BlockSpec(memory_space=pl.ANY)


def call(kernel, inputs, outputs, flops, specs=(), far_outputs=False, scratch=()):
    specs = dict(specs)

    def whole(x):
        return pl.BlockSpec(x.shape, lambda i, nd=len(x.shape): (0,) * nd)

    nbytes = sum(x.size * x.dtype.itemsize for x in inputs)
    nbytes += sum(x.size * x.dtype.itemsize for x in outputs)
    return pl.pallas_call(
        kernel,
        grid=(1,),
        out_shape=tuple(outputs),
        in_specs=[specs.get(n, whole(x)) for n, x in enumerate(inputs)],
        out_specs=tuple(FAR if far_outputs else whole(x) for x in outputs),
        scratch_shapes=list(scratch),
        compiler_params=pltpu.CompilerParams(vmem_limit_bytes=56 << 20),
        cost_estimate=pl.CostEstimate(flops=flops, bytes_accessed=nbytes, transcendentals=0),
    )(*inputs)


def shards(
    media,
    latents,
    frames,
    time_embed,
    media_gain,
    media_bias,
    latent_gain,
    latent_bias,
    ffn_gain,
    ffn_bias,
    w_query,
    w_key,
    w_value,
    w_out,
    w_up,
    w_down,
    grad_out,
):
    item_count, seq_count = lax.axis_size("items"), lax.axis_size("seq")
    count = item_count * seq_count
    seq_index = lax.axis_index("seq")
    me = lax.axis_index("items") * seq_count + seq_index
    unused_items, media_rows, width = media.shape
    latent_rows = latents.shape[1]
    head_size = width // H
    frames_here = media_rows // PATCH
    scaling = head_size ** (-0.5)

    bits = [1 << k for k in reversed(range(30))]
    item_bits = [m for m in bits if seq_count <= m < count]
    seq_bits = [m for m in bits if m < seq_count]
    head, (fold, near), side, tail = item_bits[:-2], item_bits[-2:], seq_bits[0], seq_bits[1:]
    orders = (
        head + [fold, near, side] + tail,
        head + [side, fold, near] + tail,
        head + [near, side, fold] + tail,
    )
    ffn_order = head + [near, side] + tail
    block = width // count
    regular = block % 16 == 0

    def share(x):
        return jax.ShapeDtypeStruct(x, BF)

    latent_in = latents[0].astype(F32)
    latent_normed, latent_unit, latent_rstd = layer_norm(latent_in, latent_gain, latent_bias)
    latent_normed = latent_normed.astype(BF)
    time_rows = lax.dynamic_slice_in_dim(time_embed, seq_index * frames_here, frames_here, 0)
    shifted = (
        media[0].astype(F32).reshape(frames_here, PATCH, width) + time_rows[:, None, :]
    ).reshape(media_rows, width)
    media_normed, media_unit, media_rstd = layer_norm(shifted, media_gain, media_bias)
    sources = jnp.concatenate([media_normed.astype(BF), latent_normed], axis=0)

    def spread(x):
        x = x.reshape(x.shape[0], count, -1).transpose(1, 0, 2)
        pairs = x.reshape(-1, 2, fold, *x.shape[1:])
        pairs = jnp.concatenate([pairs[:, 1:], pairs[:, :1]], axis=1).reshape(x.shape)
        x = jnp.concatenate([x, pairs], axis=2)
        x = lax.all_to_all(x, AXES, split_axis=0, concat_axis=0, tiled=True)
        return x.reshape(-1, x.shape[2])

    cols_here = width // seq_count

    def seq_blocks(x, axis):
        return jnp.concatenate(
            [
                lax.dynamic_index_in_dim(x, seq_index ^ t, 0, keepdims=False)
                for t in range(seq_count)
            ],
            axis=axis,
        )

    def columns_of(x, m):
        return lax.dynamic_slice_in_dim(x, (seq_index ^ m) * cols_here, cols_here, 1)

    def reordered(x, m):
        blocks = x.reshape(seq_count, latent_rows, x.shape[1])
        return jnp.concatenate([blocks[t ^ m] for t in range(seq_count)], axis=0)

    parts = len(orders)
    units = w_down.shape[0]
    out_orders = (orders[0], head + [fold, side, near] + tail)
    if regular:
        first = GatherRel(jnp.concatenate([w_key, w_value], axis=1)[None], head)
        second = GatherRel(w_out[None], head + [fold])

        def split(x, orders, done):
            cols = x.shape[2] // len(orders)
            return [
                GatherApart(x[..., k * cols : (k + 1) * cols], order[done:])
                for k, order in enumerate(orders)
            ]

        down_job = GatherRel(w_down[None], [fold])
        started = exchange(count, first, down_job)
        while first.order:
            exchange(count, first)
        latent_item = share_seq(latent_normed, seq_count, count)
        pieces = [columns_of(w_query, m) for m in range(seq_count)]
        pieces = [pieces[0]] + [trade(pieces[m], m, count) for m in range(1, seq_count)]
        query_cols = Gather(
            seq_blocks(jnp.stack(pieces), 0), head + [near, fold], me
        )
        first = split(first.x, orders, len(head))
        started = exchange(count, *first, second, query_cols, wait=(down_job.x,))
        rows_all = lax.all_gather(
            jnp.concatenate([after(latent_normed, started), grad_out[0]], axis=1), AXES, axis=0
        )
        exchange(count, *first, second, query_cols)
        second = split(second.x, out_orders, len(head) + 1)
        started = exchange(count, *first)
        half_mine, half_other = call(
            halves_kernel,
            (me[None], after(sources, started)),
            (share((sources.shape[0], width // 2)),) * 2,
            0,
            specs={0: SCALAR},
        )
        half_other = trade(half_other, 1, count)
        for job in first:
            job.last(count, half_other)
        ready = [piece for job in first for piece in job.x]
        exchange(count, *second, query_cols, wait=ready)
        started = exchange(count, *second)
        up_pair = spread(after(w_up, *ready))
        key_value = Stacks([job.x for job in first], orders)
    else:
        started = w_key
        up_pair = spread(w_up)
        rows_all = lax.all_gather(
            jnp.concatenate([latent_normed, grad_out[0]], axis=1), AXES, axis=0
        )
        latent_item = share_seq(latent_normed, seq_count, count)
        pieces = [columns_of(w_query, m) for m in range(seq_count)]
        pieces = [pieces[0]] + [trade(pieces[m], m, count) for m in range(1, seq_count)]
        query_cols = Gather(seq_blocks(jnp.stack(pieces), 0), item_bits, me)
        down_job = GatherRel(w_down[None], [fold])
        exchange(count, down_job)
        both = lax.all_gather(jnp.concatenate([w_key, w_value], 1), AXES, axis=0, tiled=True)
        key_value = Plain(both)
        out_full = Plain(lax.all_gather(w_out, AXES, axis=0, tiled=True))

    def with_weights(kernel, inputs, whole, outputs, flops, keep=True, scratch=()):
        inputs = [me[None]] + list(inputs)
        specs = {0: SCALAR}
        for n in range(len(whole.arrays)):
            specs[len(inputs) + n] = FAR
        scratch = list(scratch) + ([pltpu.VMEM((width, whole.cols), BF)] if keep else [])
        return call(
            lambda *refs: kernel(whole, *refs),
            (*inputs, *whole.arrays),
            outputs,
            flops,
            specs=specs,
            scratch=scratch + [pltpu.SemaphoreType.DMA((len(whole.orders),))],
        )

    source_count = sources.shape[0]
    keys = with_weights(
        project_kernel,
        (sources,),
        key_value,
        (share((source_count, 2 * width)),),
        4 * source_count * width * width,
    )[0]
    while query_cols.order:
        exchange(count, query_cols)
    query_slice = query_cols.x.reshape(width, cols_here)
    query_mine = (dot(latent_item, query_slice) * scaling).astype(BF)
    sends = [reordered(query_mine, m) for m in range(1, seq_count)]
    *sends, keys = lax.optimization_barrier((*sends, keys))
    pieces = [query_mine] + [trade(x, m + 1, count) for m, x in enumerate(sends)]
    queries = seq_blocks(jnp.stack(pieces), 1)
    down_pair = down_job.x.reshape(-1, width)
    if regular:
        for job in second:
            job.last(count, keys)
        out_full = Stacks([job.x for job in second], out_orders)

    seen = jnp.clip((frames - seq_index * frames_here) * PATCH, 0, media_rows).astype(jnp.int32)
    all_rows = queries.shape[0]
    pair_flops = 2 * H // 2 * 2 * all_rows * 256 * sources.shape[0]
    mixed = call(
        lambda *refs: attend_kernel(media_rows, *refs),
        (seen, queries, keys),
        (share((all_rows, width + 128)),),
        2 * pair_flops,
        specs={0: SCALAR},
    )[0]

    def own_parts(x):
        blocks = x.reshape(seq_count, latent_rows, x.shape[1])
        return [blocks[0]] + [trade(blocks[m], m, count) for m in range(1, seq_count)]


    rows_wide = jax.ShapeDtypeStruct((latent_rows, width), F32)
    rows_low = jax.ShapeDtypeStruct((latent_rows, width), BF)
    mixture_wide, mixture, log_total, hidden, ffn_in = with_weights(
        lambda *refs: combine_kernel(seq_count, *refs),
        (*own_parts(mixed), latents[0], ffn_gain[None], ffn_bias[None]),
        out_full,
        (
            rows_wide,
            rows_low,
            jax.ShapeDtypeStruct((latent_rows, 128), F32),
            rows_wide,
            rows_low,
        ),
        2 * latent_rows * width * width,
    )
    mixture_all = lax.all_gather(mixture, AXES, axis=0, tiled=True)

    ffn_rows = GatherRel(ffn_in[None], ffn_order)
    while len(ffn_rows.order) > 1:
        exchange(count, ffn_rows)
    mine = ffn_rows.x
    other = trade(mine, ffn_order[-1], count)
    some = mine.shape[0]
    all_ffn = 2 * some * latent_rows
    units_low = share((all_ffn, 2 * units))
    halves = (jax.ShapeDtypeStruct(mine.shape, F32), share(mine.shape))
    ffn_flops = 2 * all_ffn * 2 * units * width
    keep, send, active, pre, ffn_all, grad_all = call(
        lambda *refs: ffn_kernel(ffn_order, *refs),
        (me[None], mine, other, up_pair, down_pair, rows_all),
        (*halves, units_low, units_low, *(share((all_ffn, width)),) * 2),
        3 * ffn_flops,
        specs={0: SCALAR, 5: FAR},
        scratch=(pltpu.SemaphoreType.DMA(()),),
    )
    back = Halves([keep], [send], [ffn_order])
    back.step(count)
    back.split()
    back.step(count)
    down_keep, down_send, up_sums, keep, send = call(
        ffn_sums_kernel,
        (ffn_all, after(grad_all, back.token), active, pre, down_pair),
        (
            jax.ShapeDtypeStruct((units, width), F32),
            share((units, width)),
            share((width, 2 * units)),
            *halves,
        ),
        3 * ffn_flops,
    )
    result = Halves([keep], [send], [ffn_order])
    back.split()
    back.step(count, (down_send,))
    while back.orders[0]:
        back.split()
        back.step(count)

    hidden_grad, attended_low, packed, ffn_sums = with_weights(
        hidden_back_kernel,
        (
            back.keep[0],
            back.others[0],
            hidden,
            grad_out[0],
            mixture_wide,
            log_total,
            ffn_gain[None],
        ),
        out_full,
        (
            rows_wide,
            rows_low,
            share((latent_rows, width + 128)),
            jax.ShapeDtypeStruct((8, width), F32),
        ),
        2 * latent_rows * width * width,
    )
    down_other = trade(after(down_send, packed), fold, count)
    up_blocks = after(up_sums, packed).reshape(count, -1, 2 * units)
    up_blocks = lax.all_to_all(up_blocks, AXES, split_axis=0, concat_axis=0, tiled=True)
    pieces = [packed] + [trade(packed, m, count) for m in range(1, seq_count)]
    query_part, row_grad = call(
        lambda *refs: attend_back_kernel(media_rows, seq_count, *refs),
        (seen, queries, keys, *pieces),
        (share((all_rows, width)), share(keys.shape)),
        5 * pair_flops,
        specs={0: SCALAR},
    )
    sends = [reordered(columns_of(query_part, m), m) for m in range(seq_count)]
    row_send, mixture_all, *sends = lax.optimization_barrier((row_grad, mixture_all, *sends))
    row_other = trade(row_send, 1, count)
    pieces = [sends[0]] + [trade(sends[m], m, count) for m in range(1, seq_count)]
    row_other, *pieces = lax.optimization_barrier((row_other, *pieces))
    query_cols_grad = sum(x.astype(F32) for x in pieces).astype(BF)
    query_side = dot(query_cols_grad, query_slice, ((1,), (1,))).astype(BF)
    query_side = own_parts(jnp.concatenate([query_side, query_cols_grad], axis=1))
    query_rows = seq_blocks(jnp.stack([x[:, width:] for x in query_side]), 1)
    rows = lax.all_gather(
        jnp.concatenate([attended_low, query_rows], axis=1), AXES, axis=0, tiled=True
    )

    cols = 2 * width // parts
    result.step(count, (query_side[1],))
    if regular:
        place = share((count // 4, block, cols))
        outs = call(
            lambda *refs: sums_kernel([order[:-1] for order in orders], *refs),
            (me[None], half_mine, half_other, row_grad, row_other),
            (place,) * (2 * parts),
            4 * width * width * source_count,
            specs={0: SCALAR, 1: FAR, 2: FAR, 3: FAR, 4: FAR},
            scratch=(
                pltpu.VMEM((2 * source_count, width // 2), BF),
                pltpu.VMEM((2 * source_count, 2 * width), BF),
                pltpu.VMEM((8, block, cols), BF),
                pltpu.SemaphoreType.DMA((1 + parts,)),
            ),
        )
        weights = Halves(outs[::2], outs[1::2], [order[:-1] for order in orders])
        weights.step(count, query_side[1:])
        started = weights.token
    else:
        full = dot(sources, row_grad, ((0,), (0,))).astype(BF)
        full = lax.psum_scatter(full, AXES, scatter_dimension=0, tiled=True).astype(F32)
        started = query_rows
    result.split()
    result.step(count, (started,))

    media_grad, latent_source, media_sums = with_weights(
        source_kernel,
        (after(row_grad, started), media[0], time_rows, media_gain[None]),
        key_value,
        (
            share((media_rows, width)),
            jax.ShapeDtypeStruct((latent_rows, width), F32),
            jax.ShapeDtypeStruct((8, width), F32),
        ),
        4 * source_count * width * width,
        scratch=[pltpu.VMEM((source_count, width), F32)],
    )
    latents_grad, latent_sums = call(
        lambda *refs: latent_kernel(seq_count, scaling, *refs),
        (*query_side, latent_source, latents[0], latent_gain[None], hidden_grad),
        (rows_low, jax.ShapeDtypeStruct((8, width), F32)),
        2 * latent_rows * width * width,
    )
    time_local = lax.dynamic_update_slice_in_dim(
        jnp.zeros((FRAMES, width), F32),
        media_sums[2 : 2 + frames_here],
        seq_index * frames_here,
        0,
    )
    sums = Sum(
        jnp.concatenate(
            [
                time_local,
                media_sums[:2],
                latent_sums[:2],
                ffn_sums[:2],
                jnp.zeros((2, width), F32),
            ],
            axis=0,
        ),
        [near, fold] + head + seq_bits,
    )
    if regular:
        while weights.orders[0]:
            weights.split()
            weights.step(count)
            if result.orders[0]:
                result.split()
                result.step(count, (weights.token,))
            if sums.order:
                exchange(count, sums, wait=(weights.token,))
        full = jnp.concatenate([x[0] for x in weights.total()], axis=1)
    while result.orders[0]:
        result.split()
        result.step(count)
    down_grad = down_keep + down_other.astype(F32)
    up_blocks = up_blocks.reshape(-1, 2, fold, width // count, 2 * units).astype(F32)
    swapped = jnp.concatenate([up_blocks[:, 1:], up_blocks[:, :1]], axis=1)
    up_grad = up_blocks[..., :units] + swapped[..., units:]
    up_grad = up_grad.reshape(count, -1, units).transpose(1, 0, 2).reshape(-1, count * units)
    while sums.order:
        exchange(count, sums)
    sums = sums.x
    latents_out = hidden + result.total()[0][0]

    def my_columns(x):
        return lax.dynamic_slice_in_dim(x, me * block, block, 1)

    out_grad = dot(my_columns(mixture_all), rows[:, :width], ((0,), (0,)))
    latent_all = my_columns(rows_all.reshape(-1, 2 * width))
    query_grad = dot(latent_all, rows[:, width : 2 * width], ((0,), (0,))) * scaling
    return (
        latents_out.astype(BF)[None],
        latents_grad[None],
        media_grad[None],
        sums[:FRAMES],
        sums[FRAMES],
        sums[FRAMES + 1],
        sums[FRAMES + 2],
        sums[FRAMES + 3],
        sums[FRAMES + 4],
        sums[FRAMES + 5],
        query_grad,
        full[:, :width],
        full[:, width:],
        out_grad,
        up_grad,
        down_grad,
    )


def solution(mesh):
    rows, split = P("items", "seq", None), P(AXES, None)
    return jax.shard_map(
        shards,
        mesh=mesh,
        in_specs=(rows, rows, P("items")) + (P(),) * 7 + (split,) * 6 + (rows,),
        out_specs=(rows,) * 3 + (P(),) * 7 + (split,) * 6,
        check_vma=False,
    )
```

```python
import jax
import jax.numpy as jnp
from jax import lax
from jax.experimental import pallas as pl
from jax.experimental.pallas import tpu as pltpu
from jax.sharding import PartitionSpec as P

H = 16
FRAMES = 8
PATCH = 256
AXES = ("items", "seq")
BF = jnp.bfloat16
F32 = jnp.float32


def layer_norm(values, gain, bias):
    center = jnp.mean(values, axis=-1, keepdims=True)
    spread = jnp.mean(jnp.square(values - center), axis=-1, keepdims=True)
    rstd = lax.rsqrt(spread + 1e-05)
    unit = (values - center) * rstd
    return unit * gain + bias, unit, rstd


def layer_norm_back(grad, unit, rstd, gain):
    scaled = grad * gain
    inner = scaled - jnp.mean(scaled, axis=-1, keepdims=True)
    inner = inner - unit * jnp.mean(scaled * unit, axis=-1, keepdims=True)
    return inner * rstd, jnp.sum(grad * unit, axis=0), jnp.sum(grad, axis=0)


def dot(a, b, dims=((1,), (0,))):
    return lax.dot_general(a, b, (dims, ((), ())), preferred_element_type=F32)


def trade(x, mask, count):
    return lax.ppermute(x, AXES, [(i, i ^ mask) for i in range(count)])


def after(x, *others):
    return lax.optimization_barrier((x,) + others)[0]


class Gather:
    def __init__(self, x, order, me):
        self.x, self.order, self.me, self.done = x, list(order), me, []

    def rows(self):
        if isinstance(self.x, (list, tuple)):
            mine, other = self.x
            axis = sum(m > self.done[-1] for m in self.done)
            mine, other = jnp.expand_dims(mine, axis), jnp.expand_dims(other, axis)
            self.x = jnp.where(
                (self.me & self.done[-1]) != 0,
                jnp.concatenate([other, mine], axis),
                jnp.concatenate([mine, other], axis),
            )
        return self.x

    def send(self):
        return self.rows(), self.order[0]

    def take(self, sent, other):
        self.done.append(self.order.pop(0))
        self.x = (sent, other)


class GatherRel:
    def __init__(self, x, order):
        self.order, self.x = list(order), x

    def send(self):
        return self.x, self.order[0]

    def take(self, sent, other):
        self.order.pop(0)
        self.x = jnp.concatenate([sent, other], axis=0)


class GatherApart(GatherRel):
    def take(self, sent, other):
        if len(self.order) > 2:
            GatherRel.take(self, sent, other)
        else:
            self.order.pop(0)
            self.x = (sent, other)

    def last(self, count, join=False):
        mask = self.order.pop(0)
        pieces = (jnp.concatenate(self.x, axis=0),) if join else tuple(self.x)
        self.x = [*pieces, *[trade(x, mask, count) for x in pieces]]


class Halves:
    def __init__(self, keep, send, orders):
        self.orders, self.keep, self.sends = [list(order) for order in orders], keep, send

    def step(self, count, wait=()):
        sent = lax.optimization_barrier(tuple(self.sends) + tuple(wait))
        masks = [order.pop() for order in self.orders]
        self.others = [trade(x, mask, count) for x, mask in zip(sent, masks)]
        self.token = sent[0]

    def split(self):
        self.keep, self.sends = add_split(self.keep, self.others)

    def total(self):
        return [k.astype(F32) + o.astype(F32) for k, o in zip(self.keep, self.others)]


def add_split_kernel(pairs, *refs):
    ins, outs = refs[: 4 * pairs], refs[4 * pairs :]
    for k in range(pairs):
        keep, keep2, other, other2 = ins[4 * k : 4 * k + 4]
        out, send = outs[2 * k : 2 * k + 2]
        out[...] = (keep[...].astype(F32) + other[...].astype(F32)).reshape(out.shape)
        send[...] = (keep2[...].astype(F32) + other2[...].astype(F32)).astype(BF).reshape(send.shape)


def add_split(keeps, others):
    half = keeps[0].shape[0] // 2
    some = min(half, 2)
    ins, specs, outs, out_specs = [], [], [], []
    for keep, other in zip(keeps, others):
        tail = keep.shape[1:]
        low = pl.BlockSpec((some,) + tail, lambda i: (i, 0, 0))
        high = pl.BlockSpec((some,) + tail, lambda i: (i + half // some, 0, 0))
        ins += [keep, keep, other, other]
        specs += [low, high, low, high]
        outs += [jax.ShapeDtypeStruct((half,) + tail, F32), jax.ShapeDtypeStruct((half,) + tail, BF)]
        out_specs += [low, low]
    out = pl.pallas_call(
        lambda *refs: add_split_kernel(len(ins) // 4, *refs),
        grid=(half // some,),
        out_shape=tuple(outs),
        in_specs=specs,
        out_specs=tuple(out_specs),
        compiler_params=pltpu.CompilerParams(vmem_limit_bytes=56 << 20),
        cost_estimate=pl.CostEstimate(
            flops=1, bytes_accessed=1, transcendentals=0
        ),
    )(*ins)
    return list(out[::2]), list(out[1::2])


class Sum:
    def __init__(self, x, order):
        self.order, self.x = list(order), x

    def send(self):
        return self.x, self.order[0]

    def take(self, sent, other):
        self.order.pop(0)
        self.x = self.x + other


def exchange(count, *jobs, wait=()):
    sends = [job.send() for job in jobs]
    sent = lax.optimization_barrier(tuple(x for x, unused in sends) + tuple(wait))
    for job, x, (unused, mask) in zip(jobs, sent, sends):
        job.take(x, trade(x, mask, count))
    return sent[0]


def sync(jobs, *arrays):
    held = [job.x for job in jobs]
    held, arrays = lax.optimization_barrier((held, arrays))
    for job, x in zip(jobs, held):
        job.x = x
    return arrays


def share_seq(x, seq_count, count):
    return jnp.concatenate([x] + [trade(x, m, count) for m in range(1, seq_count)], axis=0)


def windows(width):
    size = width // H
    for pair in range(H // 2):
        base = (pair // 2) * 4 * size + (pair % 2) * 128
        yield pair, base, (2 * pair * size - base, (2 * pair + 1) * size - base, (2 * pair + 2) * size - base)


def stacked(rows, edges):
    column = lax.broadcasted_iota(jnp.int32, rows.shape, 1)
    first = (column >= edges[0]) & (column < edges[1])
    second = (column >= edges[1]) & (column < edges[2])
    zero = jnp.zeros_like(rows)
    return jnp.concatenate([jnp.where(first, rows, zero), jnp.where(second, rows, zero)], axis=0)


def unstacked(both, edges):
    count = both.shape[0] // 2
    column = lax.broadcasted_iota(jnp.int32, (count, both.shape[1]), 1)
    first = (column >= edges[0]) & (column < edges[1])
    second = (column >= edges[1]) & (column < edges[2])
    return jnp.where(first, both[:count], jnp.where(second, both[count:], 0.0))


def masked_scores(seen, queries, keys, media_rows):
    scores = dot(queries, keys, ((1,), (1,)))
    place = lax.broadcasted_iota(jnp.int32, scores.shape, 1)
    return jnp.where((place < seen) | (place >= media_rows), scores, -1e30)


def attend_kernel(media_rows, seen_ref, q_ref, kv_ref, out_ref):
    count, width = q_ref.shape
    seen = seen_ref[0]
    lane = lax.broadcasted_iota(jnp.int32, (count, 128), 1)
    stats = jnp.zeros((count, 128), F32)
    carry = None
    for pair, base, edges in windows(width):
        cols, value_cols = slice(base, base + 256), slice(width + base, width + base + 256)
        scores = masked_scores(seen, stacked(q_ref[:, cols], edges), kv_ref[:, cols], media_rows)
        top = jnp.max(scores, axis=1, keepdims=True)
        probs = jnp.exp(scores - top)
        total = jnp.sum(probs, axis=1, keepdims=True)
        mixed = unstacked(dot(probs.astype(BF), kv_ref[:, value_cols]) / total, edges)
        if pair % 2 == 0:
            out_ref[:, base : base + 128] = mixed[:, :128].astype(BF)
            carry = mixed[:, 128:]
        else:
            out_ref[:, base : base + 128] = (carry + mixed[:, :128]).astype(BF)
            out_ref[:, base + 128 : base + 256] = mixed[:, 128:].astype(BF)
        for k in range(2):
            rows = slice(k * count, (k + 1) * count)
            for n, value in enumerate((top, total)):
                value = value[rows]
                for term in range(3):
                    low = value.astype(BF).astype(F32)
                    stats = jnp.where(lane == (3 * n + term) * H + 2 * pair + k, low, stats)
                    value = value - low
    out_ref[:, width:] = stats.astype(BF)


def attend_back_kernel(media_rows, pieces, seen_ref, q_ref, kv_ref, *refs):
    dq_ref, dkv_ref = refs[pieces:]
    count, width = q_ref.shape
    seen = seen_ref[0]
    lane = lax.broadcasted_iota(jnp.int32, (count, 128), 1)
    packed = jnp.concatenate([ref[...] for ref in refs[:pieces]], axis=0)
    stats = packed[:, width:].astype(F32)

    def column(at):
        parts = []
        for k in range(2):
            here = (lane == at + k) | (lane == at + H + k) | (lane == at + 2 * H + k)
            parts.append(jnp.sum(jnp.where(here, stats, 0.0), axis=1, keepdims=True))
        return jnp.concatenate(parts, axis=0)

    carry = None
    for pair, base, edges in windows(width):
        cols = slice(base, base + 256)
        queries, grads = stacked(q_ref[:, cols], edges), stacked(packed[:, cols], edges)
        keys, values = kv_ref[:, cols], kv_ref[:, width + base : width + base + 256]
        scores = masked_scores(seen, queries, keys, media_rows)
        probs = jnp.exp(scores - column(2 * pair))
        prob_grad = dot(grads, values, ((1,), (1,)))
        score_grad = (probs * (prob_grad - column(3 * H + 2 * pair))).astype(BF)
        new = (
            (dq_ref, 0, dot(score_grad, keys)),
            (dkv_ref, 0, dot(score_grad, queries, ((0,), (0,)))),
            (dkv_ref, width, dot(probs.astype(BF), grads, ((0,), (0,)))),
        )
        new = [(ref, at + base, unstacked(x, edges) if ref is dq_ref else x) for ref, at, x in new]
        if pair % 2 == 0:
            for ref, at, x in new:
                ref[:, at : at + 128] = x[:, :128].astype(BF)
            carry = [x[:, 128:] for unused_ref, unused_at, x in new]
        else:
            for (ref, at, x), old in zip(new, carry):
                ref[:, at : at + 128] = (old + x[:, :128]).astype(BF)
                ref[:, at + 128 : at + 256] = x[:, 128:].astype(BF)


def lane_heads(shape, width, dim):
    lane = lax.broadcasted_iota(jnp.int32, shape, dim)
    column = lax.broadcasted_iota(jnp.int32, shape, 1 - dim)
    size = width // H
    first = (lane % H) * size
    return lane // H, column - first, (column >= first) & (column < first + size)


def three_terms(x):
    terms = []
    for unused in range(3):
        terms.append(x.astype(BF))
        x = x - terms[-1].astype(F32)
    return terms


def combine_kernel(pieces, whole, me_ref, *refs):
    parts, refs = refs[:pieces], refs[pieces:]
    latent_ref, gain_ref, bias_ref, *refs = refs
    *refs, wide_ref, low_ref, stat_ref, hidden_ref, ffn_ref, w_ref, sems = refs
    waits = whole.fetch(me_ref[0], refs, w_ref, sems)
    rows, width = latent_ref.shape
    group, unused, inside = lane_heads((128, width), width, 0)
    spread_top = jnp.where(inside & (group < 3), 1.0, 0.0).astype(BF)
    spread_total = jnp.where(inside & (group >= 3) & (group < 6), 1.0, 0.0).astype(BF)
    tops = [dot(ref[:, width:], spread_top) for ref in parts]
    top = tops[0]
    for other in tops[1:]:
        top = jnp.maximum(top, other)
    total = jnp.zeros((rows, width), F32)
    mixed = jnp.zeros((rows, width), F32)
    for ref, mine in zip(parts, tops):
        weight = jnp.exp(mine - top) * dot(ref[:, width:], spread_total)
        total += weight
        mixed += weight * ref[:, :width].astype(F32)
    mixed = mixed / total
    wide_ref[...] = mixed
    low = mixed.astype(BF)
    low_ref[...] = low
    group, offset, unused = lane_heads((width, 128), width, 1)
    stats = jnp.zeros((rows, 128), F32)
    for k, term in enumerate(three_terms(top + jnp.log(total))):
        pick = jnp.where((group == k) & (offset == 0), 1.0, 0.0).astype(BF)
        stats += dot(term, pick)
    stat_ref[...] = stats
    for wait in waits:
        wait.wait()
    hidden = latent_ref[...].astype(F32) + dot(low, w_ref[...])
    hidden_ref[...] = hidden
    ffn_ref[...] = layer_norm(hidden, gain_ref[...], bias_ref[...])[0].astype(BF)


def hidden_back_kernel(whole, me_ref, *refs):
    keep_ref, other_ref, hidden_ref, upstream_ref, wide_ref, stat_ref, gain_ref, *refs = refs
    *refs, hidden_grad_ref, low_ref, packed_ref, sums_ref, w_ref, sems = refs
    waits = whole.fetch(me_ref[0], refs, w_ref, sems)
    rows, width = hidden_ref.shape
    grad = keep_ref[0].astype(F32) + other_ref[0].astype(F32)
    gain = gain_ref[...]
    unused, unit, rstd = layer_norm(hidden_ref[...], gain, gain)
    norm_grad, gain_grad, bias_grad = layer_norm_back(grad, unit, rstd, gain)
    row = lax.broadcasted_iota(jnp.int32, (8, width), 0)
    sums_ref[...] = jnp.where(row == 0, gain_grad[None], jnp.where(row == 1, bias_grad[None], 0.0))
    hidden_grad = upstream_ref[...].astype(F32) + norm_grad
    hidden_grad_ref[...] = hidden_grad
    low = hidden_grad.astype(BF)
    low_ref[...] = low
    for wait in waits:
        wait.wait()
    mixture_grad = dot(low, w_ref[...], ((1,), (1,))).astype(BF)
    packed_ref[:, :width] = mixture_grad
    group, unused, inside = lane_heads((width, 128), width, 1)
    heads = jnp.where(inside & (group >= 3) & (group < 6), 1.0, 0.0).astype(BF)
    inner = jnp.zeros((rows, 128), F32)
    for term in three_terms(wide_ref[...] * mixture_grad.astype(F32)):
        inner += dot(term, heads)
    lane = lax.broadcasted_iota(jnp.int32, (rows, 128), 1) // H
    stats = stat_ref[...]
    for k, term in enumerate(three_terms(inner)):
        stats = jnp.where(lane == 3 + k, term.astype(F32), stats)
    packed_ref[:, width:] = stats.astype(BF)


def owner_of(place, order):
    return sum(mask for k, mask in enumerate(order) if (place >> k) % 2)


def place_of(owner, order):
    return sum(((owner // mask) % 2) << k for k, mask in enumerate(order))


class Stacks:
    def __init__(self, parts, orders):
        self.each = len(parts[0])
        self.arrays = [x for pieces in parts for x in pieces]
        self.orders = orders
        self.cols = sum(pieces[0].shape[2] for pieces in parts)
        widths = [pieces[0].shape[2] for pieces in parts]
        self.ends = [sum(widths[: k + 1]) for k in range(len(parts))]

    def fetch(self, me, refs, into, sems):
        at, waits = 0, []
        for k, order in enumerate(self.orders):
            pieces = refs[self.each * k : self.each * (k + 1)]
            some, block, cols = pieces[0].shape
            for place in range(self.each * some):
                owner = me ^ owner_of(place, order)
                to = into.at[pl.ds(pl.multiple_of(owner * block, 16), block), at : at + cols]
                source = pieces[place // some].at[place % some]
                pltpu.make_async_copy(source, to, sems.at[k]).start()
            part = into.at[:, at : at + cols]
            waits.append(pltpu.make_async_copy(part, part, sems.at[k]))
            at += cols
        return waits


class Plain:
    def __init__(self, x):
        self.arrays, self.orders = [x], (None,)
        self.cols = x.shape[1]
        self.ends = [self.cols]

    def fetch(self, me, refs, into, sems):
        copy = pltpu.make_async_copy(refs[0], into, sems.at[0])
        copy.start()
        return [copy]


def halves_kernel(me_ref, s_ref, mine_ref, other_ref):
    block = 48
    for parity in range(2):

        @pl.when(me_ref[0] % 2 == parity)
        def _():
            for out_ref, which in ((mine_ref, parity), (other_ref, 1 - parity)):
                for n in range(out_ref.shape[1] // block):
                    at = (2 * n + which) * block
                    out_ref[:, n * block : (n + 1) * block] = s_ref[:, at : at + block]


def order_kernel(whole, me_ref, *refs):
    *refs, out_ref, sems = refs
    for wait in whole.fetch(me_ref[0], refs, out_ref, sems):
        wait.wait()


def project_kernel(whole, me_ref, s_ref, *refs):
    *refs, out_ref, w_ref, sems = refs
    at = 0
    for wait, end in zip(whole.fetch(me_ref[0], refs, w_ref, sems), whole.ends):
        wait.wait()
        out_ref[:, at:end] = dot(s_ref[...], w_ref[:, at:end]).astype(BF)
        at = end


def gelu_parts(x):
    c = 0.7978845608028654
    t = jnp.tanh(c * (x + 0.044715 * (x * x * x)))
    slope = 0.5 * (1.0 + t) + 0.5 * x * (1.0 - t * t) * (c * (1.0 + 3 * 0.044715 * (x * x)))
    return 0.5 * x * (1.0 + t), slope


def ffn_kernel(
    order,
    me_ref,
    mine_ref,
    other_ref,
    up_ref,
    down_ref,
    all_ref,
    keep_ref,
    send_ref,
    active_ref,
    pre_ref,
    rows_ref,
    grad_rows_ref,
    sem,
):
    some, each, width = mine_ref.shape
    for place in range(2 * some):
        owner = me_ref[0] ^ owner_of(place, order)
        pltpu.make_async_copy(
            all_ref.at[owner, :, width : 2 * width],
            grad_rows_ref.at[place * each : (place + 1) * each],
            sem,
        ).start()
    rows_ref[: some * each, :] = mine_ref[...].reshape(some * each, width)
    rows_ref[some * each :, :] = other_ref[...].reshape(some * each, width)
    active, slope = gelu_parts(dot(rows_ref[...], up_ref[...]))
    active_ref[...] = active.astype(BF)
    pltpu.make_async_copy(grad_rows_ref, grad_rows_ref, sem).wait()
    pre_grad = (dot(grad_rows_ref[...], down_ref[...], ((1,), (1,))) * slope).astype(BF)
    pre_ref[...] = pre_grad
    total = dot(pre_grad, up_ref[...], ((1,), (1,)))
    keep_ref[...] = total[: some * each].reshape(keep_ref.shape)
    send_ref[...] = total[some * each :].astype(BF).reshape(send_ref.shape)


def ffn_sums_kernel(
    rows_ref,
    grad_rows_ref,
    active_ref,
    pre_ref,
    down_ref,
    down_keep_ref,
    down_send_ref,
    up_keep_ref,
    up_send_ref,
    keep_ref,
    send_ref,
):
    first = ((0,), (0,))
    units = down_keep_ref.shape[0]
    down = dot(active_ref[...], grad_rows_ref[...], first)
    down_keep_ref[...] = down[:units]
    down_send_ref[...] = down[units:].astype(BF)
    up = dot(rows_ref[...], pre_ref[...], first)
    up_keep_ref[...] = up[:, :units].astype(BF)
    up_send_ref[...] = up[:, units:].astype(BF)
    out = dot(active_ref[...], down_ref[...])
    half = out.shape[0] // 2
    keep_ref[...] = out[:half].reshape(keep_ref.shape)
    send_ref[...] = out[half:].astype(BF).reshape(send_ref.shape)


def source_kernel(whole, me_ref, g_ref, media_ref, time_ref, gain_ref, *refs):
    *refs, media_grad_ref, latent_ref, sums_ref, acc_ref, w_ref, sems = refs
    at = 0
    for wait, end in zip(whole.fetch(me_ref[0], refs, w_ref, sems), whole.ends):
        wait.wait()
        new = dot(g_ref[:, at:end], w_ref[:, at:end], ((1,), (1,)))
        acc_ref[...] = acc_ref[...] + new if at else new
        at = end
    media_rows, width = media_ref.shape
    gain = gain_ref[...]
    rows = [jnp.zeros((1, width), F32), jnp.zeros((1, width), F32)]
    for frame in range(media_rows // PATCH):
        here = slice(frame * PATCH, (frame + 1) * PATCH)
        shifted = media_ref[here, :].astype(F32) + time_ref[frame : frame + 1, :]
        unused, unit, rstd = layer_norm(shifted, gain, gain)
        grad = acc_ref[here, :]
        shifted_grad, gain_grad, bias_grad = layer_norm_back(grad, unit, rstd, gain)
        media_grad_ref[here, :] = shifted_grad.astype(BF)
        rows[0] += gain_grad[None]
        rows[1] += bias_grad[None]
        rows.append(jnp.sum(shifted_grad, axis=0, keepdims=True))
    at = lax.broadcasted_iota(jnp.int32, sums_ref.shape, 0)
    sums = jnp.zeros(sums_ref.shape, F32)
    for k, row in enumerate(rows):
        sums = jnp.where(at == k, row, sums)
    sums_ref[...] = sums
    latent_ref[...] = acc_ref[media_rows:, :]


def latent_kernel(pieces, scaling, *refs):
    parts, refs = refs[:pieces], refs[pieces:]
    source_ref, latent_ref, gain_ref, hidden_grad_ref, out_ref, sums_ref = refs
    gain = gain_ref[...]
    width = gain.shape[1]
    query_side = sum(ref[:, :width].astype(F32) for ref in parts)
    grad = source_ref[...] + query_side * scaling
    unused, unit, rstd = layer_norm(latent_ref[...].astype(F32), gain, gain)
    latent_grad, gain_grad, bias_grad = layer_norm_back(grad, unit, rstd, gain)
    out_ref[...] = (hidden_grad_ref[...] + latent_grad).astype(BF)
    at = lax.broadcasted_iota(jnp.int32, sums_ref.shape, 0)
    sums_ref[...] = jnp.where(
        at == 0, gain_grad[None], jnp.where(at == 1, bias_grad[None], 0.0)
    )


def sums_kernel(orders, me_ref, s_ref, s2_ref, g_ref, g2_ref, *refs):
    *out_refs, s_held, g_held, held, sems = refs
    me = me_ref[0] - me_ref[0] % 2
    half, block, unused = out_refs[0].shape
    widths = [ref.shape[2] for ref in out_refs[::2]]
    starts = [sum(widths[:k]) for k in range(len(widths))]
    rows = s_ref.shape[0]
    for k, ref in enumerate((s_ref, s2_ref)):
        pltpu.make_async_copy(ref, s_held.at[k * rows : (k + 1) * rows], sems.at[0]).start()
    for part in range(len(orders)):
        columns = slice(starts[part], starts[part] + widths[part])
        for k, ref in enumerate((g_ref, g2_ref)):
            to = g_held.at[k * rows : (k + 1) * rows, columns]
            pltpu.make_async_copy(ref.at[:, columns], to, sems.at[1 + part]).start()
    pltpu.make_async_copy(s_held, s_held, sems.at[0]).wait()
    some = held.shape[0]
    for part, order in enumerate(orders):
        columns = slice(starts[part], starts[part] + widths[part])
        here = g_held.at[:, columns]
        pltpu.make_async_copy(here, here, sems.at[1 + part]).wait()
        first = (me // order[-1]) % 2
        for start in range(0, 2 * half, some):
            full = dot(s_held[:, start * block : (start + some) * block], here[...], ((0,), (0,)))
            cols = widths[part]
            held[:, :, :cols] = full.astype(BF).reshape(some, block, cols)
            for bit in range(2):

                @pl.when(first == bit)
                def _(bit=bit, start=start, part=part, order=order, cols=cols):
                    for n in range(some):
                        owner = 2 * (start + n)
                        place = place_of(owner ^ me, order) % half
                        send = (owner // order[-1]) % 2 != bit
                        out_refs[2 * part + send][place] = held[n, :, :cols]


SCALAR = pl.BlockSpec(memory_space=pltpu.SMEM)
FAR = pl.BlockSpec(memory_space=pl.ANY)


def call(kernel, inputs, outputs, flops, specs=(), far_outputs=False, scratch=()):
    specs = dict(specs)

    def whole(x):
        return pl.BlockSpec(x.shape, lambda i, nd=len(x.shape): (0,) * nd)

    nbytes = sum(x.size * x.dtype.itemsize for x in inputs)
    nbytes += sum(x.size * x.dtype.itemsize for x in outputs)
    return pl.pallas_call(
        kernel,
        grid=(1,),
        out_shape=tuple(outputs),
        in_specs=[specs.get(n, whole(x)) for n, x in enumerate(inputs)],
        out_specs=tuple(FAR if far_outputs else whole(x) for x in outputs),
        scratch_shapes=list(scratch),
        compiler_params=pltpu.CompilerParams(vmem_limit_bytes=56 << 20),
        cost_estimate=pl.CostEstimate(flops=flops // 1000, bytes_accessed=nbytes // 1000, transcendentals=0),
    )(*inputs)


def shards(
    media,
    latents,
    frames,
    time_embed,
    media_gain,
    media_bias,
    latent_gain,
    latent_bias,
    ffn_gain,
    ffn_bias,
    w_query,
    w_key,
    w_value,
    w_out,
    w_up,
    w_down,
    grad_out,
):
    item_count, seq_count = lax.axis_size("items"), lax.axis_size("seq")
    count = item_count * seq_count
    seq_index = lax.axis_index("seq")
    me = lax.axis_index("items") * seq_count + seq_index
    unused_items, media_rows, width = media.shape
    latent_rows = latents.shape[1]
    head_size = width // H
    frames_here = media_rows // PATCH
    scaling = head_size ** (-0.5)

    bits = [1 << k for k in reversed(range(30))]
    item_bits = [m for m in bits if seq_count <= m < count]
    seq_bits = [m for m in bits if m < seq_count]
    head, (fold, near), side, tail = item_bits[:-2], item_bits[-2:], seq_bits[0], seq_bits[1:]
    orders = (
        head + [fold, near, side] + tail,
        head + [side, fold, near] + tail,
        head + [near, side, fold] + tail,
    )
    ffn_order = item_bits + seq_bits[:-1]
    core = seq_bits[-1]
    block = width // count
    regular = block % 16 == 0

    def share(x):
        return jax.ShapeDtypeStruct(x, BF)

    latent_in = latents[0].astype(F32)
    latent_normed, latent_unit, latent_rstd = layer_norm(latent_in, latent_gain, latent_bias)
    latent_normed = latent_normed.astype(BF)
    time_rows = lax.dynamic_slice_in_dim(time_embed, seq_index * frames_here, frames_here, 0)
    shifted = (
        media[0].astype(F32).reshape(frames_here, PATCH, width) + time_rows[:, None, :]
    ).reshape(media_rows, width)
    media_normed, media_unit, media_rstd = layer_norm(shifted, media_gain, media_bias)
    sources = jnp.concatenate([media_normed.astype(BF), latent_normed], axis=0)

    def in_columns(x):
        return x.reshape(x.shape[0], count, -1).transpose(1, 0, 2)

    def spread(x):
        x = lax.all_to_all(x, AXES, split_axis=0, concat_axis=0, tiled=True)
        return x.reshape(-1, x.shape[2])

    cols_here = width // seq_count

    def seq_blocks(x, axis):
        return jnp.concatenate(
            [
                lax.dynamic_index_in_dim(x, seq_index ^ t, 0, keepdims=False)
                for t in range(seq_count)
            ],
            axis=axis,
        )

    def columns_of(x, m):
        return lax.dynamic_slice_in_dim(x, (seq_index ^ m) * cols_here, cols_here, 1)

    def reordered(x, m):
        blocks = x.reshape(seq_count, latent_rows, x.shape[1])
        return jnp.concatenate([blocks[t ^ m] for t in range(seq_count)], axis=0)

    parts = len(orders)
    units = w_down.shape[0]
    out_orders = (head + [near, fold, side] + tail, head + [near, side, fold] + tail)
    shares = (width * 5 // 6, width * 5 // 6, width // 3)
    def query_pieces(x):
        pieces = [columns_of(x, m) for m in range(seq_count)]
        return [pieces[0]] + [trade(pieces[m], m, count) for m in range(1, seq_count)]

    if regular:
        first = GatherRel(jnp.concatenate([w_key, w_value], axis=1)[None], head)
        second = GatherRel(w_out[None], head + [near])

        def split(x, shares, orders, done):
            return [
                GatherApart(x[..., sum(shares[:k]) : sum(shares[: k + 1])], order[done:])
                for k, order in enumerate(orders)
            ]

        while first.order:
            exchange(count, first)
        latent_item = share_seq(latent_normed, seq_count, count)
        pieces = query_pieces(w_query)
        half_mine, half_other = call(
            halves_kernel,
            (me[None], sources),
            (share((sources.shape[0], width // 2)),) * 2,
            0,
            specs={0: SCALAR},
        )
        rows_mine = jnp.concatenate([latent_normed, grad_out[0]], axis=1)
        sources, latent_item, half_mine, half_other, rows_mine, *pieces = sync(
            [first], sources, latent_item, half_mine, half_other, rows_mine, *pieces
        )
        query_cols = Gather(seq_blocks(jnp.stack(pieces), 0), [near] + head + [fold], me)
        first = split(first.x, shares, orders, len(head))
        exchange(count, *first, second, query_cols)
        sync([*first, second, query_cols])
        exchange(count, *first, second, query_cols)
        (up_in,) = sync([*first, second, query_cols], in_columns(w_up))
        second = split(second.x, (width // 2, width // 2), out_orders, len(head) + 1)
        exchange(count, *first, query_cols)
        sources, latent_item, rows_mine, half_other = sync(
            [*first, query_cols], sources, latent_item, rows_mine, half_other
        )
        for job in first:
            job.last(count)
        rows_all = lax.all_gather(rows_mine, AXES, axis=0)
    else:
        up_mine = spread(in_columns(w_up))
        rows_all = lax.all_gather(
            jnp.concatenate([latent_normed, grad_out[0]], axis=1), AXES, axis=0
        )
        latent_item = share_seq(latent_normed, seq_count, count)
        query_cols = Gather(seq_blocks(jnp.stack(query_pieces(w_query)), 0), item_bits, me)
        while query_cols.order:
            exchange(count, query_cols)
        both = lax.all_gather(jnp.concatenate([w_key, w_value], 1), AXES, axis=0, tiled=True)
        key_value = Plain(both)
        out_full = Plain(lax.all_gather(w_out, AXES, axis=0, tiled=True))

    def with_weights(kernel, inputs, whole, outputs, flops, keep=True, scratch=()):
        inputs = [me[None]] + list(inputs)
        specs = {0: SCALAR}
        for n in range(len(whole.arrays)):
            specs[len(inputs) + n] = FAR
        scratch = list(scratch) + ([pltpu.VMEM((width, whole.cols), BF)] if keep else [])
        return call(
            lambda *refs: kernel(whole, *refs),
            (*inputs, *whole.arrays),
            outputs,
            flops,
            specs=specs,
            scratch=scratch + [pltpu.SemaphoreType.DMA((len(whole.orders),))],
        )

    query_slice = query_cols.rows().reshape(width, cols_here)
    query_mine = (dot(latent_item, query_slice) * scaling).astype(BF)
    sends = [reordered(query_mine, m) for m in range(1, seq_count)]
    if regular:
        query_mine, *sends = sync([*first, *second], query_mine, *sends)
        key_value = Stacks([job.x for job in first], orders)
        exchange(count, *second)
    pieces = [query_mine] + [trade(x, m + 1, count) for m, x in enumerate(sends)]
    source_count = sources.shape[0]
    keys = with_weights(
        project_kernel,
        (sources,),
        key_value,
        (share((source_count, 2 * width)),),
        4 * source_count * width * width,
    )[0]
    if regular:
        keys, half_other, up_in, *pieces = sync(second, keys, half_other, up_in, *pieces)
        up_mine = spread(up_in)
        half_other = trade(half_other, 1, count)
        exchange(count, *second)
    queries = seq_blocks(jnp.stack(pieces), 1)
    seen = jnp.clip((frames - seq_index * frames_here) * PATCH, 0, media_rows).astype(jnp.int32)
    all_rows = queries.shape[0]
    pair_flops = 2 * H // 2 * 2 * all_rows * 256 * sources.shape[0]
    mixed = call(
        lambda *refs: attend_kernel(media_rows, *refs),
        (seen, queries, keys),
        (share((all_rows, width + 128)),),
        2 * pair_flops,
        specs={0: SCALAR},
    )[0]

    def own_parts(x):
        blocks = x.reshape(seq_count, latent_rows, x.shape[1])
        return [blocks[0]] + [trade(blocks[m], m, count) for m in range(1, seq_count)]


    mixed_parts = own_parts(mixed)
    if regular:
        mixed_parts = sync(second, *mixed_parts)
        for job in second:
            job.last(count, join=True)
        sync(second)
        out_full = Stacks([job.x for job in second], out_orders)
    up_other, down_other = trade(up_mine, core, count), trade(w_down, core, count)
    up_pair = jnp.concatenate([up_mine, up_other], axis=1)
    down_pair = jnp.concatenate([w_down, down_other], axis=0)
    rows_wide = jax.ShapeDtypeStruct((latent_rows, width), F32)
    rows_low = jax.ShapeDtypeStruct((latent_rows, width), BF)
    mixture_wide, mixture, log_total, hidden, ffn_in = with_weights(
        lambda *refs: combine_kernel(seq_count, *refs),
        (*mixed_parts, latents[0], ffn_gain[None], ffn_bias[None]),
        out_full,
        (
            rows_wide,
            rows_low,
            jax.ShapeDtypeStruct((latent_rows, 128), F32),
            rows_wide,
            rows_low,
        ),
        2 * latent_rows * width * width,
    )
    ffn_rows = GatherRel(ffn_in[None], ffn_order)
    while len(ffn_rows.order) > 1:
        exchange(count, ffn_rows)
    mine = ffn_rows.x
    other = trade(mine, ffn_order[-1], count)
    some = mine.shape[0]
    all_ffn = 2 * some * latent_rows
    units_low = share((all_ffn, 2 * units))
    halves = (jax.ShapeDtypeStruct(mine.shape, F32), share(mine.shape))
    ffn_flops = 2 * all_ffn * 2 * units * width
    keep, send, active, pre, ffn_all, grad_all = call(
        lambda *refs: ffn_kernel(ffn_order, *refs),
        (me[None], mine, other, up_pair, down_pair, rows_all),
        (*halves, units_low, units_low, *(share((all_ffn, width)),) * 2),
        3 * ffn_flops,
        specs={0: SCALAR, 5: FAR},
        scratch=(pltpu.SemaphoreType.DMA(()),),
    )
    back = Halves([keep], [send], [ffn_order])
    back.step(count)
    down_keep, down_send, up_keep, up_send, keep, send = call(
        ffn_sums_kernel,
        (ffn_all, after(grad_all, back.token), active, pre, down_pair),
        (
            jax.ShapeDtypeStruct((units, width), F32),
            share((units, width)),
            share((width, units)),
            share((width, units)),
            *halves,
        ),
        3 * ffn_flops,
    )
    result = Halves([keep], [send], [ffn_order])
    wait = (down_send,)
    while back.orders[0]:
        back.split()
        back.step(count, wait)
        if not wait:
            result.split()
        result.step(count, (back.token,))
        wait = ()
        if back.orders[0]:
            back.others, result.others = lax.optimization_barrier((back.others, result.others))

    hidden_grad, attended_low, packed, ffn_sums = with_weights(
        hidden_back_kernel,
        (
            back.keep[0],
            back.others[0],
            hidden,
            grad_out[0],
            mixture_wide,
            log_total,
            ffn_gain[None],
        ),
        out_full,
        (
            rows_wide,
            rows_low,
            share((latent_rows, width + 128)),
            jax.ShapeDtypeStruct((8, width), F32),
        ),
        2 * latent_rows * width * width,
    )
    down_send, up_send = sync([], down_send, up_send, packed)[:2]
    down_other, up_other = trade(down_send, core, count), trade(up_send, core, count)
    pieces = [packed] + [trade(packed, m, count) for m in range(1, seq_count)]
    result.split()
    result.step(count, (packed,))
    query_part, row_grad = call(
        lambda *refs: attend_back_kernel(media_rows, seq_count, *refs),
        (seen, queries, keys, *pieces),
        (share((all_rows, width)), share(keys.shape)),
        5 * pair_flops,
        specs={0: SCALAR},
    )
    sends = [reordered(columns_of(query_part, m), m) for m in range(seq_count)]
    row_send, result.others, *sends = lax.optimization_barrier((row_grad, result.others, *sends))
    row_other = trade(row_send, 1, count)
    pieces = [sends[0]] + [trade(sends[m], m, count) for m in range(1, seq_count)]
    row_grad, row_other, *pieces = sync([], row_send, row_other, *pieces)
    query_cols_grad = sum(x.astype(F32) for x in pieces).astype(BF)
    query_side = dot(query_cols_grad, query_slice, ((1,), (1,))).astype(BF)
    query_side = own_parts(jnp.concatenate([query_side, query_cols_grad], axis=1))

    if regular:
        outs = call(
            lambda *refs: sums_kernel([order[:-1] for order in orders], *refs),
            (me[None], half_mine, half_other, row_grad, row_other),
            tuple(share((count // 4, block, cols)) for cols in shares for unused in range(2)),
            4 * width * width * source_count,
            specs={0: SCALAR, 1: FAR, 2: FAR, 3: FAR, 4: FAR},
            scratch=(
                pltpu.VMEM((2 * source_count, width // 2), BF),
                pltpu.VMEM((2 * source_count, 2 * width), BF),
                pltpu.VMEM((8, block, max(shares)), BF),
                pltpu.SemaphoreType.DMA((1 + parts,)),
            ),
        )
        weights = Halves(outs[::2], outs[1::2], [order[:-1] for order in orders])
        weights.step(count, (*query_side[1:], *result.others))
        started = weights.token
    else:
        full = dot(sources, row_grad, ((0,), (0,))).astype(BF)
        full = lax.psum_scatter(full, AXES, scatter_dimension=0, tiled=True).astype(F32)
        started = row_other
    result.others, up_keep, up_other = sync([], result.others, up_keep, up_other, started)[:-1]
    up_blocks = (up_keep.astype(F32) + up_other.astype(F32)).astype(BF)
    up_blocks = up_blocks.reshape(count, -1, units)
    up_blocks = lax.all_to_all(up_blocks, AXES, split_axis=0, concat_axis=0, tiled=True)
    query_rows = seq_blocks(jnp.stack([x[:, width:] for x in query_side]), 1)
    rows = lax.all_gather(
        jnp.concatenate([attended_low, query_rows, mixture], axis=1), AXES, axis=0, tiled=True
    )

    media_grad, latent_source, media_sums = with_weights(
        source_kernel,
        (after(row_grad, started), media[0], time_rows, media_gain[None]),
        key_value,
        (
            share((media_rows, width)),
            jax.ShapeDtypeStruct((latent_rows, width), F32),
            jax.ShapeDtypeStruct((8, width), F32),
        ),
        4 * source_count * width * width,
        scratch=[pltpu.VMEM((source_count, width), F32)],
    )
    latents_grad, latent_sums = call(
        lambda *refs: latent_kernel(seq_count, scaling, *refs),
        (*query_side, latent_source, latents[0], latent_gain[None], hidden_grad),
        (rows_low, jax.ShapeDtypeStruct((8, width), F32)),
        2 * latent_rows * width * width,
    )
    time_local = lax.dynamic_update_slice_in_dim(
        jnp.zeros((FRAMES, width), F32),
        media_sums[2 : 2 + frames_here],
        seq_index * frames_here,
        0,
    )
    sums = Sum(
        jnp.concatenate(
            [
                time_local,
                media_sums[:2],
                latent_sums[:2],
                ffn_sums[:2],
                jnp.zeros((2, width), F32),
            ],
            axis=0,
        ),
        [side, near, fold],
    )
    if regular:
        while weights.orders[0]:
            weights.split()
            weights.step(count)
            if len(weights.orders[0]) == 1:
                down_other, up_blocks = after(down_other, weights.token), after(up_blocks, weights.token)
            if result.orders[0]:
                result.split()
                result.step(count, (weights.token,))
            if sums.order:
                exchange(count, sums, wait=(weights.token,))
        full = jnp.concatenate([x[0] for x in weights.total()], axis=1)
    while result.orders[0]:
        result.split()
        result.step(count)
    down_grad = down_keep + down_other.astype(F32)
    up_grad = up_blocks.transpose(1, 0, 2).reshape(-1, count * units).astype(F32)
    latents_out = hidden + result.total()[0][0]

    def my_columns(x):
        return lax.dynamic_slice_in_dim(x, me * block, block, 1)

    out_grad = dot(my_columns(rows[:, 2 * width :]), rows[:, :width], ((0,), (0,)))
    latent_all = my_columns(rows_all.reshape(-1, 2 * width))
    query_grad = dot(latent_all, rows[:, width : 2 * width], ((0,), (0,))) * scaling
    while sums.order:
        exchange(count, sums)
    sums, others = sums.x, [0]
    for bit in head + tail:
        others += [mask ^ bit for mask in others]
    sums_parts = [trade(sums, mask, count) for mask in others[1:]]
    out_grad, query_grad, *sums_parts = sync([], out_grad, query_grad, *sums_parts)
    sums = sums + sum(sums_parts)
    return (
        latents_out.astype(BF)[None],
        latents_grad[None],
        media_grad[None],
        sums[:FRAMES],
        sums[FRAMES],
        sums[FRAMES + 1],
        sums[FRAMES + 2],
        sums[FRAMES + 3],
        sums[FRAMES + 4],
        sums[FRAMES + 5],
        query_grad,
        full[:, :width],
        full[:, width:],
        out_grad,
        up_grad,
        down_grad,
    )


def solution(mesh):
    rows, split = P("items", "seq", None), P(AXES, None)
    return jax.shard_map(
        shards,
        mesh=mesh,
        in_specs=(rows, rows, P("items")) + (P(),) * 7 + (split,) * 6 + (rows,),
        out_specs=(rows,) * 3 + (P(),) * 7 + (split,) * 6,
        check_vma=False,
    )
```

```python
import jax
import jax.numpy as jnp
from jax import lax
from jax.experimental import pallas as pl
from jax.experimental.pallas import tpu as pltpu
from jax.sharding import PartitionSpec as P

H = 16
FRAMES = 8
PATCH = 256
AXES = ("items", "seq")
BF = jnp.bfloat16
F32 = jnp.float32


def layer_norm(values, gain, bias):
    center = jnp.mean(values, axis=-1, keepdims=True)
    spread = jnp.mean(jnp.square(values - center), axis=-1, keepdims=True)
    rstd = lax.rsqrt(spread + 1e-05)
    unit = (values - center) * rstd
    return unit * gain + bias, unit, rstd


def layer_norm_back(grad, unit, rstd, gain):
    scaled = grad * gain
    inner = scaled - jnp.mean(scaled, axis=-1, keepdims=True)
    inner = inner - unit * jnp.mean(scaled * unit, axis=-1, keepdims=True)
    return inner * rstd, jnp.sum(grad * unit, axis=0), jnp.sum(grad, axis=0)


def dot(a, b, dims=((1,), (0,))):
    return lax.dot_general(a, b, (dims, ((), ())), preferred_element_type=F32)


def trade(x, mask, count):
    return lax.ppermute(x, AXES, [(i, i ^ mask) for i in range(count)])


def after(x, *others):
    return lax.optimization_barrier((x,) + others)[0]


class Gather:
    def __init__(self, x, order, me):
        self.x, self.order, self.me, self.done = x, list(order), me, []

    def rows(self):
        if isinstance(self.x, (list, tuple)):
            mine, other = self.x
            axis = sum(m > self.done[-1] for m in self.done)
            mine, other = jnp.expand_dims(mine, axis), jnp.expand_dims(other, axis)
            self.x = jnp.where(
                (self.me & self.done[-1]) != 0,
                jnp.concatenate([other, mine], axis),
                jnp.concatenate([mine, other], axis),
            )
        return self.x

    def send(self):
        return self.rows(), self.order[0]

    def take(self, sent, other):
        self.done.append(self.order.pop(0))
        self.x = (sent, other)


class GatherRel:
    def __init__(self, x, order):
        self.order, self.x = list(order), x

    def send(self):
        return self.x, self.order[0]

    def take(self, sent, other):
        self.order.pop(0)
        self.x = jnp.concatenate([sent, other], axis=0)


class GatherApart(GatherRel):
    def take(self, sent, other):
        if len(self.order) > 2:
            GatherRel.take(self, sent, other)
        else:
            self.order.pop(0)
            self.x = (sent, other)

    def last(self, count, join=False):
        mask = self.order.pop(0)
        pieces = (jnp.concatenate(self.x, axis=0),) if join else tuple(self.x)
        self.x = [*pieces, *[trade(x, mask, count) for x in pieces]]


class Halves:
    def __init__(self, keep, send, orders):
        self.orders, self.keep, self.sends = [list(order) for order in orders], keep, send

    def step(self, count, wait=()):
        sent = lax.optimization_barrier(tuple(self.sends) + tuple(wait))
        masks = [order.pop() for order in self.orders]
        self.others = [trade(x, mask, count) for x, mask in zip(sent, masks)]
        self.token = sent[0]

    def split(self):
        self.keep, self.sends = add_split(self.keep, self.others)

    def total(self):
        return [k.astype(F32) + o.astype(F32) for k, o in zip(self.keep, self.others)]


def add_split_kernel(pairs, *refs):
    ins, outs = refs[: 4 * pairs], refs[4 * pairs :]
    for k in range(pairs):
        keep, keep2, other, other2 = ins[4 * k : 4 * k + 4]
        out, send = outs[2 * k : 2 * k + 2]
        out[...] = (keep[...].astype(F32) + other[...].astype(F32)).reshape(out.shape)
        send[...] = (keep2[...].astype(F32) + other2[...].astype(F32)).astype(BF).reshape(send.shape)


def add_split(keeps, others):
    half = keeps[0].shape[0] // 2
    some = min(half, 2)
    ins, specs, outs, out_specs = [], [], [], []
    for keep, other in zip(keeps, others):
        tail = keep.shape[1:]
        low = pl.BlockSpec((some,) + tail, lambda i: (i, 0, 0))
        high = pl.BlockSpec((some,) + tail, lambda i: (i + half // some, 0, 0))
        ins += [keep, keep, other, other]
        specs += [low, high, low, high]
        outs += [jax.ShapeDtypeStruct((half,) + tail, F32), jax.ShapeDtypeStruct((half,) + tail, BF)]
        out_specs += [low, low]
    out = pl.pallas_call(
        lambda *refs: add_split_kernel(len(ins) // 4, *refs),
        grid=(half // some,),
        out_shape=tuple(outs),
        in_specs=specs,
        out_specs=tuple(out_specs),
        compiler_params=pltpu.CompilerParams(vmem_limit_bytes=56 << 20),
        cost_estimate=pl.CostEstimate(
            flops=1, bytes_accessed=1, transcendentals=0
        ),
    )(*ins)
    return list(out[::2]), list(out[1::2])


class Sum:
    def __init__(self, x, order):
        self.order, self.x = list(order), x

    def send(self):
        return self.x, self.order[0]

    def take(self, sent, other):
        self.order.pop(0)
        self.x = self.x + other


def exchange(count, *jobs, wait=()):
    sends = [job.send() for job in jobs]
    sent = lax.optimization_barrier(tuple(x for x, unused in sends) + tuple(wait))
    for job, x, (unused, mask) in zip(jobs, sent, sends):
        job.take(x, trade(x, mask, count))
    return sent[0]


def sync(jobs, *arrays):
    held = [job.x for job in jobs]
    held, arrays = lax.optimization_barrier((held, arrays))
    for job, x in zip(jobs, held):
        job.x = x
    return arrays


def share_seq(x, seq_count, count):
    return jnp.concatenate([x] + [trade(x, m, count) for m in range(1, seq_count)], axis=0)


def windows(width):
    size = width // H
    for pair in range(H // 2):
        base = (pair // 2) * 4 * size + (pair % 2) * 128
        yield pair, base, (2 * pair * size - base, (2 * pair + 1) * size - base, (2 * pair + 2) * size - base)


def stacked(rows, edges):
    column = lax.broadcasted_iota(jnp.int32, rows.shape, 1)
    first = (column >= edges[0]) & (column < edges[1])
    second = (column >= edges[1]) & (column < edges[2])
    zero = jnp.zeros_like(rows)
    return jnp.concatenate([jnp.where(first, rows, zero), jnp.where(second, rows, zero)], axis=0)


def unstacked(both, edges):
    count = both.shape[0] // 2
    column = lax.broadcasted_iota(jnp.int32, (count, both.shape[1]), 1)
    first = (column >= edges[0]) & (column < edges[1])
    second = (column >= edges[1]) & (column < edges[2])
    return jnp.where(first, both[:count], jnp.where(second, both[count:], 0.0))


def masked_scores(seen, queries, keys, media_rows):
    scores = dot(queries, keys, ((1,), (1,)))
    place = lax.broadcasted_iota(jnp.int32, scores.shape, 1)
    return jnp.where((place < seen) | (place >= media_rows), scores, -1e30)


def attend_kernel(media_rows, seen_ref, q_ref, kv_ref, out_ref):
    count, width = q_ref.shape
    seen = seen_ref[0]
    lane = lax.broadcasted_iota(jnp.int32, (count, 128), 1)
    stats = jnp.zeros((count, 128), F32)
    carry = None
    for pair, base, edges in windows(width):
        cols, value_cols = slice(base, base + 256), slice(width + base, width + base + 256)
        scores = masked_scores(seen, stacked(q_ref[:, cols], edges), kv_ref[:, cols], media_rows)
        top = jnp.max(scores, axis=1, keepdims=True)
        probs = jnp.exp(scores - top)
        total = jnp.sum(probs, axis=1, keepdims=True)
        mixed = unstacked(dot(probs.astype(BF), kv_ref[:, value_cols]) / total, edges)
        if pair % 2 == 0:
            out_ref[:, base : base + 128] = mixed[:, :128].astype(BF)
            carry = mixed[:, 128:]
        else:
            out_ref[:, base : base + 128] = (carry + mixed[:, :128]).astype(BF)
            out_ref[:, base + 128 : base + 256] = mixed[:, 128:].astype(BF)
        for k in range(2):
            rows = slice(k * count, (k + 1) * count)
            for n, value in enumerate((top, total)):
                value = value[rows]
                for term in range(3):
                    low = value.astype(BF).astype(F32)
                    stats = jnp.where(lane == (3 * n + term) * H + 2 * pair + k, low, stats)
                    value = value - low
    out_ref[:, width:] = stats.astype(BF)


def attend_back_kernel(media_rows, pieces, seen_ref, q_ref, kv_ref, *refs):
    dq_ref, dkv_ref = refs[pieces:]
    count, width = q_ref.shape
    seen = seen_ref[0]
    lane = lax.broadcasted_iota(jnp.int32, (count, 128), 1)
    packed = jnp.concatenate([ref[...] for ref in refs[:pieces]], axis=0)
    stats = packed[:, width:].astype(F32)

    def column(at):
        parts = []
        for k in range(2):
            here = (lane == at + k) | (lane == at + H + k) | (lane == at + 2 * H + k)
            parts.append(jnp.sum(jnp.where(here, stats, 0.0), axis=1, keepdims=True))
        return jnp.concatenate(parts, axis=0)

    carry = None
    for pair, base, edges in windows(width):
        cols = slice(base, base + 256)
        queries, grads = stacked(q_ref[:, cols], edges), stacked(packed[:, cols], edges)
        keys, values = kv_ref[:, cols], kv_ref[:, width + base : width + base + 256]
        scores = masked_scores(seen, queries, keys, media_rows)
        probs = jnp.exp(scores - column(2 * pair))
        prob_grad = dot(grads, values, ((1,), (1,)))
        score_grad = (probs * (prob_grad - column(3 * H + 2 * pair))).astype(BF)
        new = (
            (dq_ref, 0, dot(score_grad, keys)),
            (dkv_ref, 0, dot(score_grad, queries, ((0,), (0,)))),
            (dkv_ref, width, dot(probs.astype(BF), grads, ((0,), (0,)))),
        )
        new = [(ref, at + base, unstacked(x, edges) if ref is dq_ref else x) for ref, at, x in new]
        if pair % 2 == 0:
            for ref, at, x in new:
                ref[:, at : at + 128] = x[:, :128].astype(BF)
            carry = [x[:, 128:] for unused_ref, unused_at, x in new]
        else:
            for (ref, at, x), old in zip(new, carry):
                ref[:, at : at + 128] = (old + x[:, :128]).astype(BF)
                ref[:, at + 128 : at + 256] = x[:, 128:].astype(BF)


def lane_heads(shape, width, dim):
    lane = lax.broadcasted_iota(jnp.int32, shape, dim)
    column = lax.broadcasted_iota(jnp.int32, shape, 1 - dim)
    size = width // H
    first = (lane % H) * size
    return lane // H, column - first, (column >= first) & (column < first + size)


def three_terms(x):
    terms = []
    for unused in range(3):
        terms.append(x.astype(BF))
        x = x - terms[-1].astype(F32)
    return terms


def combine_kernel(pieces, whole, me_ref, *refs):
    parts, refs = refs[:pieces], refs[pieces:]
    latent_ref, gain_ref, bias_ref, *refs = refs
    *refs, wide_ref, low_ref, stat_ref, hidden_ref, ffn_ref, w_ref, sems = refs
    waits = whole.fetch(me_ref[0], refs, w_ref, sems)
    rows, width = latent_ref.shape
    group, unused, inside = lane_heads((128, width), width, 0)
    spread_top = jnp.where(inside & (group < 3), 1.0, 0.0).astype(BF)
    spread_total = jnp.where(inside & (group >= 3) & (group < 6), 1.0, 0.0).astype(BF)
    tops = [dot(ref[:, width:], spread_top) for ref in parts]
    top = tops[0]
    for other in tops[1:]:
        top = jnp.maximum(top, other)
    total = jnp.zeros((rows, width), F32)
    mixed = jnp.zeros((rows, width), F32)
    for ref, mine in zip(parts, tops):
        weight = jnp.exp(mine - top) * dot(ref[:, width:], spread_total)
        total += weight
        mixed += weight * ref[:, :width].astype(F32)
    mixed = mixed / total
    wide_ref[...] = mixed
    low = mixed.astype(BF)
    low_ref[...] = low
    group, offset, unused = lane_heads((width, 128), width, 1)
    stats = jnp.zeros((rows, 128), F32)
    for k, term in enumerate(three_terms(top + jnp.log(total))):
        pick = jnp.where((group == k) & (offset == 0), 1.0, 0.0).astype(BF)
        stats += dot(term, pick)
    stat_ref[...] = stats
    for wait in waits:
        wait.wait()
    hidden = latent_ref[...].astype(F32) + dot(low, w_ref[...])
    hidden_ref[...] = hidden
    ffn_ref[...] = layer_norm(hidden, gain_ref[...], bias_ref[...])[0].astype(BF)


def hidden_back_kernel(whole, me_ref, *refs):
    keep_ref, other_ref, hidden_ref, upstream_ref, wide_ref, stat_ref, gain_ref, *refs = refs
    *refs, hidden_grad_ref, low_ref, packed_ref, sums_ref, w_ref, sems = refs
    waits = whole.fetch(me_ref[0], refs, w_ref, sems)
    rows, width = hidden_ref.shape
    grad = keep_ref[0].astype(F32) + other_ref[0].astype(F32)
    gain = gain_ref[...]
    unused, unit, rstd = layer_norm(hidden_ref[...], gain, gain)
    norm_grad, gain_grad, bias_grad = layer_norm_back(grad, unit, rstd, gain)
    row = lax.broadcasted_iota(jnp.int32, (8, width), 0)
    sums_ref[...] = jnp.where(row == 0, gain_grad[None], jnp.where(row == 1, bias_grad[None], 0.0))
    hidden_grad = upstream_ref[...].astype(F32) + norm_grad
    hidden_grad_ref[...] = hidden_grad
    low = hidden_grad.astype(BF)
    low_ref[...] = low
    for wait in waits:
        wait.wait()
    mixture_grad = dot(low, w_ref[...], ((1,), (1,))).astype(BF)
    packed_ref[:, :width] = mixture_grad
    group, unused, inside = lane_heads((width, 128), width, 1)
    heads = jnp.where(inside & (group >= 3) & (group < 6), 1.0, 0.0).astype(BF)
    inner = jnp.zeros((rows, 128), F32)
    for term in three_terms(wide_ref[...] * mixture_grad.astype(F32)):
        inner += dot(term, heads)
    lane = lax.broadcasted_iota(jnp.int32, (rows, 128), 1) // H
    stats = stat_ref[...]
    for k, term in enumerate(three_terms(inner)):
        stats = jnp.where(lane == 3 + k, term.astype(F32), stats)
    packed_ref[:, width:] = stats.astype(BF)


def owner_of(place, order):
    return sum(mask for k, mask in enumerate(order) if (place >> k) % 2)


def place_of(owner, order):
    return sum(((owner // mask) % 2) << k for k, mask in enumerate(order))


class Stacks:
    def __init__(self, parts, orders):
        self.each = len(parts[0])
        self.arrays = [x for pieces in parts for x in pieces]
        self.orders = orders
        self.cols = sum(pieces[0].shape[2] for pieces in parts)
        widths = [pieces[0].shape[2] for pieces in parts]
        self.ends = [sum(widths[: k + 1]) for k in range(len(parts))]

    def fetch(self, me, refs, into, sems):
        at, waits = 0, []
        for k, order in enumerate(self.orders):
            pieces = refs[self.each * k : self.each * (k + 1)]
            some, block, cols = pieces[0].shape
            for place in range(self.each * some):
                owner = me ^ owner_of(place, order)
                to = into.at[pl.ds(pl.multiple_of(owner * block, 16), block), at : at + cols]
                source = pieces[place // some].at[place % some]
                pltpu.make_async_copy(source, to, sems.at[k]).start()
            part = into.at[:, at : at + cols]
            waits.append(pltpu.make_async_copy(part, part, sems.at[k]))
            at += cols
        return waits


class Plain:
    def __init__(self, x):
        self.arrays, self.orders = [x], (None,)
        self.cols = x.shape[1]
        self.ends = [self.cols]

    def fetch(self, me, refs, into, sems):
        copy = pltpu.make_async_copy(refs[0], into, sems.at[0])
        copy.start()
        return [copy]


def halves_kernel(me_ref, s_ref, mine_ref, other_ref):
    block = 48
    for parity in range(2):

        @pl.when(me_ref[0] % 2 == parity)
        def _():
            for out_ref, which in ((mine_ref, parity), (other_ref, 1 - parity)):
                for n in range(out_ref.shape[1] // block):
                    at = (2 * n + which) * block
                    out_ref[:, n * block : (n + 1) * block] = s_ref[:, at : at + block]


def order_kernel(whole, me_ref, *refs):
    *refs, out_ref, sems = refs
    for wait in whole.fetch(me_ref[0], refs, out_ref, sems):
        wait.wait()


def project_kernel(whole, me_ref, s_ref, *refs):
    *refs, out_ref, w_ref, sems = refs
    at = 0
    for wait, end in zip(whole.fetch(me_ref[0], refs, w_ref, sems), whole.ends):
        wait.wait()
        out_ref[:, at:end] = dot(s_ref[...], w_ref[:, at:end]).astype(BF)
        at = end


def gelu_parts(x):
    c = 0.7978845608028654
    t = jnp.tanh(c * (x + 0.044715 * (x * x * x)))
    slope = 0.5 * (1.0 + t) + 0.5 * x * (1.0 - t * t) * (c * (1.0 + 3 * 0.044715 * (x * x)))
    return 0.5 * x * (1.0 + t), slope


def ffn_kernel(
    order,
    me_ref,
    mine_ref,
    other_ref,
    up_ref,
    down_ref,
    all_ref,
    keep_ref,
    send_ref,
    active_ref,
    pre_ref,
    rows_ref,
    grad_rows_ref,
    sem,
):
    some, each, width = mine_ref.shape
    for place in range(2 * some):
        owner = me_ref[0] ^ owner_of(place, order)
        pltpu.make_async_copy(
            all_ref.at[owner, :, width : 2 * width],
            grad_rows_ref.at[place * each : (place + 1) * each],
            sem,
        ).start()
    rows_ref[: some * each, :] = mine_ref[...].reshape(some * each, width)
    rows_ref[some * each :, :] = other_ref[...].reshape(some * each, width)
    active, slope = gelu_parts(dot(rows_ref[...], up_ref[...]))
    active_ref[...] = active.astype(BF)
    pltpu.make_async_copy(grad_rows_ref, grad_rows_ref, sem).wait()
    pre_grad = (dot(grad_rows_ref[...], down_ref[...], ((1,), (1,))) * slope).astype(BF)
    pre_ref[...] = pre_grad
    total = dot(pre_grad, up_ref[...], ((1,), (1,)))
    keep_ref[...] = total[: some * each].reshape(keep_ref.shape)
    send_ref[...] = total[some * each :].astype(BF).reshape(send_ref.shape)


def ffn_sums_kernel(
    rows_ref,
    grad_rows_ref,
    active_ref,
    pre_ref,
    down_ref,
    down_keep_ref,
    down_send_ref,
    up_keep_ref,
    up_send_ref,
    keep_ref,
    send_ref,
):
    first = ((0,), (0,))
    units = down_keep_ref.shape[0]
    down = dot(active_ref[...], grad_rows_ref[...], first)
    down_keep_ref[...] = down[:units]
    down_send_ref[...] = down[units:].astype(BF)
    up = dot(rows_ref[...], pre_ref[...], first)
    up_keep_ref[...] = up[:, :units].astype(BF)
    up_send_ref[...] = up[:, units:].astype(BF)
    out = dot(active_ref[...], down_ref[...])
    half = out.shape[0] // 2
    keep_ref[...] = out[:half].reshape(keep_ref.shape)
    send_ref[...] = out[half:].astype(BF).reshape(send_ref.shape)


def source_kernel(whole, me_ref, g_ref, media_ref, time_ref, gain_ref, *refs):
    *refs, media_grad_ref, latent_ref, sums_ref, acc_ref, w_ref, sems = refs
    at = 0
    for wait, end in zip(whole.fetch(me_ref[0], refs, w_ref, sems), whole.ends):
        wait.wait()
        new = dot(g_ref[:, at:end], w_ref[:, at:end], ((1,), (1,)))
        acc_ref[...] = acc_ref[...] + new if at else new
        at = end
    media_rows, width = media_ref.shape
    gain = gain_ref[...]
    rows = [jnp.zeros((1, width), F32), jnp.zeros((1, width), F32)]
    for frame in range(media_rows // PATCH):
        here = slice(frame * PATCH, (frame + 1) * PATCH)
        shifted = media_ref[here, :].astype(F32) + time_ref[frame : frame + 1, :]
        unused, unit, rstd = layer_norm(shifted, gain, gain)
        grad = acc_ref[here, :]
        shifted_grad, gain_grad, bias_grad = layer_norm_back(grad, unit, rstd, gain)
        media_grad_ref[here, :] = shifted_grad.astype(BF)
        rows[0] += gain_grad[None]
        rows[1] += bias_grad[None]
        rows.append(jnp.sum(shifted_grad, axis=0, keepdims=True))
    at = lax.broadcasted_iota(jnp.int32, sums_ref.shape, 0)
    sums = jnp.zeros(sums_ref.shape, F32)
    for k, row in enumerate(rows):
        sums = jnp.where(at == k, row, sums)
    sums_ref[...] = sums
    latent_ref[...] = acc_ref[media_rows:, :]


def latent_kernel(pieces, scaling, *refs):
    parts, refs = refs[:pieces], refs[pieces:]
    source_ref, latent_ref, gain_ref, hidden_grad_ref, out_ref, sums_ref = refs
    gain = gain_ref[...]
    width = gain.shape[1]
    query_side = sum(ref[:, :width].astype(F32) for ref in parts)
    grad = source_ref[...] + query_side * scaling
    unused, unit, rstd = layer_norm(latent_ref[...].astype(F32), gain, gain)
    latent_grad, gain_grad, bias_grad = layer_norm_back(grad, unit, rstd, gain)
    out_ref[...] = (hidden_grad_ref[...] + latent_grad).astype(BF)
    at = lax.broadcasted_iota(jnp.int32, sums_ref.shape, 0)
    sums_ref[...] = jnp.where(
        at == 0, gain_grad[None], jnp.where(at == 1, bias_grad[None], 0.0)
    )


def sums_kernel(orders, me_ref, s_ref, s2_ref, g_ref, g2_ref, *refs):
    *out_refs, s_held, g_held, held, sems = refs
    me = me_ref[0] - me_ref[0] % 2
    half, block, unused = out_refs[0].shape
    widths = [ref.shape[2] for ref in out_refs[::2]]
    starts = [sum(widths[:k]) for k in range(len(widths))]
    rows = s_ref.shape[0]
    for k, ref in enumerate((s_ref, s2_ref)):
        pltpu.make_async_copy(ref, s_held.at[k * rows : (k + 1) * rows], sems.at[0]).start()
    for part in range(len(orders)):
        columns = slice(starts[part], starts[part] + widths[part])
        for k, ref in enumerate((g_ref, g2_ref)):
            to = g_held.at[k * rows : (k + 1) * rows, columns]
            pltpu.make_async_copy(ref.at[:, columns], to, sems.at[1 + part]).start()
    pltpu.make_async_copy(s_held, s_held, sems.at[0]).wait()
    some = held.shape[0]
    for part, order in enumerate(orders):
        columns = slice(starts[part], starts[part] + widths[part])
        here = g_held.at[:, columns]
        pltpu.make_async_copy(here, here, sems.at[1 + part]).wait()
        first = (me // order[-1]) % 2
        for start in range(0, 2 * half, some):
            full = dot(s_held[:, start * block : (start + some) * block], here[...], ((0,), (0,)))
            cols = widths[part]
            held[:, :, :cols] = full.astype(BF).reshape(some, block, cols)
            for bit in range(2):

                @pl.when(first == bit)
                def _(bit=bit, start=start, part=part, order=order, cols=cols):
                    for n in range(some):
                        owner = 2 * (start + n)
                        place = place_of(owner ^ me, order) % half
                        send = (owner // order[-1]) % 2 != bit
                        out_refs[2 * part + send][place] = held[n, :, :cols]


SCALAR = pl.BlockSpec(memory_space=pltpu.SMEM)
FAR = pl.BlockSpec(memory_space=pl.ANY)


def call(kernel, inputs, outputs, flops, specs=(), far_outputs=False, scratch=()):
    specs = dict(specs)

    def whole(x):
        return pl.BlockSpec(x.shape, lambda i, nd=len(x.shape): (0,) * nd)

    nbytes = sum(x.size * x.dtype.itemsize for x in inputs)
    nbytes += sum(x.size * x.dtype.itemsize for x in outputs)
    return pl.pallas_call(
        kernel,
        grid=(1,),
        out_shape=tuple(outputs),
        in_specs=[specs.get(n, whole(x)) for n, x in enumerate(inputs)],
        out_specs=tuple(FAR if far_outputs else whole(x) for x in outputs),
        scratch_shapes=list(scratch),
        compiler_params=pltpu.CompilerParams(vmem_limit_bytes=56 << 20),
        cost_estimate=pl.CostEstimate(flops=flops // 1000, bytes_accessed=nbytes // 1000, transcendentals=0),
    )(*inputs)


def shards(
    media,
    latents,
    frames,
    time_embed,
    media_gain,
    media_bias,
    latent_gain,
    latent_bias,
    ffn_gain,
    ffn_bias,
    w_query,
    w_key,
    w_value,
    w_out,
    w_up,
    w_down,
    grad_out,
):
    item_count, seq_count = lax.axis_size("items"), lax.axis_size("seq")
    count = item_count * seq_count
    seq_index = lax.axis_index("seq")
    me = lax.axis_index("items") * seq_count + seq_index
    unused_items, media_rows, width = media.shape
    latent_rows = latents.shape[1]
    head_size = width // H
    frames_here = media_rows // PATCH
    scaling = head_size ** (-0.5)

    bits = [1 << k for k in reversed(range(30))]
    item_bits = [m for m in bits if seq_count <= m < count]
    seq_bits = [m for m in bits if m < seq_count]
    head, (fold, near), side, tail = item_bits[:-2], item_bits[-2:], seq_bits[0], seq_bits[1:]
    orders = (
        head + [fold, near, side] + tail,
        head + [side, fold, near] + tail,
        head + [near, side, fold] + tail,
    )
    ffn_order = item_bits + seq_bits[:-1]
    core = seq_bits[-1]
    block = width // count
    regular = block % 16 == 0

    def share(x):
        return jax.ShapeDtypeStruct(x, BF)

    latent_in = latents[0].astype(F32)
    latent_normed, latent_unit, latent_rstd = layer_norm(latent_in, latent_gain, latent_bias)
    latent_normed = latent_normed.astype(BF)
    time_rows = lax.dynamic_slice_in_dim(time_embed, seq_index * frames_here, frames_here, 0)
    shifted = (
        media[0].astype(F32).reshape(frames_here, PATCH, width) + time_rows[:, None, :]
    ).reshape(media_rows, width)
    media_normed, media_unit, media_rstd = layer_norm(shifted, media_gain, media_bias)
    sources = jnp.concatenate([media_normed.astype(BF), latent_normed], axis=0)

    def in_columns(x):
        return x.reshape(x.shape[0], count, -1).transpose(1, 0, 2)

    def spread(x):
        x = lax.all_to_all(x, AXES, split_axis=0, concat_axis=0, tiled=True)
        return x.reshape(-1, x.shape[2])

    cols_here = width // seq_count

    def seq_blocks(x, axis):
        return jnp.concatenate(
            [
                lax.dynamic_index_in_dim(x, seq_index ^ t, 0, keepdims=False)
                for t in range(seq_count)
            ],
            axis=axis,
        )

    def columns_of(x, m):
        return lax.dynamic_slice_in_dim(x, (seq_index ^ m) * cols_here, cols_here, 1)

    def reordered(x, m):
        blocks = x.reshape(seq_count, latent_rows, x.shape[1])
        return jnp.concatenate([blocks[t ^ m] for t in range(seq_count)], axis=0)

    parts = len(orders)
    units = w_down.shape[0]
    out_orders = (head + [near, fold, side] + tail, head + [near, side, fold] + tail)
    shares = (width * 5 // 6, width * 5 // 6, width // 3)
    def query_pieces(x):
        pieces = [columns_of(x, m) for m in range(seq_count)]
        return [pieces[0]] + [trade(pieces[m], m, count) for m in range(1, seq_count)]

    if regular:
        first = GatherRel(jnp.concatenate([w_key, w_value], axis=1)[None], head)
        second = GatherRel(w_out[None], head + [near])

        def split(x, shares, orders, done):
            return [
                GatherApart(x[..., sum(shares[:k]) : sum(shares[: k + 1])], order[done:])
                for k, order in enumerate(orders)
            ]

        while first.order:
            started = exchange(count, first)
        latent_item = share_seq(after(latent_normed, started), seq_count, count)
        pieces = query_pieces(after(w_query, started))
        half_mine, half_other = call(
            halves_kernel,
            (me[None], sources),
            (share((sources.shape[0], width // 2)),) * 2,
            0,
            specs={0: SCALAR},
        )
        rows_mine = jnp.concatenate([latent_normed, grad_out[0]], axis=1)
        sources, latent_item, half_mine, half_other, rows_mine, *pieces = sync(
            [first], sources, latent_item, half_mine, half_other, rows_mine, *pieces
        )
        query_cols = Gather(seq_blocks(jnp.stack(pieces), 0), [near] + head + [fold], me)
        first = split(first.x, shares, orders, len(head))
        exchange(count, *first, second, query_cols)
        sync([*first, second, query_cols])
        exchange(count, *first, second, query_cols)
        up_in, rows_mine = sync([*first, second, query_cols], w_up, rows_mine)
        rows_all = lax.all_gather(rows_mine, AXES, axis=0)
        second = split(second.x, (width // 2, width // 2), out_orders, len(head) + 1)
        exchange(count, *first, query_cols)
        sources, latent_item, half_other, up_in = sync(
            [*first, query_cols], sources, latent_item, half_other, in_columns(up_in)
        )
        for job in first:
            job.last(count)
    else:
        up_mine = spread(in_columns(w_up))
        rows_all = lax.all_gather(
            jnp.concatenate([latent_normed, grad_out[0]], axis=1), AXES, axis=0
        )
        latent_item = share_seq(latent_normed, seq_count, count)
        query_cols = Gather(seq_blocks(jnp.stack(query_pieces(w_query)), 0), item_bits, me)
        while query_cols.order:
            exchange(count, query_cols)
        both = lax.all_gather(jnp.concatenate([w_key, w_value], 1), AXES, axis=0, tiled=True)
        key_value = Plain(both)
        out_full = Plain(lax.all_gather(w_out, AXES, axis=0, tiled=True))

    def with_weights(kernel, inputs, whole, outputs, flops, keep=True, scratch=()):
        inputs = [me[None]] + list(inputs)
        specs = {0: SCALAR}
        for n in range(len(whole.arrays)):
            specs[len(inputs) + n] = FAR
        scratch = list(scratch) + ([pltpu.VMEM((width, whole.cols), BF)] if keep else [])
        return call(
            lambda *refs: kernel(whole, *refs),
            (*inputs, *whole.arrays),
            outputs,
            flops,
            specs=specs,
            scratch=scratch + [pltpu.SemaphoreType.DMA((len(whole.orders),))],
        )

    query_slice = query_cols.rows().reshape(width, cols_here)
    query_mine = (dot(latent_item, query_slice) * scaling).astype(BF)
    sends = [reordered(query_mine, m) for m in range(1, seq_count)]
    if regular:
        up_mine = spread(up_in)
        query_mine, *sends = sync([*first, *second], query_mine, *sends)
        key_value = Stacks([job.x for job in first], orders)
        exchange(count, *second)
    pieces = [query_mine] + [trade(x, m + 1, count) for m, x in enumerate(sends)]
    source_count = sources.shape[0]
    keys = with_weights(
        project_kernel,
        (sources,),
        key_value,
        (share((source_count, 2 * width)),),
        4 * source_count * width * width,
    )[0]
    if regular:
        keys, half_other, up_mine, *pieces = sync(second, keys, half_other, up_mine, *pieces)
        half_other = trade(half_other, 1, count)
        exchange(count, *second)
    queries = seq_blocks(jnp.stack(pieces), 1)
    seen = jnp.clip((frames - seq_index * frames_here) * PATCH, 0, media_rows).astype(jnp.int32)
    all_rows = queries.shape[0]
    pair_flops = 2 * H // 2 * 2 * all_rows * 256 * sources.shape[0]
    mixed = call(
        lambda *refs: attend_kernel(media_rows, *refs),
        (seen, queries, keys),
        (share((all_rows, width + 128)),),
        2 * pair_flops,
        specs={0: SCALAR},
    )[0]

    def own_parts(x):
        blocks = x.reshape(seq_count, latent_rows, x.shape[1])
        return [blocks[0]] + [trade(blocks[m], m, count) for m in range(1, seq_count)]


    mixed_parts = own_parts(mixed)
    if regular:
        mixed_parts = sync(second, *mixed_parts)
        for job in second:
            job.last(count, join=True)
        sync(second)
        out_full = Stacks([job.x for job in second], out_orders)
    up_other, down_other = trade(up_mine, core, count), trade(w_down, core, count)
    up_pair = jnp.concatenate([up_mine, up_other], axis=1)
    down_pair = jnp.concatenate([w_down, down_other], axis=0)
    rows_wide = jax.ShapeDtypeStruct((latent_rows, width), F32)
    rows_low = jax.ShapeDtypeStruct((latent_rows, width), BF)
    mixture_wide, mixture, log_total, hidden, ffn_in = with_weights(
        lambda *refs: combine_kernel(seq_count, *refs),
        (*mixed_parts, latents[0], ffn_gain[None], ffn_bias[None]),
        out_full,
        (
            rows_wide,
            rows_low,
            jax.ShapeDtypeStruct((latent_rows, 128), F32),
            rows_wide,
            rows_low,
        ),
        2 * latent_rows * width * width,
    )
    ffn_rows = GatherRel(ffn_in[None], ffn_order)
    while len(ffn_rows.order) > 1:
        exchange(count, ffn_rows)
    mine = ffn_rows.x
    other = trade(mine, ffn_order[-1], count)
    some = mine.shape[0]
    all_ffn = 2 * some * latent_rows
    units_low = share((all_ffn, 2 * units))
    halves = (jax.ShapeDtypeStruct(mine.shape, F32), share(mine.shape))
    ffn_flops = 2 * all_ffn * 2 * units * width
    keep, send, active, pre, ffn_all, grad_all = call(
        lambda *refs: ffn_kernel(ffn_order, *refs),
        (me[None], mine, other, up_pair, down_pair, rows_all),
        (*halves, units_low, units_low, *(share((all_ffn, width)),) * 2),
        3 * ffn_flops,
        specs={0: SCALAR, 5: FAR},
        scratch=(pltpu.SemaphoreType.DMA(()),),
    )
    back = Halves([keep], [send], [ffn_order])
    back.step(count)
    down_keep, down_send, up_keep, up_send, keep, send = call(
        ffn_sums_kernel,
        (ffn_all, after(grad_all, back.token), active, pre, down_pair),
        (
            jax.ShapeDtypeStruct((units, width), F32),
            share((units, width)),
            share((width, units)),
            share((width, units)),
            *halves,
        ),
        3 * ffn_flops,
    )
    result = Halves([keep], [send], [ffn_order])
    wait = (down_send,)
    while back.orders[0]:
        back.split()
        back.step(count, wait)
        if not wait:
            result.split()
        result.step(count, (back.token,))
        wait = ()
        if back.orders[0]:
            back.others, result.others = lax.optimization_barrier((back.others, result.others))

    hidden_grad, attended_low, packed, ffn_sums = with_weights(
        hidden_back_kernel,
        (
            back.keep[0],
            back.others[0],
            hidden,
            grad_out[0],
            mixture_wide,
            log_total,
            ffn_gain[None],
        ),
        out_full,
        (
            rows_wide,
            rows_low,
            share((latent_rows, width + 128)),
            jax.ShapeDtypeStruct((8, width), F32),
        ),
        2 * latent_rows * width * width,
    )
    down_send, up_send = sync([], down_send, up_send, packed)[:2]
    down_other, up_other = trade(down_send, core, count), trade(up_send, core, count)
    pieces = [packed] + [trade(packed, m, count) for m in range(1, seq_count)]
    result.split()
    result.step(count, (packed,))
    query_part, row_grad = call(
        lambda *refs: attend_back_kernel(media_rows, seq_count, *refs),
        (seen, queries, keys, *pieces),
        (share((all_rows, width)), share(keys.shape)),
        5 * pair_flops,
        specs={0: SCALAR},
    )
    sends = [reordered(columns_of(query_part, m), m) for m in range(seq_count)]
    row_send, result.others, *sends = lax.optimization_barrier((row_grad, result.others, *sends))
    row_other = trade(row_send, 1, count)
    pieces = [sends[0]] + [trade(sends[m], m, count) for m in range(1, seq_count)]
    row_grad, row_other, *pieces = sync([], row_send, row_other, *pieces)
    query_cols_grad = sum(x.astype(F32) for x in pieces).astype(BF)
    query_side = dot(query_cols_grad, query_slice, ((1,), (1,))).astype(BF)
    query_side = own_parts(jnp.concatenate([query_side, query_cols_grad], axis=1))

    if regular:
        outs = call(
            lambda *refs: sums_kernel([order[:-1] for order in orders], *refs),
            (me[None], half_mine, half_other, row_grad, row_other),
            tuple(share((count // 4, block, cols)) for cols in shares for unused in range(2)),
            4 * width * width * source_count,
            specs={0: SCALAR, 1: FAR, 2: FAR, 3: FAR, 4: FAR},
            scratch=(
                pltpu.VMEM((2 * source_count, width // 2), BF),
                pltpu.VMEM((2 * source_count, 2 * width), BF),
                pltpu.VMEM((8, block, max(shares)), BF),
                pltpu.SemaphoreType.DMA((1 + parts,)),
            ),
        )
        weights = Halves(outs[::2], outs[1::2], [order[:-1] for order in orders])
        weights.step(count, (*query_side[1:], *result.others))
        started = weights.token
    else:
        full = dot(sources, row_grad, ((0,), (0,))).astype(BF)
        full = lax.psum_scatter(full, AXES, scatter_dimension=0, tiled=True).astype(F32)
        started = row_other
    result.others, up_keep, up_other = sync([], result.others, up_keep, up_other, started)[:-1]
    up_blocks = (up_keep.astype(F32) + up_other.astype(F32)).astype(BF)
    up_blocks = up_blocks.reshape(count, -1, units)
    up_blocks = lax.all_to_all(up_blocks, AXES, split_axis=0, concat_axis=0, tiled=True)
    query_rows = seq_blocks(jnp.stack([x[:, width:] for x in query_side]), 1)
    rows = lax.all_gather(
        jnp.concatenate([attended_low, query_rows, mixture], axis=1), AXES, axis=0, tiled=True
    )

    media_grad, latent_source, media_sums = with_weights(
        source_kernel,
        (after(row_grad, started), media[0], time_rows, media_gain[None]),
        key_value,
        (
            share((media_rows, width)),
            jax.ShapeDtypeStruct((latent_rows, width), F32),
            jax.ShapeDtypeStruct((8, width), F32),
        ),
        4 * source_count * width * width,
        scratch=[pltpu.VMEM((source_count, width), F32)],
    )
    latents_grad, latent_sums = call(
        lambda *refs: latent_kernel(seq_count, scaling, *refs),
        (*query_side, latent_source, latents[0], latent_gain[None], hidden_grad),
        (rows_low, jax.ShapeDtypeStruct((8, width), F32)),
        2 * latent_rows * width * width,
    )
    time_local = lax.dynamic_update_slice_in_dim(
        jnp.zeros((FRAMES, width), F32),
        media_sums[2 : 2 + frames_here],
        seq_index * frames_here,
        0,
    )
    sums = Sum(
        jnp.concatenate(
            [
                time_local,
                media_sums[:2],
                latent_sums[:2],
                ffn_sums[:2],
                jnp.zeros((2, width), F32),
            ],
            axis=0,
        ),
        [side, near, fold],
    )
    if regular:
        while weights.orders[0]:
            weights.split()
            weights.step(count)
            if len(weights.orders[0]) == 1:
                down_other, up_blocks = after(down_other, weights.token), after(up_blocks, weights.token)
            if result.orders[0]:
                result.split()
                result.step(count, (weights.token,))
            if sums.order:
                exchange(count, sums, wait=(weights.token,))
        full = jnp.concatenate([x[0] for x in weights.total()], axis=1)
    while result.orders[0]:
        result.split()
        result.step(count)
    down_grad = down_keep + down_other.astype(F32)
    up_grad = up_blocks.transpose(1, 0, 2).reshape(-1, count * units).astype(F32)
    latents_out = hidden + result.total()[0][0]

    def my_columns(x):
        return lax.dynamic_slice_in_dim(x, me * block, block, 1)

    out_grad = dot(my_columns(rows[:, 2 * width :]), rows[:, :width], ((0,), (0,)))
    latent_all = my_columns(rows_all.reshape(-1, 2 * width))
    query_grad = dot(latent_all, rows[:, width : 2 * width], ((0,), (0,))) * scaling
    while sums.order:
        exchange(count, sums)
    sums, others = sums.x, [0]
    for bit in head + tail:
        others += [mask ^ bit for mask in others]
    sums_parts = [trade(sums, mask, count) for mask in others[1:]]
    out_grad, query_grad, *sums_parts = sync([], out_grad, query_grad, *sums_parts)
    sums = sums + sum(sums_parts)
    return (
        latents_out.astype(BF)[None],
        latents_grad[None],
        media_grad[None],
        sums[:FRAMES],
        sums[FRAMES],
        sums[FRAMES + 1],
        sums[FRAMES + 2],
        sums[FRAMES + 3],
        sums[FRAMES + 4],
        sums[FRAMES + 5],
        query_grad,
        full[:, :width],
        full[:, width:],
        out_grad,
        up_grad,
        down_grad,
    )


def solution(mesh):
    rows, split = P("items", "seq", None), P(AXES, None)
    return jax.shard_map(
        shards,
        mesh=mesh,
        in_specs=(rows, rows, P("items")) + (P(),) * 7 + (split,) * 6 + (rows,),
        out_specs=(rows,) * 3 + (P(),) * 7 + (split,) * 6,
        check_vma=False,
    )
```

```python
import jax
import jax.numpy as jnp
from jax import lax
from jax.experimental import pallas as pl
from jax.experimental.pallas import tpu as pltpu
from jax.sharding import PartitionSpec as P

H = 16
FRAMES = 8
PATCH = 256
AXES = ("items", "seq")
BF = jnp.bfloat16
F32 = jnp.float32


def layer_norm(values, gain, bias):
    center = jnp.mean(values, axis=-1, keepdims=True)
    spread = jnp.mean(jnp.square(values - center), axis=-1, keepdims=True)
    rstd = lax.rsqrt(spread + 1e-05)
    unit = (values - center) * rstd
    return unit * gain + bias, unit, rstd


def layer_norm_back(grad, unit, rstd, gain):
    scaled = grad * gain
    inner = scaled - jnp.mean(scaled, axis=-1, keepdims=True)
    inner = inner - unit * jnp.mean(scaled * unit, axis=-1, keepdims=True)
    return inner * rstd, jnp.sum(grad * unit, axis=0), jnp.sum(grad, axis=0)


def dot(a, b, dims=((1,), (0,))):
    return lax.dot_general(a, b, (dims, ((), ())), preferred_element_type=F32)


def trade(x, mask, count):
    return lax.ppermute(x, AXES, [(i, i ^ mask) for i in range(count)])


def after(x, *others):
    return lax.optimization_barrier((x,) + others)[0]


class Gather:
    def __init__(self, x, order, me):
        self.x, self.order, self.me, self.done = x, list(order), me, []

    def rows(self):
        if isinstance(self.x, (list, tuple)):
            mine, other = self.x
            axis = sum(m > self.done[-1] for m in self.done)
            mine, other = jnp.expand_dims(mine, axis), jnp.expand_dims(other, axis)
            self.x = jnp.where(
                (self.me & self.done[-1]) != 0,
                jnp.concatenate([other, mine], axis),
                jnp.concatenate([mine, other], axis),
            )
        return self.x

    def send(self):
        return self.rows(), self.order[0]

    def take(self, sent, other):
        self.done.append(self.order.pop(0))
        self.x = (sent, other)


class GatherRel:
    def __init__(self, x, order):
        self.order, self.x = list(order), x

    def send(self):
        return self.x, self.order[0]

    def take(self, sent, other):
        self.order.pop(0)
        self.x = jnp.concatenate([sent, other], axis=0)


class GatherApart(GatherRel):
    def take(self, sent, other):
        if len(self.order) > 2:
            GatherRel.take(self, sent, other)
        else:
            self.order.pop(0)
            self.x = (sent, other)

    def last(self, count, join=False):
        mask = self.order.pop(0)
        pieces = (jnp.concatenate(self.x, axis=0),) if join else tuple(self.x)
        self.x = [*pieces, *[trade(x, mask, count) for x in pieces]]


class Halves:
    def __init__(self, keep, send, orders):
        self.orders, self.keep, self.sends = [list(order) for order in orders], keep, send

    def step(self, count, wait=()):
        sent = lax.optimization_barrier(tuple(self.sends) + tuple(wait))
        masks = [order.pop() for order in self.orders]
        self.others = [trade(x, mask, count) for x, mask in zip(sent, masks)]
        self.token = sent[0]

    def split(self):
        self.keep, self.sends = add_split(self.keep, self.others)

    def total(self):
        return [k.astype(F32) + o.astype(F32) for k, o in zip(self.keep, self.others)]


def add_split_kernel(pairs, *refs):
    ins, outs = refs[: 4 * pairs], refs[4 * pairs :]
    for k in range(pairs):
        keep, keep2, other, other2 = ins[4 * k : 4 * k + 4]
        out, send = outs[2 * k : 2 * k + 2]
        out[...] = (keep[...].astype(F32) + other[...].astype(F32)).reshape(out.shape)
        send[...] = (keep2[...].astype(F32) + other2[...].astype(F32)).astype(BF).reshape(send.shape)


def add_split(keeps, others):
    half = keeps[0].shape[0] // 2
    some = min(half, 2)
    ins, specs, outs, out_specs = [], [], [], []
    for keep, other in zip(keeps, others):
        tail = keep.shape[1:]
        low = pl.BlockSpec((some,) + tail, lambda i: (i, 0, 0))
        high = pl.BlockSpec((some,) + tail, lambda i: (i + half // some, 0, 0))
        ins += [keep, keep, other, other]
        specs += [low, high, low, high]
        outs += [jax.ShapeDtypeStruct((half,) + tail, F32), jax.ShapeDtypeStruct((half,) + tail, BF)]
        out_specs += [low, low]
    out = pl.pallas_call(
        lambda *refs: add_split_kernel(len(ins) // 4, *refs),
        grid=(half // some,),
        out_shape=tuple(outs),
        in_specs=specs,
        out_specs=tuple(out_specs),
        compiler_params=pltpu.CompilerParams(vmem_limit_bytes=56 << 20),
        cost_estimate=pl.CostEstimate(
            flops=1, bytes_accessed=1, transcendentals=0
        ),
    )(*ins)
    return list(out[::2]), list(out[1::2])


class Sum:
    def __init__(self, x, order):
        self.order, self.x = list(order), x

    def send(self):
        return self.x, self.order[0]

    def take(self, sent, other):
        self.order.pop(0)
        self.x = self.x + other


def exchange(count, *jobs, wait=()):
    sends = [job.send() for job in jobs]
    sent = lax.optimization_barrier(tuple(x for x, unused in sends) + tuple(wait))
    for job, x, (unused, mask) in zip(jobs, sent, sends):
        job.take(x, trade(x, mask, count))
    return sent[0]


def sync(jobs, *arrays):
    held = [job.x for job in jobs]
    held, arrays = lax.optimization_barrier((held, arrays))
    for job, x in zip(jobs, held):
        job.x = x
    return arrays


def share_seq(x, seq_count, count):
    return jnp.concatenate([x] + [trade(x, m, count) for m in range(1, seq_count)], axis=0)


def windows(width):
    size = width // H
    for pair in range(H // 2):
        base = (pair // 2) * 4 * size + (pair % 2) * 128
        yield pair, base, (2 * pair * size - base, (2 * pair + 1) * size - base, (2 * pair + 2) * size - base)


def stacked(rows, edges):
    column = lax.broadcasted_iota(jnp.int32, rows.shape, 1)
    first = (column >= edges[0]) & (column < edges[1])
    second = (column >= edges[1]) & (column < edges[2])
    zero = jnp.zeros_like(rows)
    return jnp.concatenate([jnp.where(first, rows, zero), jnp.where(second, rows, zero)], axis=0)


def unstacked(both, edges):
    count = both.shape[0] // 2
    column = lax.broadcasted_iota(jnp.int32, (count, both.shape[1]), 1)
    first = (column >= edges[0]) & (column < edges[1])
    second = (column >= edges[1]) & (column < edges[2])
    return jnp.where(first, both[:count], jnp.where(second, both[count:], 0.0))


def masked_scores(seen, queries, keys, media_rows):
    scores = dot(queries, keys, ((1,), (1,)))
    place = lax.broadcasted_iota(jnp.int32, scores.shape, 1)
    return jnp.where((place < seen) | (place >= media_rows), scores, -1e30)


def attend_kernel(media_rows, seen_ref, q_ref, kv_ref, out_ref):
    count, width = q_ref.shape
    seen = seen_ref[0]
    lane = lax.broadcasted_iota(jnp.int32, (count, 128), 1)
    stats = jnp.zeros((count, 128), F32)
    carry = None
    for pair, base, edges in windows(width):
        cols, value_cols = slice(base, base + 256), slice(width + base, width + base + 256)
        scores = masked_scores(seen, stacked(q_ref[:, cols], edges), kv_ref[:, cols], media_rows)
        top = jnp.max(scores, axis=1, keepdims=True)
        probs = jnp.exp(scores - top)
        total = jnp.sum(probs, axis=1, keepdims=True)
        mixed = unstacked(dot(probs.astype(BF), kv_ref[:, value_cols]) / total, edges)
        if pair % 2 == 0:
            out_ref[:, base : base + 128] = mixed[:, :128].astype(BF)
            carry = mixed[:, 128:]
        else:
            out_ref[:, base : base + 128] = (carry + mixed[:, :128]).astype(BF)
            out_ref[:, base + 128 : base + 256] = mixed[:, 128:].astype(BF)
        for k in range(2):
            rows = slice(k * count, (k + 1) * count)
            for n, value in enumerate((top, total)):
                value = value[rows]
                for term in range(3):
                    low = value.astype(BF).astype(F32)
                    stats = jnp.where(lane == (3 * n + term) * H + 2 * pair + k, low, stats)
                    value = value - low
    out_ref[:, width:] = stats.astype(BF)


def attend_back_kernel(media_rows, pieces, seen_ref, q_ref, kv_ref, *refs):
    dq_ref, dkv_ref = refs[pieces:]
    count, width = q_ref.shape
    seen = seen_ref[0]
    lane = lax.broadcasted_iota(jnp.int32, (count, 128), 1)
    packed = jnp.concatenate([ref[...] for ref in refs[:pieces]], axis=0)
    stats = packed[:, width:].astype(F32)

    def column(at):
        parts = []
        for k in range(2):
            here = (lane == at + k) | (lane == at + H + k) | (lane == at + 2 * H + k)
            parts.append(jnp.sum(jnp.where(here, stats, 0.0), axis=1, keepdims=True))
        return jnp.concatenate(parts, axis=0)

    carry = None
    for pair, base, edges in windows(width):
        cols = slice(base, base + 256)
        queries, grads = stacked(q_ref[:, cols], edges), stacked(packed[:, cols], edges)
        keys, values = kv_ref[:, cols], kv_ref[:, width + base : width + base + 256]
        scores = masked_scores(seen, queries, keys, media_rows)
        probs = jnp.exp(scores - column(2 * pair))
        prob_grad = dot(grads, values, ((1,), (1,)))
        score_grad = (probs * (prob_grad - column(3 * H + 2 * pair))).astype(BF)
        new = (
            (dq_ref, 0, dot(score_grad, keys)),
            (dkv_ref, 0, dot(score_grad, queries, ((0,), (0,)))),
            (dkv_ref, width, dot(probs.astype(BF), grads, ((0,), (0,)))),
        )
        new = [(ref, at + base, unstacked(x, edges) if ref is dq_ref else x) for ref, at, x in new]
        if pair % 2 == 0:
            for ref, at, x in new:
                ref[:, at : at + 128] = x[:, :128].astype(BF)
            carry = [x[:, 128:] for unused_ref, unused_at, x in new]
        else:
            for (ref, at, x), old in zip(new, carry):
                ref[:, at : at + 128] = (old + x[:, :128]).astype(BF)
                ref[:, at + 128 : at + 256] = x[:, 128:].astype(BF)


def lane_heads(shape, width, dim):
    lane = lax.broadcasted_iota(jnp.int32, shape, dim)
    column = lax.broadcasted_iota(jnp.int32, shape, 1 - dim)
    size = width // H
    first = (lane % H) * size
    return lane // H, column - first, (column >= first) & (column < first + size)


def three_terms(x):
    terms = []
    for unused in range(3):
        terms.append(x.astype(BF))
        x = x - terms[-1].astype(F32)
    return terms


def combine_kernel(pieces, whole, me_ref, *refs):
    parts, refs = refs[:pieces], refs[pieces:]
    latent_ref, gain_ref, bias_ref, *refs = refs
    *refs, wide_ref, low_ref, stat_ref, hidden_ref, ffn_ref, w_ref, sems = refs
    waits = whole.fetch(me_ref[0], refs, w_ref, sems)
    rows, width = latent_ref.shape
    group, unused, inside = lane_heads((128, width), width, 0)
    spread_top = jnp.where(inside & (group < 3), 1.0, 0.0).astype(BF)
    spread_total = jnp.where(inside & (group >= 3) & (group < 6), 1.0, 0.0).astype(BF)
    tops = [dot(ref[:, width:], spread_top) for ref in parts]
    top = tops[0]
    for other in tops[1:]:
        top = jnp.maximum(top, other)
    total = jnp.zeros((rows, width), F32)
    mixed = jnp.zeros((rows, width), F32)
    for ref, mine in zip(parts, tops):
        weight = jnp.exp(mine - top) * dot(ref[:, width:], spread_total)
        total += weight
        mixed += weight * ref[:, :width].astype(F32)
    mixed = mixed / total
    wide_ref[...] = mixed
    low = mixed.astype(BF)
    low_ref[...] = low
    group, offset, unused = lane_heads((width, 128), width, 1)
    stats = jnp.zeros((rows, 128), F32)
    for k, term in enumerate(three_terms(top + jnp.log(total))):
        pick = jnp.where((group == k) & (offset == 0), 1.0, 0.0).astype(BF)
        stats += dot(term, pick)
    stat_ref[...] = stats
    for wait in waits:
        wait.wait()
    hidden = latent_ref[...].astype(F32) + dot(low, w_ref[...])
    hidden_ref[...] = hidden
    ffn_ref[...] = layer_norm(hidden, gain_ref[...], bias_ref[...])[0].astype(BF)


def hidden_back_kernel(whole, me_ref, *refs):
    keep_ref, other_ref, hidden_ref, upstream_ref, wide_ref, stat_ref, gain_ref, *refs = refs
    *refs, hidden_grad_ref, low_ref, packed_ref, sums_ref, w_ref, sems = refs
    waits = whole.fetch(me_ref[0], refs, w_ref, sems)
    rows, width = hidden_ref.shape
    grad = keep_ref[0].astype(F32) + other_ref[0].astype(F32)
    gain = gain_ref[...]
    unused, unit, rstd = layer_norm(hidden_ref[...], gain, gain)
    norm_grad, gain_grad, bias_grad = layer_norm_back(grad, unit, rstd, gain)
    row = lax.broadcasted_iota(jnp.int32, (8, width), 0)
    sums_ref[...] = jnp.where(row == 0, gain_grad[None], jnp.where(row == 1, bias_grad[None], 0.0))
    hidden_grad = upstream_ref[...].astype(F32) + norm_grad
    hidden_grad_ref[...] = hidden_grad
    low = hidden_grad.astype(BF)
    low_ref[...] = low
    for wait in waits:
        wait.wait()
    mixture_grad = dot(low, w_ref[...], ((1,), (1,))).astype(BF)
    packed_ref[:, :width] = mixture_grad
    group, unused, inside = lane_heads((width, 128), width, 1)
    heads = jnp.where(inside & (group >= 3) & (group < 6), 1.0, 0.0).astype(BF)
    inner = jnp.zeros((rows, 128), F32)
    for term in three_terms(wide_ref[...] * mixture_grad.astype(F32)):
        inner += dot(term, heads)
    lane = lax.broadcasted_iota(jnp.int32, (rows, 128), 1) // H
    stats = stat_ref[...]
    for k, term in enumerate(three_terms(inner)):
        stats = jnp.where(lane == 3 + k, term.astype(F32), stats)
    packed_ref[:, width:] = stats.astype(BF)


def owner_of(place, order):
    return sum(mask for k, mask in enumerate(order) if (place >> k) % 2)


def place_of(owner, order):
    return sum(((owner // mask) % 2) << k for k, mask in enumerate(order))


class Stacks:
    def __init__(self, parts, orders):
        self.each = len(parts[0])
        self.arrays = [x for pieces in parts for x in pieces]
        self.orders = orders
        self.cols = sum(pieces[0].shape[2] for pieces in parts)
        widths = [pieces[0].shape[2] for pieces in parts]
        self.ends = [sum(widths[: k + 1]) for k in range(len(parts))]

    def fetch(self, me, refs, into, sems):
        at, waits = 0, []
        for k, order in enumerate(self.orders):
            pieces = refs[self.each * k : self.each * (k + 1)]
            some, block, cols = pieces[0].shape
            for place in range(self.each * some):
                owner = me ^ owner_of(place, order)
                to = into.at[pl.ds(pl.multiple_of(owner * block, 16), block), at : at + cols]
                source = pieces[place // some].at[place % some]
                pltpu.make_async_copy(source, to, sems.at[k]).start()
            part = into.at[:, at : at + cols]
            waits.append(pltpu.make_async_copy(part, part, sems.at[k]))
            at += cols
        return waits


class Plain:
    def __init__(self, x):
        self.arrays, self.orders = [x], (None,)
        self.cols = x.shape[1]
        self.ends = [self.cols]

    def fetch(self, me, refs, into, sems):
        copy = pltpu.make_async_copy(refs[0], into, sems.at[0])
        copy.start()
        return [copy]


def halves_kernel(me_ref, s_ref, mine_ref, other_ref):
    block = 48
    for parity in range(2):

        @pl.when(me_ref[0] % 2 == parity)
        def _():
            for out_ref, which in ((mine_ref, parity), (other_ref, 1 - parity)):
                for n in range(out_ref.shape[1] // block):
                    at = (2 * n + which) * block
                    out_ref[:, n * block : (n + 1) * block] = s_ref[:, at : at + block]


def order_kernel(whole, me_ref, *refs):
    *refs, out_ref, sems = refs
    for wait in whole.fetch(me_ref[0], refs, out_ref, sems):
        wait.wait()


def project_kernel(whole, me_ref, s_ref, *refs):
    *refs, out_ref, w_ref, sems = refs
    at = 0
    for wait, end in zip(whole.fetch(me_ref[0], refs, w_ref, sems), whole.ends):
        wait.wait()
        out_ref[:, at:end] = dot(s_ref[...], w_ref[:, at:end]).astype(BF)
        at = end


def gelu_parts(x):
    c = 0.7978845608028654
    t = jnp.tanh(c * (x + 0.044715 * (x * x * x)))
    slope = 0.5 * (1.0 + t) + 0.5 * x * (1.0 - t * t) * (c * (1.0 + 3 * 0.044715 * (x * x)))
    return 0.5 * x * (1.0 + t), slope


def ffn_kernel(
    order,
    me_ref,
    mine_ref,
    other_ref,
    up_ref,
    down_ref,
    all_ref,
    keep_ref,
    send_ref,
    active_ref,
    pre_ref,
    rows_ref,
    grad_rows_ref,
    sem,
):
    some, each, width = mine_ref.shape
    for place in range(2 * some):
        owner = me_ref[0] ^ owner_of(place, order)
        pltpu.make_async_copy(
            all_ref.at[owner, :, width : 2 * width],
            grad_rows_ref.at[place * each : (place + 1) * each],
            sem,
        ).start()
    rows_ref[: some * each, :] = mine_ref[...].reshape(some * each, width)
    rows_ref[some * each :, :] = other_ref[...].reshape(some * each, width)
    active, slope = gelu_parts(dot(rows_ref[...], up_ref[...]))
    active_ref[...] = active.astype(BF)
    pltpu.make_async_copy(grad_rows_ref, grad_rows_ref, sem).wait()
    pre_grad = (dot(grad_rows_ref[...], down_ref[...], ((1,), (1,))) * slope).astype(BF)
    pre_ref[...] = pre_grad
    total = dot(pre_grad, up_ref[...], ((1,), (1,)))
    keep_ref[...] = total[: some * each].reshape(keep_ref.shape)
    send_ref[...] = total[some * each :].astype(BF).reshape(send_ref.shape)


def ffn_sums_kernel(
    rows_ref,
    grad_rows_ref,
    active_ref,
    pre_ref,
    down_ref,
    down_keep_ref,
    down_send_ref,
    up_keep_ref,
    up_send_ref,
    keep_ref,
    send_ref,
):
    first = ((0,), (0,))
    units = down_keep_ref.shape[0]
    down = dot(active_ref[...], grad_rows_ref[...], first)
    down_keep_ref[...] = down[:units]
    down_send_ref[...] = down[units:].astype(BF)
    up = dot(rows_ref[...], pre_ref[...], first)
    up_keep_ref[...] = up[:, :units].astype(BF)
    up_send_ref[...] = up[:, units:].astype(BF)
    out = dot(active_ref[...], down_ref[...])
    half = out.shape[0] // 2
    keep_ref[...] = out[:half].reshape(keep_ref.shape)
    send_ref[...] = out[half:].astype(BF).reshape(send_ref.shape)


def source_kernel(whole, me_ref, g_ref, media_ref, time_ref, gain_ref, *refs):
    *refs, media_grad_ref, latent_ref, sums_ref, acc_ref, w_ref, sems = refs
    at = 0
    for wait, end in zip(whole.fetch(me_ref[0], refs, w_ref, sems), whole.ends):
        wait.wait()
        new = dot(g_ref[:, at:end], w_ref[:, at:end], ((1,), (1,)))
        acc_ref[...] = acc_ref[...] + new if at else new
        at = end
    media_rows, width = media_ref.shape
    gain = gain_ref[...]
    rows = [jnp.zeros((1, width), F32), jnp.zeros((1, width), F32)]
    for frame in range(media_rows // PATCH):
        here = slice(frame * PATCH, (frame + 1) * PATCH)
        shifted = media_ref[here, :].astype(F32) + time_ref[frame : frame + 1, :]
        unused, unit, rstd = layer_norm(shifted, gain, gain)
        grad = acc_ref[here, :]
        shifted_grad, gain_grad, bias_grad = layer_norm_back(grad, unit, rstd, gain)
        media_grad_ref[here, :] = shifted_grad.astype(BF)
        rows[0] += gain_grad[None]
        rows[1] += bias_grad[None]
        rows.append(jnp.sum(shifted_grad, axis=0, keepdims=True))
    at = lax.broadcasted_iota(jnp.int32, sums_ref.shape, 0)
    sums = jnp.zeros(sums_ref.shape, F32)
    for k, row in enumerate(rows):
        sums = jnp.where(at == k, row, sums)
    sums_ref[...] = sums
    latent_ref[...] = acc_ref[media_rows:, :]


def latent_kernel(pieces, scaling, *refs):
    parts, refs = refs[:pieces], refs[pieces:]
    source_ref, latent_ref, gain_ref, hidden_grad_ref, out_ref, sums_ref = refs
    gain = gain_ref[...]
    width = gain.shape[1]
    query_side = sum(ref[:, :width].astype(F32) for ref in parts)
    grad = source_ref[...] + query_side * scaling
    unused, unit, rstd = layer_norm(latent_ref[...].astype(F32), gain, gain)
    latent_grad, gain_grad, bias_grad = layer_norm_back(grad, unit, rstd, gain)
    out_ref[...] = (hidden_grad_ref[...] + latent_grad).astype(BF)
    at = lax.broadcasted_iota(jnp.int32, sums_ref.shape, 0)
    sums_ref[...] = jnp.where(
        at == 0, gain_grad[None], jnp.where(at == 1, bias_grad[None], 0.0)
    )


def sums_kernel(orders, me_ref, s_ref, s2_ref, g_ref, g2_ref, *refs):
    *out_refs, s_held, g_held, held, sems = refs
    me = me_ref[0] - me_ref[0] % 2
    half, block, unused = out_refs[0].shape
    widths = [ref.shape[2] for ref in out_refs[::2]]
    starts = [sum(widths[:k]) for k in range(len(widths))]
    rows = s_ref.shape[0]
    for k, ref in enumerate((s_ref, s2_ref)):
        pltpu.make_async_copy(ref, s_held.at[k * rows : (k + 1) * rows], sems.at[0]).start()
    for part in range(len(orders)):
        columns = slice(starts[part], starts[part] + widths[part])
        for k, ref in enumerate((g_ref, g2_ref)):
            to = g_held.at[k * rows : (k + 1) * rows, columns]
            pltpu.make_async_copy(ref.at[:, columns], to, sems.at[1 + part]).start()
    pltpu.make_async_copy(s_held, s_held, sems.at[0]).wait()
    some = held.shape[0]
    for part, order in enumerate(orders):
        columns = slice(starts[part], starts[part] + widths[part])
        here = g_held.at[:, columns]
        pltpu.make_async_copy(here, here, sems.at[1 + part]).wait()
        first = (me // order[-1]) % 2
        for start in range(0, 2 * half, some):
            full = dot(s_held[:, start * block : (start + some) * block], here[...], ((0,), (0,)))
            cols = widths[part]
            held[:, :, :cols] = full.astype(BF).reshape(some, block, cols)
            for bit in range(2):

                @pl.when(first == bit)
                def _(bit=bit, start=start, part=part, order=order, cols=cols):
                    for n in range(some):
                        owner = 2 * (start + n)
                        place = place_of(owner ^ me, order) % half
                        send = (owner // order[-1]) % 2 != bit
                        out_refs[2 * part + send][place] = held[n, :, :cols]


SCALAR = pl.BlockSpec(memory_space=pltpu.SMEM)
FAR = pl.BlockSpec(memory_space=pl.ANY)


def call(kernel, inputs, outputs, flops, specs=(), far_outputs=False, scratch=()):
    specs = dict(specs)

    def whole(x):
        return pl.BlockSpec(x.shape, lambda i, nd=len(x.shape): (0,) * nd)

    nbytes = sum(x.size * x.dtype.itemsize for x in inputs)
    nbytes += sum(x.size * x.dtype.itemsize for x in outputs)
    return pl.pallas_call(
        kernel,
        grid=(1,),
        out_shape=tuple(outputs),
        in_specs=[specs.get(n, whole(x)) for n, x in enumerate(inputs)],
        out_specs=tuple(FAR if far_outputs else whole(x) for x in outputs),
        scratch_shapes=list(scratch),
        compiler_params=pltpu.CompilerParams(vmem_limit_bytes=56 << 20),
        cost_estimate=pl.CostEstimate(flops=flops // 1000, bytes_accessed=nbytes // 1000, transcendentals=0),
    )(*inputs)


def shards(
    media,
    latents,
    frames,
    time_embed,
    media_gain,
    media_bias,
    latent_gain,
    latent_bias,
    ffn_gain,
    ffn_bias,
    w_query,
    w_key,
    w_value,
    w_out,
    w_up,
    w_down,
    grad_out,
):
    item_count, seq_count = lax.axis_size("items"), lax.axis_size("seq")
    count = item_count * seq_count
    seq_index = lax.axis_index("seq")
    me = lax.axis_index("items") * seq_count + seq_index
    unused_items, media_rows, width = media.shape
    latent_rows = latents.shape[1]
    head_size = width // H
    frames_here = media_rows // PATCH
    scaling = head_size ** (-0.5)

    bits = [1 << k for k in reversed(range(30))]
    item_bits = [m for m in bits if seq_count <= m < count]
    seq_bits = [m for m in bits if m < seq_count]
    head, (fold, near), side, tail = item_bits[:-2], item_bits[-2:], seq_bits[0], seq_bits[1:]
    orders = (
        head + [fold, near, side] + tail,
        head + [side, fold, near] + tail,
        head + [near, side, fold] + tail,
    )
    ffn_order = item_bits + seq_bits[:-1]
    core = seq_bits[-1]
    block = width // count
    regular = block % 16 == 0

    def share(x):
        return jax.ShapeDtypeStruct(x, BF)

    latent_in = latents[0].astype(F32)
    latent_normed, latent_unit, latent_rstd = layer_norm(latent_in, latent_gain, latent_bias)
    latent_normed = latent_normed.astype(BF)
    time_rows = lax.dynamic_slice_in_dim(time_embed, seq_index * frames_here, frames_here, 0)
    shifted = (
        media[0].astype(F32).reshape(frames_here, PATCH, width) + time_rows[:, None, :]
    ).reshape(media_rows, width)
    media_normed, media_unit, media_rstd = layer_norm(shifted, media_gain, media_bias)
    sources = jnp.concatenate([media_normed.astype(BF), latent_normed], axis=0)

    def in_columns(x):
        return x.reshape(x.shape[0], count, -1).transpose(1, 0, 2)

    def spread(x):
        x = lax.all_to_all(x, AXES, split_axis=0, concat_axis=0, tiled=True)
        return x.reshape(-1, x.shape[2])

    cols_here = width // seq_count

    def seq_blocks(x, axis):
        return jnp.concatenate(
            [
                lax.dynamic_index_in_dim(x, seq_index ^ t, 0, keepdims=False)
                for t in range(seq_count)
            ],
            axis=axis,
        )

    def columns_of(x, m):
        return lax.dynamic_slice_in_dim(x, (seq_index ^ m) * cols_here, cols_here, 1)

    def reordered(x, m):
        blocks = x.reshape(seq_count, latent_rows, x.shape[1])
        return jnp.concatenate([blocks[t ^ m] for t in range(seq_count)], axis=0)

    parts = len(orders)
    units = w_down.shape[0]
    out_orders = (head + [near, fold, side] + tail, head + [near, side, fold] + tail)
    shares = (width * 5 // 6, width * 5 // 6, width // 3)
    def query_pieces(x):
        pieces = [columns_of(x, m) for m in range(seq_count)]
        return [pieces[0]] + [trade(pieces[m], m, count) for m in range(1, seq_count)]

    if regular:
        first = GatherRel(jnp.concatenate([w_key, w_value], axis=1)[None], head)
        second = GatherRel(w_out[None], head + [near])

        def split(x, shares, orders, done):
            return [
                GatherApart(x[..., sum(shares[:k]) : sum(shares[: k + 1])], order[done:])
                for k, order in enumerate(orders)
            ]

        while first.order:
            started = exchange(count, first)
        latent_item = share_seq(after(latent_normed, started), seq_count, count)
        pieces = query_pieces(after(w_query, started))
        half_mine, half_other = call(
            halves_kernel,
            (me[None], sources),
            (share((sources.shape[0], width // 2)),) * 2,
            0,
            specs={0: SCALAR},
        )
        rows_mine = jnp.concatenate([latent_normed, grad_out[0]], axis=1)
        sources, latent_item, half_mine, half_other, rows_mine, *pieces = sync(
            [first], sources, latent_item, half_mine, half_other, rows_mine, *pieces
        )
        query_cols = Gather(seq_blocks(jnp.stack(pieces), 0), [near] + head + [fold], me)
        first = split(first.x, shares, orders, len(head))
        exchange(count, *first, second, query_cols)
        sync([*first, second, query_cols])
        exchange(count, *first, second, query_cols)
        up_in, rows_mine = sync([*first, second, query_cols], w_up, rows_mine)
        rows_all = lax.all_gather(rows_mine, AXES, axis=0)
        second = split(second.x, (width // 2, width // 2), out_orders, len(head) + 1)
        exchange(count, *first, query_cols)
        sources, latent_item, half_other, up_in = sync(
            [*first, query_cols], sources, latent_item, half_other, in_columns(up_in)
        )
        for job in first:
            job.last(count)
    else:
        up_mine = spread(in_columns(w_up))
        rows_all = lax.all_gather(
            jnp.concatenate([latent_normed, grad_out[0]], axis=1), AXES, axis=0
        )
        latent_item = share_seq(latent_normed, seq_count, count)
        query_cols = Gather(seq_blocks(jnp.stack(query_pieces(w_query)), 0), item_bits, me)
        while query_cols.order:
            exchange(count, query_cols)
        both = lax.all_gather(jnp.concatenate([w_key, w_value], 1), AXES, axis=0, tiled=True)
        key_value = Plain(both)
        out_full = Plain(lax.all_gather(w_out, AXES, axis=0, tiled=True))

    def with_weights(kernel, inputs, whole, outputs, flops, keep=True, scratch=()):
        inputs = [me[None]] + list(inputs)
        specs = {0: SCALAR}
        for n in range(len(whole.arrays)):
            specs[len(inputs) + n] = FAR
        scratch = list(scratch) + ([pltpu.VMEM((width, whole.cols), BF)] if keep else [])
        return call(
            lambda *refs: kernel(whole, *refs),
            (*inputs, *whole.arrays),
            outputs,
            flops,
            specs=specs,
            scratch=scratch + [pltpu.SemaphoreType.DMA((len(whole.orders),))],
        )

    query_slice = query_cols.rows().reshape(width, cols_here)
    query_mine = (dot(latent_item, query_slice) * scaling).astype(BF)
    sends = [reordered(query_mine, m) for m in range(1, seq_count)]
    if regular:
        up_mine = spread(up_in)
        query_mine, *sends = sync([*first, *second], query_mine, *sends)
        key_value = Stacks([job.x for job in first], orders)
        exchange(count, *second)
    pieces = [query_mine] + [trade(x, m + 1, count) for m, x in enumerate(sends)]
    source_count = sources.shape[0]
    keys = with_weights(
        project_kernel,
        (sources,),
        key_value,
        (share((source_count, 2 * width)),),
        4 * source_count * width * width,
    )[0]
    if regular:
        keys, half_other, up_mine, *pieces = sync(second, keys, half_other, up_mine, *pieces)
        half_other = trade(half_other, 1, count)
        exchange(count, *second)
    queries = seq_blocks(jnp.stack(pieces), 1)
    seen = jnp.clip((frames - seq_index * frames_here) * PATCH, 0, media_rows).astype(jnp.int32)
    all_rows = queries.shape[0]
    pair_flops = 2 * H // 2 * 2 * all_rows * 256 * sources.shape[0]
    mixed = call(
        lambda *refs: attend_kernel(media_rows, *refs),
        (seen, queries, keys),
        (share((all_rows, width + 128)),),
        2 * pair_flops,
        specs={0: SCALAR},
    )[0]

    def own_parts(x):
        blocks = x.reshape(seq_count, latent_rows, x.shape[1])
        return [blocks[0]] + [trade(blocks[m], m, count) for m in range(1, seq_count)]


    mixed_parts = own_parts(mixed)
    if regular:
        mixed_parts = sync(second, *mixed_parts)
        for job in second:
            job.last(count, join=True)
        sync(second)
        out_full = Stacks([job.x for job in second], out_orders)
    up_other, down_other = trade(up_mine, core, count), trade(w_down, core, count)
    up_pair = jnp.concatenate([up_mine, up_other], axis=1)
    down_pair = jnp.concatenate([w_down, down_other], axis=0)
    rows_wide = jax.ShapeDtypeStruct((latent_rows, width), F32)
    rows_low = jax.ShapeDtypeStruct((latent_rows, width), BF)
    mixture_wide, mixture, log_total, hidden, ffn_in = with_weights(
        lambda *refs: combine_kernel(seq_count, *refs),
        (*mixed_parts, latents[0], ffn_gain[None], ffn_bias[None]),
        out_full,
        (
            rows_wide,
            rows_low,
            jax.ShapeDtypeStruct((latent_rows, 128), F32),
            rows_wide,
            rows_low,
        ),
        2 * latent_rows * width * width,
    )
    ffn_rows = GatherRel(ffn_in[None], ffn_order)
    while len(ffn_rows.order) > 1:
        exchange(count, ffn_rows)
    mine = ffn_rows.x
    other = trade(mine, ffn_order[-1], count)
    some = mine.shape[0]
    all_ffn = 2 * some * latent_rows
    units_low = share((all_ffn, 2 * units))
    halves = (jax.ShapeDtypeStruct(mine.shape, F32), share(mine.shape))
    ffn_flops = 2 * all_ffn * 2 * units * width
    keep, send, active, pre, ffn_all, grad_all = call(
        lambda *refs: ffn_kernel(ffn_order, *refs),
        (me[None], mine, other, up_pair, down_pair, rows_all),
        (*halves, units_low, units_low, *(share((all_ffn, width)),) * 2),
        3 * ffn_flops,
        specs={0: SCALAR, 5: FAR},
        scratch=(pltpu.SemaphoreType.DMA(()),),
    )
    back = Halves([keep], [send], [ffn_order])
    back.step(count)
    down_keep, down_send, up_keep, up_send, keep, send = call(
        ffn_sums_kernel,
        (ffn_all, after(grad_all, back.token), active, pre, down_pair),
        (
            jax.ShapeDtypeStruct((units, width), F32),
            share((units, width)),
            share((width, units)),
            share((width, units)),
            *halves,
        ),
        3 * ffn_flops,
    )
    result = Halves([keep], [send], [ffn_order])
    wait = (down_send,)
    while back.orders[0]:
        back.split()
        back.step(count, wait)
        if not wait:
            result.split()
        result.step(count, (back.token,))
        wait = ()
        if back.orders[0]:
            back.others, result.others = lax.optimization_barrier((back.others, result.others))

    hidden_grad, attended_low, packed, ffn_sums = with_weights(
        hidden_back_kernel,
        (
            back.keep[0],
            back.others[0],
            hidden,
            grad_out[0],
            mixture_wide,
            log_total,
            ffn_gain[None],
        ),
        out_full,
        (
            rows_wide,
            rows_low,
            share((latent_rows, width + 128)),
            jax.ShapeDtypeStruct((8, width), F32),
        ),
        2 * latent_rows * width * width,
    )
    down_send, up_send = sync([], down_send, up_send, packed)[:2]
    down_other, up_other = trade(down_send, core, count), trade(up_send, core, count)
    pieces = [packed] + [trade(packed, m, count) for m in range(1, seq_count)]
    result.split()
    result.step(count, (packed,))
    query_part, row_grad = call(
        lambda *refs: attend_back_kernel(media_rows, seq_count, *refs),
        (seen, queries, keys, *pieces),
        (share((all_rows, width)), share(keys.shape)),
        5 * pair_flops,
        specs={0: SCALAR},
    )
    sends = [reordered(columns_of(query_part, m), m) for m in range(seq_count)]
    row_send, result.others, *sends = lax.optimization_barrier((row_grad, result.others, *sends))
    row_other = trade(row_send, 1, count)
    pieces = [sends[0]] + [trade(sends[m], m, count) for m in range(1, seq_count)]
    row_grad, row_other, *pieces = sync([], row_send, row_other, *pieces)
    query_cols_grad = sum(x.astype(F32) for x in pieces).astype(BF)
    query_side = dot(query_cols_grad, query_slice, ((1,), (1,))).astype(BF)
    query_side = own_parts(jnp.concatenate([query_side, query_cols_grad], axis=1))

    if regular:
        outs = call(
            lambda *refs: sums_kernel([order[:-1] for order in orders], *refs),
            (me[None], half_mine, half_other, row_grad, row_other),
            tuple(share((count // 4, block, cols)) for cols in shares for unused in range(2)),
            4 * width * width * source_count,
            specs={0: SCALAR, 1: FAR, 2: FAR, 3: FAR, 4: FAR},
            scratch=(
                pltpu.VMEM((2 * source_count, width // 2), BF),
                pltpu.VMEM((2 * source_count, 2 * width), BF),
                pltpu.VMEM((8, block, max(shares)), BF),
                pltpu.SemaphoreType.DMA((1 + parts,)),
            ),
        )
        weights = Halves(outs[::2], outs[1::2], [order[:-1] for order in orders])
        weights.step(count, (*query_side[1:], *result.others))
        started = weights.token
    else:
        full = dot(sources, row_grad, ((0,), (0,))).astype(BF)
        full = lax.psum_scatter(full, AXES, scatter_dimension=0, tiled=True).astype(F32)
        started = row_other
    result.others, up_keep, up_other = sync([], result.others, up_keep, up_other, started)[:-1]
    up_blocks = (up_keep.astype(F32) + up_other.astype(F32)).astype(BF)
    up_blocks = up_blocks.reshape(count, -1, units)
    up_blocks = lax.all_to_all(up_blocks, AXES, split_axis=0, concat_axis=0, tiled=True)
    query_rows = seq_blocks(jnp.stack([x[:, width:] for x in query_side]), 1)
    rows = lax.all_gather(
        jnp.concatenate([attended_low, query_rows, mixture], axis=1), AXES, axis=0, tiled=True
    )

    media_grad, latent_source, media_sums = with_weights(
        source_kernel,
        (after(row_grad, started), media[0], time_rows, media_gain[None]),
        key_value,
        (
            share((media_rows, width)),
            jax.ShapeDtypeStruct((latent_rows, width), F32),
            jax.ShapeDtypeStruct((8, width), F32),
        ),
        4 * source_count * width * width,
        scratch=[pltpu.VMEM((source_count, width), F32)],
    )
    latents_grad, latent_sums = call(
        lambda *refs: latent_kernel(seq_count, scaling, *refs),
        (*query_side, latent_source, latents[0], latent_gain[None], hidden_grad),
        (rows_low, jax.ShapeDtypeStruct((8, width), F32)),
        2 * latent_rows * width * width,
    )
    time_local = lax.dynamic_update_slice_in_dim(
        jnp.zeros((FRAMES, width), F32),
        media_sums[2 : 2 + frames_here],
        seq_index * frames_here,
        0,
    )
    sums = Sum(
        jnp.concatenate(
            [
                time_local,
                media_sums[:2],
                latent_sums[:2],
                ffn_sums[:2],
                jnp.zeros((2, width), F32),
            ],
            axis=0,
        ),
        [side, near, fold],
    )
    if regular:
        while weights.orders[0]:
            weights.split()
            weights.step(count)
            if len(weights.orders[0]) == 1:
                down_other, up_blocks = after(down_other, weights.token), after(up_blocks, weights.token)
            if result.orders[0]:
                result.split()
                result.step(count, (weights.token,))
            if sums.order:
                exchange(count, sums, wait=(weights.token,))
        full = jnp.concatenate([x[0] for x in weights.total()], axis=1)
    while result.orders[0]:
        result.split()
        result.step(count)
    down_grad = down_keep + down_other.astype(F32)
    up_grad = up_blocks.transpose(1, 0, 2).reshape(-1, count * units).astype(F32)
    latents_out = hidden + result.total()[0][0]

    def my_columns(x):
        return lax.dynamic_slice_in_dim(x, me * block, block, 1)

    out_grad = dot(my_columns(rows[:, 2 * width :]), rows[:, :width], ((0,), (0,)))
    latent_all = my_columns(rows_all.reshape(-1, 2 * width))
    query_grad = dot(latent_all, rows[:, width : 2 * width], ((0,), (0,))) * scaling
    while sums.order:
        exchange(count, sums)
    sums, others = sums.x, [0]
    for bit in head + tail:
        others += [mask ^ bit for mask in others]
    sums_parts = [trade(sums, mask, count) for mask in others[1:]]
    out_grad, query_grad, *sums_parts = sync([], out_grad, query_grad, *sums_parts)
    sums_parts = [sums, *sums_parts]
    while len(sums_parts) > 1:
        sums_parts = [a + b for a, b in zip(sums_parts[::2], sums_parts[1::2])]
    sums = sums_parts[0]
    return (
        latents_out.astype(BF)[None],
        latents_grad[None],
        media_grad[None],
        sums[:FRAMES],
        sums[FRAMES],
        sums[FRAMES + 1],
        sums[FRAMES + 2],
        sums[FRAMES + 3],
        sums[FRAMES + 4],
        sums[FRAMES + 5],
        query_grad,
        full[:, :width],
        full[:, width:],
        out_grad,
        up_grad,
        down_grad,
    )


def solution(mesh):
    rows, split = P("items", "seq", None), P(AXES, None)
    return jax.shard_map(
        shards,
        mesh=mesh,
        in_specs=(rows, rows, P("items")) + (P(),) * 7 + (split,) * 6 + (rows,),
        out_specs=(rows,) * 3 + (P(),) * 7 + (split,) * 6,
        check_vma=False,
    )
```

```python
import jax
import jax.numpy as jnp
from jax import lax
from jax.experimental import pallas as pl
from jax.experimental.pallas import tpu as pltpu
from jax.sharding import PartitionSpec as P

H = 16
FRAMES = 8
PATCH = 256
AXES = ("items", "seq")
BF = jnp.bfloat16
F32 = jnp.float32


def layer_norm(values, gain, bias):
    center = jnp.mean(values, axis=-1, keepdims=True)
    spread = jnp.mean(jnp.square(values - center), axis=-1, keepdims=True)
    rstd = lax.rsqrt(spread + 1e-05)
    unit = (values - center) * rstd
    return unit * gain + bias, unit, rstd


def layer_norm_back(grad, unit, rstd, gain):
    scaled = grad * gain
    inner = scaled - jnp.mean(scaled, axis=-1, keepdims=True)
    inner = inner - unit * jnp.mean(scaled * unit, axis=-1, keepdims=True)
    return inner * rstd, jnp.sum(grad * unit, axis=0), jnp.sum(grad, axis=0)


def dot(a, b, dims=((1,), (0,))):
    return lax.dot_general(a, b, (dims, ((), ())), preferred_element_type=F32)


def trade(x, mask, count):
    return lax.ppermute(x, AXES, [(i, i ^ mask) for i in range(count)])


def after(x, *others):
    return lax.optimization_barrier((x,) + others)[0]


class Gather:
    def __init__(self, x, order, me):
        self.x, self.order, self.me, self.done = x, list(order), me, []

    def rows(self):
        if isinstance(self.x, (list, tuple)):
            mine, other = self.x
            axis = sum(m > self.done[-1] for m in self.done)
            mine, other = jnp.expand_dims(mine, axis), jnp.expand_dims(other, axis)
            self.x = jnp.where(
                (self.me & self.done[-1]) != 0,
                jnp.concatenate([other, mine], axis),
                jnp.concatenate([mine, other], axis),
            )
        return self.x

    def send(self):
        return self.rows(), self.order[0]

    def take(self, sent, other):
        self.done.append(self.order.pop(0))
        self.x = (sent, other)


class GatherRel:
    def __init__(self, x, order):
        self.order, self.x = list(order), x

    def send(self):
        return self.x, self.order[0]

    def take(self, sent, other):
        self.order.pop(0)
        self.x = jnp.concatenate([sent, other], axis=0)


class GatherApart(GatherRel):
    def take(self, sent, other):
        if len(self.order) > 2:
            GatherRel.take(self, sent, other)
        else:
            self.order.pop(0)
            self.x = (sent, other)

    def last(self, count, join=False):
        mask = self.order.pop(0)
        pieces = (jnp.concatenate(self.x, axis=0),) if join else tuple(self.x)
        self.x = [*pieces, *[trade(x, mask, count) for x in pieces]]


class Halves:
    def __init__(self, keep, send, orders):
        self.orders, self.keep, self.sends = [list(order) for order in orders], keep, send

    def step(self, count, wait=()):
        sent = lax.optimization_barrier(tuple(self.sends) + tuple(wait))
        masks = [order.pop() for order in self.orders]
        self.others = [trade(x, mask, count) for x, mask in zip(sent, masks)]
        self.token = sent[0]

    def split(self):
        self.keep, self.sends = add_split(self.keep, self.others)

    def total(self):
        return [k.astype(F32) + o.astype(F32) for k, o in zip(self.keep, self.others)]


def add_split_kernel(pairs, *refs):
    ins, outs = refs[: 4 * pairs], refs[4 * pairs :]
    for k in range(pairs):
        keep, keep2, other, other2 = ins[4 * k : 4 * k + 4]
        out, send = outs[2 * k : 2 * k + 2]
        total = keep[...].astype(F32) + other[...].astype(F32)
        out[...] = total.astype(out.dtype).reshape(out.shape)
        send[...] = (keep2[...].astype(F32) + other2[...].astype(F32)).astype(BF).reshape(send.shape)


def add_split(keeps, others):
    half = keeps[0].shape[0] // 2
    some = min(half, 2)
    ins, specs, outs, out_specs = [], [], [], []
    for keep, other in zip(keeps, others):
        tail = keep.shape[1:]
        low = pl.BlockSpec((some,) + tail, lambda i: (i, 0, 0))
        high = pl.BlockSpec((some,) + tail, lambda i: (i + half // some, 0, 0))
        ins += [keep, keep, other, other]
        specs += [low, high, low, high]
        outs += [
            jax.ShapeDtypeStruct((half,) + tail, keep.dtype),
            jax.ShapeDtypeStruct((half,) + tail, BF),
        ]
        out_specs += [low, low]
    out = pl.pallas_call(
        lambda *refs: add_split_kernel(len(ins) // 4, *refs),
        grid=(half // some,),
        out_shape=tuple(outs),
        in_specs=specs,
        out_specs=tuple(out_specs),
        compiler_params=pltpu.CompilerParams(vmem_limit_bytes=56 << 20),
        cost_estimate=pl.CostEstimate(
            flops=1, bytes_accessed=1, transcendentals=0
        ),
    )(*ins)
    return list(out[::2]), list(out[1::2])


class Sum:
    def __init__(self, x, order):
        self.order, self.x = list(order), x

    def send(self):
        return self.x, self.order[0]

    def take(self, sent, other):
        self.order.pop(0)
        self.x = self.x + other


def exchange(count, *jobs, wait=()):
    sends = [job.send() for job in jobs]
    sent = lax.optimization_barrier(tuple(x for x, unused in sends) + tuple(wait))
    for job, x, (unused, mask) in zip(jobs, sent, sends):
        job.take(x, trade(x, mask, count))
    return sent[0]


def sync(jobs, *arrays):
    held = [job.x for job in jobs]
    held, arrays = lax.optimization_barrier((held, arrays))
    for job, x in zip(jobs, held):
        job.x = x
    return arrays


def share_seq(x, seq_count, count):
    return jnp.concatenate([x] + [trade(x, m, count) for m in range(1, seq_count)], axis=0)


def windows(width):
    size = width // H
    for pair in range(H // 2):
        base = (pair // 2) * 4 * size + (pair % 2) * 128
        yield pair, base, (2 * pair * size - base, (2 * pair + 1) * size - base, (2 * pair + 2) * size - base)


def stacked(rows, edges):
    column = lax.broadcasted_iota(jnp.int32, rows.shape, 1)
    first = (column >= edges[0]) & (column < edges[1])
    second = (column >= edges[1]) & (column < edges[2])
    zero = jnp.zeros_like(rows)
    return jnp.concatenate([jnp.where(first, rows, zero), jnp.where(second, rows, zero)], axis=0)


def unstacked(both, edges):
    count = both.shape[0] // 2
    column = lax.broadcasted_iota(jnp.int32, (count, both.shape[1]), 1)
    first = (column >= edges[0]) & (column < edges[1])
    second = (column >= edges[1]) & (column < edges[2])
    return jnp.where(first, both[:count], jnp.where(second, both[count:], 0.0))


def masked_scores(seen, queries, keys, media_rows):
    scores = dot(queries, keys, ((1,), (1,)))
    place = lax.broadcasted_iota(jnp.int32, scores.shape, 1)
    return jnp.where((place < seen) | (place >= media_rows), scores, -1e30)


def attend_kernel(media_rows, seen_ref, q_ref, kv_ref, out_ref):
    count, width = q_ref.shape
    seen = seen_ref[0]
    lane = lax.broadcasted_iota(jnp.int32, (count, 128), 1)
    stats = jnp.zeros((count, 128), F32)
    carry = None
    for pair, base, edges in windows(width):
        cols, value_cols = slice(base, base + 256), slice(width + base, width + base + 256)
        scores = masked_scores(seen, stacked(q_ref[:, cols], edges), kv_ref[:, cols], media_rows)
        top = jnp.max(scores, axis=1, keepdims=True)
        probs = jnp.exp(scores - top)
        total = jnp.sum(probs, axis=1, keepdims=True)
        mixed = unstacked(dot(probs.astype(BF), kv_ref[:, value_cols]) / total, edges)
        if pair % 2 == 0:
            out_ref[:, base : base + 128] = mixed[:, :128].astype(BF)
            carry = mixed[:, 128:]
        else:
            out_ref[:, base : base + 128] = (carry + mixed[:, :128]).astype(BF)
            out_ref[:, base + 128 : base + 256] = mixed[:, 128:].astype(BF)
        for k in range(2):
            rows = slice(k * count, (k + 1) * count)
            for n, value in enumerate((top, total)):
                value = value[rows]
                for term in range(3):
                    low = value.astype(BF).astype(F32)
                    stats = jnp.where(lane == (3 * n + term) * H + 2 * pair + k, low, stats)
                    value = value - low
    out_ref[:, width:] = stats.astype(BF)


def attend_back_kernel(media_rows, pieces, seen_ref, q_ref, kv_ref, *refs):
    dq_ref, dkv_ref = refs[pieces:]
    count, width = q_ref.shape
    seen = seen_ref[0]
    lane = lax.broadcasted_iota(jnp.int32, (count, 128), 1)
    packed = jnp.concatenate([ref[...] for ref in refs[:pieces]], axis=0)
    stats = packed[:, width:].astype(F32)

    def column(at):
        parts = []
        for k in range(2):
            here = (lane == at + k) | (lane == at + H + k) | (lane == at + 2 * H + k)
            parts.append(jnp.sum(jnp.where(here, stats, 0.0), axis=1, keepdims=True))
        return jnp.concatenate(parts, axis=0)

    carry = None
    for pair, base, edges in windows(width):
        cols = slice(base, base + 256)
        queries, grads = stacked(q_ref[:, cols], edges), stacked(packed[:, cols], edges)
        keys, values = kv_ref[:, cols], kv_ref[:, width + base : width + base + 256]
        scores = masked_scores(seen, queries, keys, media_rows)
        probs = jnp.exp(scores - column(2 * pair))
        prob_grad = dot(grads, values, ((1,), (1,)))
        score_grad = (probs * (prob_grad - column(3 * H + 2 * pair))).astype(BF)
        new = (
            (dq_ref, 0, dot(score_grad, keys)),
            (dkv_ref, 0, dot(score_grad, queries, ((0,), (0,)))),
            (dkv_ref, width, dot(probs.astype(BF), grads, ((0,), (0,)))),
        )
        new = [(ref, at + base, unstacked(x, edges) if ref is dq_ref else x) for ref, at, x in new]
        if pair % 2 == 0:
            for ref, at, x in new:
                ref[:, at : at + 128] = x[:, :128].astype(BF)
            carry = [x[:, 128:] for unused_ref, unused_at, x in new]
        else:
            for (ref, at, x), old in zip(new, carry):
                ref[:, at : at + 128] = (old + x[:, :128]).astype(BF)
                ref[:, at + 128 : at + 256] = x[:, 128:].astype(BF)


def lane_heads(shape, width, dim):
    lane = lax.broadcasted_iota(jnp.int32, shape, dim)
    column = lax.broadcasted_iota(jnp.int32, shape, 1 - dim)
    size = width // H
    first = (lane % H) * size
    return lane // H, column - first, (column >= first) & (column < first + size)


def three_terms(x):
    terms = []
    for unused in range(3):
        terms.append(x.astype(BF))
        x = x - terms[-1].astype(F32)
    return terms


def combine_kernel(pieces, whole, me_ref, *refs):
    parts, refs = refs[:pieces], refs[pieces:]
    latent_ref, gain_ref, bias_ref, *refs = refs
    *refs, wide_ref, low_ref, stat_ref, hidden_ref, ffn_ref, w_ref, sems = refs
    waits = whole.fetch(me_ref[0], refs, w_ref, sems)
    rows, width = latent_ref.shape
    group, unused, inside = lane_heads((128, width), width, 0)
    spread_top = jnp.where(inside & (group < 3), 1.0, 0.0).astype(BF)
    spread_total = jnp.where(inside & (group >= 3) & (group < 6), 1.0, 0.0).astype(BF)
    tops = [dot(ref[:, width:], spread_top) for ref in parts]
    top = tops[0]
    for other in tops[1:]:
        top = jnp.maximum(top, other)
    total = jnp.zeros((rows, width), F32)
    mixed = jnp.zeros((rows, width), F32)
    for ref, mine in zip(parts, tops):
        weight = jnp.exp(mine - top) * dot(ref[:, width:], spread_total)
        total += weight
        mixed += weight * ref[:, :width].astype(F32)
    mixed = mixed / total
    wide_ref[...] = mixed
    low = mixed.astype(BF)
    low_ref[...] = low
    group, offset, unused = lane_heads((width, 128), width, 1)
    stats = jnp.zeros((rows, 128), F32)
    for k, term in enumerate(three_terms(top + jnp.log(total))):
        pick = jnp.where((group == k) & (offset == 0), 1.0, 0.0).astype(BF)
        stats += dot(term, pick)
    stat_ref[...] = stats
    for wait in waits:
        wait.wait()
    hidden = latent_ref[...].astype(F32) + dot(low, w_ref[...])
    hidden_ref[...] = hidden
    ffn_ref[...] = layer_norm(hidden, gain_ref[...], bias_ref[...])[0].astype(BF)


def hidden_back_kernel(whole, me_ref, *refs):
    keep_ref, other_ref, hidden_ref, upstream_ref, wide_ref, stat_ref, gain_ref, *refs = refs
    *refs, hidden_grad_ref, low_ref, packed_ref, sums_ref, w_ref, sems = refs
    waits = whole.fetch(me_ref[0], refs, w_ref, sems)
    rows, width = hidden_ref.shape
    grad = keep_ref[0].astype(F32) + other_ref[0].astype(F32)
    gain = gain_ref[...]
    unused, unit, rstd = layer_norm(hidden_ref[...], gain, gain)
    norm_grad, gain_grad, bias_grad = layer_norm_back(grad, unit, rstd, gain)
    row = lax.broadcasted_iota(jnp.int32, (8, width), 0)
    sums_ref[...] = jnp.where(row == 0, gain_grad[None], jnp.where(row == 1, bias_grad[None], 0.0))
    hidden_grad = upstream_ref[...].astype(F32) + norm_grad
    hidden_grad_ref[...] = hidden_grad
    low = hidden_grad.astype(BF)
    low_ref[...] = low
    for wait in waits:
        wait.wait()
    mixture_grad = dot(low, w_ref[...], ((1,), (1,))).astype(BF)
    packed_ref[:, :width] = mixture_grad
    group, unused, inside = lane_heads((width, 128), width, 1)
    heads = jnp.where(inside & (group >= 3) & (group < 6), 1.0, 0.0).astype(BF)
    inner = jnp.zeros((rows, 128), F32)
    for term in three_terms(wide_ref[...] * mixture_grad.astype(F32)):
        inner += dot(term, heads)
    lane = lax.broadcasted_iota(jnp.int32, (rows, 128), 1) // H
    stats = stat_ref[...]
    for k, term in enumerate(three_terms(inner)):
        stats = jnp.where(lane == 3 + k, term.astype(F32), stats)
    packed_ref[:, width:] = stats.astype(BF)


def owner_of(place, order):
    return sum(mask for k, mask in enumerate(order) if (place >> k) % 2)


def place_of(owner, order):
    return sum(((owner // mask) % 2) << k for k, mask in enumerate(order))


class Stacks:
    def __init__(self, parts, orders):
        self.each = len(parts[0])
        self.arrays = [x for pieces in parts for x in pieces]
        self.orders = orders
        self.cols = sum(pieces[0].shape[2] for pieces in parts)
        widths = [pieces[0].shape[2] for pieces in parts]
        self.ends = [sum(widths[: k + 1]) for k in range(len(parts))]

    def fetch(self, me, refs, into, sems):
        at, waits = 0, []
        for k, order in enumerate(self.orders):
            pieces = refs[self.each * k : self.each * (k + 1)]
            some, block, cols = pieces[0].shape
            for place in range(self.each * some):
                owner = me ^ owner_of(place, order)
                to = into.at[pl.ds(pl.multiple_of(owner * block, 16), block), at : at + cols]
                source = pieces[place // some].at[place % some]
                pltpu.make_async_copy(source, to, sems.at[k]).start()
            part = into.at[:, at : at + cols]
            waits.append(pltpu.make_async_copy(part, part, sems.at[k]))
            at += cols
        return waits


class Plain:
    def __init__(self, x):
        self.arrays, self.orders = [x], (None,)
        self.cols = x.shape[1]
        self.ends = [self.cols]

    def fetch(self, me, refs, into, sems):
        copy = pltpu.make_async_copy(refs[0], into, sems.at[0])
        copy.start()
        return [copy]


def halves_kernel(me_ref, s_ref, mine_ref, other_ref):
    block = 48
    for parity in range(2):

        @pl.when(me_ref[0] % 2 == parity)
        def _():
            for out_ref, which in ((mine_ref, parity), (other_ref, 1 - parity)):
                for n in range(out_ref.shape[1] // block):
                    at = (2 * n + which) * block
                    out_ref[:, n * block : (n + 1) * block] = s_ref[:, at : at + block]


def order_kernel(whole, me_ref, *refs):
    *refs, out_ref, sems = refs
    for wait in whole.fetch(me_ref[0], refs, out_ref, sems):
        wait.wait()


def project_kernel(whole, me_ref, s_ref, *refs):
    *refs, out_ref, w_ref, sems = refs
    at = 0
    for wait, end in zip(whole.fetch(me_ref[0], refs, w_ref, sems), whole.ends):
        wait.wait()
        out_ref[:, at:end] = dot(s_ref[...], w_ref[:, at:end]).astype(BF)
        at = end


def gelu_parts(x):
    c = 0.7978845608028654
    t = jnp.tanh(c * (x + 0.044715 * (x * x * x)))
    slope = 0.5 * (1.0 + t) + 0.5 * x * (1.0 - t * t) * (c * (1.0 + 3 * 0.044715 * (x * x)))
    return 0.5 * x * (1.0 + t), slope


def ffn_kernel(
    order,
    me_ref,
    mine_ref,
    other_ref,
    up_mine_ref,
    up_other_ref,
    down_ref,
    all_ref,
    keep_ref,
    send_ref,
    active_ref,
    pre_ref,
    rows_ref,
    grad_rows_ref,
    up_ref,
    sem,
):
    some, each, width = mine_ref.shape
    for place in range(2 * some):
        owner = me_ref[0] ^ owner_of(place, order)
        pltpu.make_async_copy(
            all_ref.at[owner, :, width : 2 * width],
            grad_rows_ref.at[place * each : (place + 1) * each],
            sem,
        ).start()
    rows_ref[: some * each, :] = mine_ref[...].reshape(some * each, width)
    rows_ref[some * each :, :] = other_ref[...].reshape(some * each, width)
    units = up_mine_ref.shape[1]
    up_ref[:, :units] = up_mine_ref[...]
    up_ref[:, units:] = up_other_ref[...]
    active, slope = gelu_parts(dot(rows_ref[...], up_ref[...]))
    active_ref[...] = active.astype(BF)
    pltpu.make_async_copy(grad_rows_ref, grad_rows_ref, sem).wait()
    pre_grad = (dot(grad_rows_ref[...], down_ref[...], ((1,), (1,))) * slope).astype(BF)
    pre_ref[...] = pre_grad
    total = dot(pre_grad, up_ref[...], ((1,), (1,)))
    keep_ref[...] = total[: some * each].reshape(keep_ref.shape)
    send_ref[...] = total[some * each :].astype(BF).reshape(send_ref.shape)


def ffn_sums_kernel(
    rows_ref,
    grad_rows_ref,
    active_ref,
    pre_ref,
    down_ref,
    down_keep_ref,
    down_send_ref,
    up_keep_ref,
    up_send_ref,
    keep_ref,
    send_ref,
):
    first = ((0,), (0,))
    units = down_keep_ref.shape[0]
    down = dot(active_ref[...], grad_rows_ref[...], first)
    down_keep_ref[...] = down[:units]
    down_send_ref[...] = down[units:].astype(BF)
    up = dot(rows_ref[...], pre_ref[...], first)
    up_keep_ref[...] = up[:, :units].astype(BF)
    up_send_ref[...] = up[:, units:].astype(BF)
    out = dot(active_ref[...], down_ref[...])
    half = out.shape[0] // 2
    keep_ref[...] = out[:half].reshape(keep_ref.shape)
    send_ref[...] = out[half:].astype(BF).reshape(send_ref.shape)


def source_kernel(whole, me_ref, g_ref, media_ref, time_ref, gain_ref, *refs):
    *refs, media_grad_ref, latent_ref, sums_ref, acc_ref, w_ref, sems = refs
    at = 0
    for wait, end in zip(whole.fetch(me_ref[0], refs, w_ref, sems), whole.ends):
        wait.wait()
        new = dot(g_ref[:, at:end], w_ref[:, at:end], ((1,), (1,)))
        acc_ref[...] = acc_ref[...] + new if at else new
        at = end
    media_rows, width = media_ref.shape
    gain = gain_ref[...]
    rows = [jnp.zeros((1, width), F32), jnp.zeros((1, width), F32)]
    for frame in range(media_rows // PATCH):
        here = slice(frame * PATCH, (frame + 1) * PATCH)
        shifted = media_ref[here, :].astype(F32) + time_ref[frame : frame + 1, :]
        unused, unit, rstd = layer_norm(shifted, gain, gain)
        grad = acc_ref[here, :]
        shifted_grad, gain_grad, bias_grad = layer_norm_back(grad, unit, rstd, gain)
        media_grad_ref[here, :] = shifted_grad.astype(BF)
        rows[0] += gain_grad[None]
        rows[1] += bias_grad[None]
        rows.append(jnp.sum(shifted_grad, axis=0, keepdims=True))
    at = lax.broadcasted_iota(jnp.int32, sums_ref.shape, 0)
    sums = jnp.zeros(sums_ref.shape, F32)
    for k, row in enumerate(rows):
        sums = jnp.where(at == k, row, sums)
    sums_ref[...] = sums
    latent_ref[...] = acc_ref[media_rows:, :]


def latent_kernel(pieces, scaling, *refs):
    parts, refs = refs[:pieces], refs[pieces:]
    source_ref, latent_ref, gain_ref, hidden_grad_ref, out_ref, sums_ref = refs
    gain = gain_ref[...]
    width = gain.shape[1]
    query_side = sum(ref[:, :width].astype(F32) for ref in parts)
    grad = source_ref[...] + query_side * scaling
    unused, unit, rstd = layer_norm(latent_ref[...].astype(F32), gain, gain)
    latent_grad, gain_grad, bias_grad = layer_norm_back(grad, unit, rstd, gain)
    out_ref[...] = (hidden_grad_ref[...] + latent_grad).astype(BF)
    at = lax.broadcasted_iota(jnp.int32, sums_ref.shape, 0)
    sums_ref[...] = jnp.where(
        at == 0, gain_grad[None], jnp.where(at == 1, bias_grad[None], 0.0)
    )


def sums_kernel(orders, me_ref, s_ref, s2_ref, g_ref, g2_ref, *refs):
    *out_refs, s_held, g_held, held, sems = refs
    me = me_ref[0] - me_ref[0] % 2
    half, block, unused = out_refs[0].shape
    widths = [ref.shape[2] for ref in out_refs[::2]]
    starts = [sum(widths[:k]) for k in range(len(widths))]
    rows = s_ref.shape[0]
    for k, ref in enumerate((s_ref, s2_ref)):
        pltpu.make_async_copy(ref, s_held.at[k * rows : (k + 1) * rows], sems.at[0]).start()
    for part in range(len(orders)):
        columns = slice(starts[part], starts[part] + widths[part])
        for k, ref in enumerate((g_ref, g2_ref)):
            to = g_held.at[k * rows : (k + 1) * rows, columns]
            pltpu.make_async_copy(ref.at[:, columns], to, sems.at[1 + part]).start()
    pltpu.make_async_copy(s_held, s_held, sems.at[0]).wait()
    some = held.shape[0]
    for part, order in enumerate(orders):
        columns = slice(starts[part], starts[part] + widths[part])
        here = g_held.at[:, columns]
        pltpu.make_async_copy(here, here, sems.at[1 + part]).wait()
        first = (me // order[-1]) % 2
        for start in range(0, 2 * half, some):
            full = dot(s_held[:, start * block : (start + some) * block], here[...], ((0,), (0,)))
            cols = widths[part]
            held[:, :, :cols] = full.astype(BF).reshape(some, block, cols)
            for bit in range(2):

                @pl.when(first == bit)
                def _(bit=bit, start=start, part=part, order=order, cols=cols):
                    for n in range(some):
                        owner = 2 * (start + n)
                        place = place_of(owner ^ me, order) % half
                        send = (owner // order[-1]) % 2 != bit
                        out_refs[2 * part + send][place] = held[n, :, :cols]


SCALAR = pl.BlockSpec(memory_space=pltpu.SMEM)
FAR = pl.BlockSpec(memory_space=pl.ANY)


def call(kernel, inputs, outputs, flops, specs=(), far_outputs=False, scratch=()):
    specs = dict(specs)

    def whole(x):
        return pl.BlockSpec(x.shape, lambda i, nd=len(x.shape): (0,) * nd)

    nbytes = sum(x.size * x.dtype.itemsize for x in inputs)
    nbytes += sum(x.size * x.dtype.itemsize for x in outputs)
    return pl.pallas_call(
        kernel,
        grid=(1,),
        out_shape=tuple(outputs),
        in_specs=[specs.get(n, whole(x)) for n, x in enumerate(inputs)],
        out_specs=tuple(FAR if far_outputs else whole(x) for x in outputs),
        scratch_shapes=list(scratch),
        compiler_params=pltpu.CompilerParams(vmem_limit_bytes=56 << 20),
        cost_estimate=pl.CostEstimate(flops=flops // 1000, bytes_accessed=nbytes // 1000, transcendentals=0),
    )(*inputs)


def shards(
    media,
    latents,
    frames,
    time_embed,
    media_gain,
    media_bias,
    latent_gain,
    latent_bias,
    ffn_gain,
    ffn_bias,
    w_query,
    w_key,
    w_value,
    w_out,
    w_up,
    w_down,
    grad_out,
):
    item_count, seq_count = lax.axis_size("items"), lax.axis_size("seq")
    count = item_count * seq_count
    seq_index = lax.axis_index("seq")
    me = lax.axis_index("items") * seq_count + seq_index
    unused_items, media_rows, width = media.shape
    latent_rows = latents.shape[1]
    head_size = width // H
    frames_here = media_rows // PATCH
    scaling = head_size ** (-0.5)

    bits = [1 << k for k in reversed(range(30))]
    item_bits = [m for m in bits if seq_count <= m < count]
    seq_bits = [m for m in bits if m < seq_count]
    head, (fold, near), side, tail = item_bits[:-2], item_bits[-2:], seq_bits[0], seq_bits[1:]
    orders = (
        head + [fold, near, side] + tail,
        head + [side, fold, near] + tail,
        head + [near, side, fold] + tail,
    )
    ffn_order = item_bits + seq_bits[:-1]
    core = seq_bits[-1]
    block = width // count
    regular = block % 16 == 0

    def share(x):
        return jax.ShapeDtypeStruct(x, BF)

    latent_in = latents[0].astype(F32)
    latent_normed, latent_unit, latent_rstd = layer_norm(latent_in, latent_gain, latent_bias)
    latent_normed = latent_normed.astype(BF)
    time_rows = lax.dynamic_slice_in_dim(time_embed, seq_index * frames_here, frames_here, 0)
    shifted = (
        media[0].astype(F32).reshape(frames_here, PATCH, width) + time_rows[:, None, :]
    ).reshape(media_rows, width)
    media_normed, media_unit, media_rstd = layer_norm(shifted, media_gain, media_bias)
    sources = jnp.concatenate([media_normed.astype(BF), latent_normed], axis=0)

    def in_columns(x):
        return x.reshape(x.shape[0], count, -1).transpose(1, 0, 2)

    def spread(x):
        x = lax.all_to_all(x, AXES, split_axis=0, concat_axis=0, tiled=True)
        return x.reshape(-1, x.shape[2])

    cols_here = width // seq_count

    def seq_blocks(x, axis):
        return jnp.concatenate(
            [
                lax.dynamic_index_in_dim(x, seq_index ^ t, 0, keepdims=False)
                for t in range(seq_count)
            ],
            axis=axis,
        )

    def columns_of(x, m):
        return lax.dynamic_slice_in_dim(x, (seq_index ^ m) * cols_here, cols_here, 1)

    def reordered(x, m):
        blocks = x.reshape(seq_count, latent_rows, x.shape[1])
        return jnp.concatenate([blocks[t ^ m] for t in range(seq_count)], axis=0)

    parts = len(orders)
    units = w_down.shape[0]
    out_orders = (head + [near, fold, side] + tail, head + [near, side, fold] + tail)
    shares = (width * 5 // 6, width * 5 // 6, width // 3)
    def query_pieces(x):
        pieces = [columns_of(x, m) for m in range(seq_count)]
        return [pieces[0]] + [trade(pieces[m], m, count) for m in range(1, seq_count)]

    if regular:
        first = GatherRel(jnp.concatenate([w_key, w_value], axis=1)[None], head)
        second = GatherRel(w_out[None], head + [near])

        def split(x, shares, orders, done):
            return [
                GatherApart(x[..., sum(shares[:k]) : sum(shares[: k + 1])], order[done:])
                for k, order in enumerate(orders)
            ]

        while first.order:
            started = exchange(count, first)
        latent_item = share_seq(after(latent_normed, started), seq_count, count)
        pieces = query_pieces(after(w_query, started))
        half_mine, half_other = call(
            halves_kernel,
            (me[None], sources),
            (share((sources.shape[0], width // 2)),) * 2,
            0,
            specs={0: SCALAR},
        )
        rows_mine = jnp.concatenate([latent_normed, grad_out[0]], axis=1)
        sources, latent_item, half_mine, half_other, rows_mine, *pieces = sync(
            [first], sources, latent_item, half_mine, half_other, rows_mine, *pieces
        )
        query_cols = Gather(seq_blocks(jnp.stack(pieces), 0), [near] + head + [fold], me)
        first = split(first.x, shares, orders, len(head))
        exchange(count, *first, second, query_cols)
        sync([*first, second, query_cols])
        exchange(count, *first, second, query_cols)
        up_in, rows_mine = sync([*first, second, query_cols], w_up, rows_mine)
        rows_all = lax.all_gather(rows_mine, AXES, axis=0)
        second = split(second.x, (width // 2, width // 2), out_orders, len(head) + 1)
        exchange(count, *first, query_cols)
        sources, latent_item, half_other, up_in = sync(
            [*first, query_cols], sources, latent_item, half_other, in_columns(up_in)
        )
        for job in first:
            job.last(count)
    else:
        up_mine = spread(in_columns(w_up))
        rows_all = lax.all_gather(
            jnp.concatenate([latent_normed, grad_out[0]], axis=1), AXES, axis=0
        )
        latent_item = share_seq(latent_normed, seq_count, count)
        query_cols = Gather(seq_blocks(jnp.stack(query_pieces(w_query)), 0), item_bits, me)
        while query_cols.order:
            exchange(count, query_cols)
        both = lax.all_gather(jnp.concatenate([w_key, w_value], 1), AXES, axis=0, tiled=True)
        key_value = Plain(both)
        out_full = Plain(lax.all_gather(w_out, AXES, axis=0, tiled=True))

    def with_weights(kernel, inputs, whole, outputs, flops, keep=True, scratch=()):
        inputs = [me[None]] + list(inputs)
        specs = {0: SCALAR}
        for n in range(len(whole.arrays)):
            specs[len(inputs) + n] = FAR
        scratch = list(scratch) + ([pltpu.VMEM((width, whole.cols), BF)] if keep else [])
        return call(
            lambda *refs: kernel(whole, *refs),
            (*inputs, *whole.arrays),
            outputs,
            flops,
            specs=specs,
            scratch=scratch + [pltpu.SemaphoreType.DMA((len(whole.orders),))],
        )

    query_slice = query_cols.rows().reshape(width, cols_here)
    query_mine = (dot(latent_item, query_slice) * scaling).astype(BF)
    sends = [reordered(query_mine, m) for m in range(1, seq_count)]
    if regular:
        up_mine = spread(up_in)
        query_mine, *sends = sync([*first, *second], query_mine, *sends)
        key_value = Stacks([job.x for job in first], orders)
        exchange(count, *second)
    pieces = [query_mine] + [trade(x, m + 1, count) for m, x in enumerate(sends)]
    source_count = sources.shape[0]
    keys = with_weights(
        project_kernel,
        (sources,),
        key_value,
        (share((source_count, 2 * width)),),
        4 * source_count * width * width,
    )[0]
    if regular:
        keys, half_other, up_mine, *pieces = sync(second, keys, half_other, up_mine, *pieces)
        half_other = trade(half_other, 1, count)
        exchange(count, *second)
    queries = seq_blocks(jnp.stack(pieces), 1)
    seen = jnp.clip((frames - seq_index * frames_here) * PATCH, 0, media_rows).astype(jnp.int32)
    all_rows = queries.shape[0]
    pair_flops = 2 * H // 2 * 2 * all_rows * 256 * sources.shape[0]
    mixed = call(
        lambda *refs: attend_kernel(media_rows, *refs),
        (seen, queries, keys),
        (share((all_rows, width + 128)),),
        2 * pair_flops,
        specs={0: SCALAR},
    )[0]

    def own_parts(x):
        blocks = x.reshape(seq_count, latent_rows, x.shape[1])
        return [blocks[0]] + [trade(blocks[m], m, count) for m in range(1, seq_count)]


    mixed_parts = own_parts(mixed)
    if regular:
        mixed_parts = sync(second, *mixed_parts)
        for job in second:
            job.last(count, join=True)
        sync(second)
        out_full = Stacks([job.x for job in second], out_orders)
    up_other, down_other = trade(up_mine, core, count), trade(w_down, core, count)
    down_pair = jnp.concatenate([w_down, down_other], axis=0)
    rows_wide = jax.ShapeDtypeStruct((latent_rows, width), F32)
    rows_low = jax.ShapeDtypeStruct((latent_rows, width), BF)
    mixture_wide, mixture, log_total, hidden, ffn_in = with_weights(
        lambda *refs: combine_kernel(seq_count, *refs),
        (*mixed_parts, latents[0], ffn_gain[None], ffn_bias[None]),
        out_full,
        (
            rows_wide,
            rows_low,
            jax.ShapeDtypeStruct((latent_rows, 128), F32),
            rows_wide,
            rows_low,
        ),
        2 * latent_rows * width * width,
    )
    ffn_rows = GatherRel(ffn_in[None], ffn_order)
    while len(ffn_rows.order) > 1:
        exchange(count, ffn_rows)
    mine = ffn_rows.x
    other = trade(mine, ffn_order[-1], count)
    some = mine.shape[0]
    all_ffn = 2 * some * latent_rows
    units_low = share((all_ffn, 2 * units))
    halves = (jax.ShapeDtypeStruct(mine.shape, F32), share(mine.shape))
    ffn_flops = 2 * all_ffn * 2 * units * width
    keep, send, active, pre, ffn_all, grad_all = call(
        lambda *refs: ffn_kernel(ffn_order, *refs),
        (me[None], mine, other, up_mine, up_other, down_pair, rows_all),
        (*halves, units_low, units_low, *(share((all_ffn, width)),) * 2),
        3 * ffn_flops,
        specs={0: SCALAR, 6: FAR},
        scratch=(pltpu.VMEM((width, 2 * units), BF), pltpu.SemaphoreType.DMA(())),
    )
    back = Halves([keep], [send], [ffn_order])
    back.step(count)
    down_keep, down_send, up_keep, up_send, keep, send = call(
        ffn_sums_kernel,
        (ffn_all, after(grad_all, back.token), active, pre, down_pair),
        (
            jax.ShapeDtypeStruct((units, width), F32),
            share((units, width)),
            share((width, units)),
            share((width, units)),
            *halves,
        ),
        3 * ffn_flops,
    )
    result = Halves([keep], [send], [ffn_order])
    wait = (down_send,)
    while back.orders[0]:
        back.split()
        back.step(count, wait)
        if not wait:
            result.split()
        result.step(count, (back.token,))
        wait = ()
        if back.orders[0]:
            back.others, result.others = lax.optimization_barrier((back.others, result.others))

    hidden_grad, attended_low, packed, ffn_sums = with_weights(
        hidden_back_kernel,
        (
            back.keep[0],
            back.others[0],
            hidden,
            grad_out[0],
            mixture_wide,
            log_total,
            ffn_gain[None],
        ),
        out_full,
        (
            rows_wide,
            rows_low,
            share((latent_rows, width + 128)),
            jax.ShapeDtypeStruct((8, width), F32),
        ),
        2 * latent_rows * width * width,
    )
    down_send, up_send = sync([], down_send, up_send, packed)[:2]
    down_other, up_other = trade(down_send, core, count), trade(up_send, core, count)
    pieces = [packed] + [trade(packed, m, count) for m in range(1, seq_count)]
    result.split()
    result.step(count, (packed,))
    query_part, row_grad = call(
        lambda *refs: attend_back_kernel(media_rows, seq_count, *refs),
        (seen, queries, keys, *pieces),
        (share((all_rows, width)), share(keys.shape)),
        5 * pair_flops,
        specs={0: SCALAR},
    )
    sends = [reordered(columns_of(query_part, m), m) for m in range(seq_count)]
    row_send, result.others, *sends = lax.optimization_barrier((row_grad, result.others, *sends))
    row_other = trade(row_send, 1, count)
    pieces = [sends[0]] + [trade(sends[m], m, count) for m in range(1, seq_count)]
    row_grad, row_other, *pieces = sync([], row_send, row_other, *pieces)
    query_cols_grad = sum(x.astype(F32) for x in pieces).astype(BF)
    query_side = dot(query_cols_grad, query_slice, ((1,), (1,))).astype(BF)
    query_side = own_parts(jnp.concatenate([query_side, query_cols_grad], axis=1))

    if regular:
        outs = call(
            lambda *refs: sums_kernel([order[:-1] for order in orders], *refs),
            (me[None], half_mine, half_other, row_grad, row_other),
            tuple(share((count // 4, block, cols)) for cols in shares for unused in range(2)),
            4 * width * width * source_count,
            specs={0: SCALAR, 1: FAR, 2: FAR, 3: FAR, 4: FAR},
            scratch=(
                pltpu.VMEM((2 * source_count, width // 2), BF),
                pltpu.VMEM((2 * source_count, 2 * width), BF),
                pltpu.VMEM((8, block, max(shares)), BF),
                pltpu.SemaphoreType.DMA((1 + parts,)),
            ),
        )
        weights = Halves(outs[::2], outs[1::2], [order[:-1] for order in orders])
        weights.step(count, (*query_side[1:], *result.others))
        started = weights.token
    else:
        full = dot(sources, row_grad, ((0,), (0,))).astype(BF)
        full = lax.psum_scatter(full, AXES, scatter_dimension=0, tiled=True).astype(F32)
        started = row_other
    result.others, up_keep, up_other = sync([], result.others, up_keep, up_other, started)[:-1]
    up_blocks = (up_keep.astype(F32) + up_other.astype(F32)).astype(BF)
    up_blocks = up_blocks.reshape(count, -1, units)
    up_blocks = lax.all_to_all(up_blocks, AXES, split_axis=0, concat_axis=0, tiled=True)
    query_rows = seq_blocks(jnp.stack([x[:, width:] for x in query_side]), 1)
    rows = lax.all_gather(
        jnp.concatenate([attended_low, query_rows, mixture], axis=1), AXES, axis=0, tiled=True
    )

    media_grad, latent_source, media_sums = with_weights(
        source_kernel,
        (after(row_grad, started), media[0], time_rows, media_gain[None]),
        key_value,
        (
            share((media_rows, width)),
            jax.ShapeDtypeStruct((latent_rows, width), F32),
            jax.ShapeDtypeStruct((8, width), F32),
        ),
        4 * source_count * width * width,
        scratch=[pltpu.VMEM((source_count, width), F32)],
    )
    latents_grad, latent_sums = call(
        lambda *refs: latent_kernel(seq_count, scaling, *refs),
        (*query_side, latent_source, latents[0], latent_gain[None], hidden_grad),
        (rows_low, jax.ShapeDtypeStruct((8, width), F32)),
        2 * latent_rows * width * width,
    )
    time_local = lax.dynamic_update_slice_in_dim(
        jnp.zeros((FRAMES, width), F32),
        media_sums[2 : 2 + frames_here],
        seq_index * frames_here,
        0,
    )
    sums = Sum(
        jnp.concatenate(
            [
                time_local,
                media_sums[:2],
                latent_sums[:2],
                ffn_sums[:2],
                jnp.zeros((2, width), F32),
            ],
            axis=0,
        ),
        [side, near, fold],
    )
    if regular:
        while weights.orders[0]:
            weights.split()
            weights.step(count)
            if len(weights.orders[0]) == 1:
                down_other, up_blocks = after(down_other, weights.token), after(up_blocks, weights.token)
            if result.orders[0]:
                result.split()
                result.step(count, (weights.token,))
            if sums.order:
                exchange(count, sums, wait=(weights.token,))
        full = jnp.concatenate([x[0] for x in weights.total()], axis=1)
    while result.orders[0]:
        result.split()
        result.step(count)
    down_grad = down_keep + down_other.astype(F32)
    up_grad = up_blocks.transpose(1, 0, 2).reshape(-1, count * units).astype(F32)
    latents_out = hidden + result.total()[0][0]

    def my_columns(x):
        return lax.dynamic_slice_in_dim(x, me * block, block, 1)

    out_grad = dot(my_columns(rows[:, 2 * width :]), rows[:, :width], ((0,), (0,)))
    latent_all = my_columns(rows_all.reshape(-1, 2 * width))
    query_grad = dot(latent_all, rows[:, width : 2 * width], ((0,), (0,))) * scaling
    while sums.order:
        exchange(count, sums)
    sums, others = sums.x, [0]
    for bit in head + tail:
        others += [mask ^ bit for mask in others]
    sums_parts = [trade(sums, mask, count) for mask in others[1:]]
    out_grad, query_grad, *sums_parts = sync([], out_grad, query_grad, *sums_parts)
    sums_parts = [sums, *sums_parts]
    while len(sums_parts) > 1:
        sums_parts = [a + b for a, b in zip(sums_parts[::2], sums_parts[1::2])]
    sums = sums_parts[0]
    return (
        latents_out.astype(BF)[None],
        latents_grad[None],
        media_grad[None],
        sums[:FRAMES],
        sums[FRAMES],
        sums[FRAMES + 1],
        sums[FRAMES + 2],
        sums[FRAMES + 3],
        sums[FRAMES + 4],
        sums[FRAMES + 5],
        query_grad,
        full[:, :width],
        full[:, width:],
        out_grad,
        up_grad,
        down_grad,
    )


def solution(mesh):
    rows, split = P("items", "seq", None), P(AXES, None)
    return jax.shard_map(
        shards,
        mesh=mesh,
        in_specs=(rows, rows, P("items")) + (P(),) * 7 + (split,) * 6 + (rows,),
        out_specs=(rows,) * 3 + (P(),) * 7 + (split,) * 6,
        check_vma=False,
    )
```
